32 devices in a mesh: rep: 4 (over y, x), rows: 8 (over z, core).
Axes of the slice: x: 2, y: 2, z: 4, core: 2. Of those that a mesh axis runs over, the one named last changes fastest.
Arguments:
- latents: float32 [4, 8192, 1024], P('rep', 'rows'), may hold values from -6 to 6
- cotangent: float32 [4, 8192, 1024], P('rep', 'rows'), may hold values from -6 to 6
- segment_ids: int32 [4, 8192], P('rep', 'rows'), may hold values from 0 to 95, as said below
- weights: float32 [1024, 6144], P('rows')
- small_params: float32 [9, 1024], P(None, 'rows')
- first_mats: float32 [1024, 6144], P('rows'), may hold values from -0.15 to 0.15
- second_mats: float32 [1024, 6144], P('rows'), may hold values from 6.25e-05 to 0.00025
- average_mats: float32 [1024, 6144], P('rows'), may hold values from -0.6 to 0.6
- first_small: float32 [9, 1024], P(None, 'rows'), may hold values from -0.15 to 0.15
- second_small: float32 [9, 1024], P(None, 'rows'), may hold values from 6.25e-05 to 0.00025
- average_small: float32 [9, 1024], P(None, 'rows'), may hold values from -1.5 to 1.5
Outputs:
- latents_out: float32 [4, 8192, 1024], P('rep', 'rows')
- latents_grad: float32 [4, 8192, 1024], P('rep', 'rows')
- grad_norm: float32 [1], replicated
- clipped_mats: float32 [1024, 6144], P('rows')
- clipped_small: float32 [9, 1024], P(None, 'rows')
- new_weights: float32 [1024, 6144], P('rows')
- new_small: float32 [9, 1024], P(None, 'rows')
- first_mats_out: float32 [1024, 6144], P('rows')
- second_mats_out: float32 [1024, 6144], P('rows')
- average_mats_out: float32 [1024, 6144], P('rows')
- first_small_out: float32 [9, 1024], P(None, 'rows')
- second_small_out: float32 [9, 1024], P(None, 'rows')
- average_small_out: float32 [9, 1024], P(None, 'rows')
- weights_low: bfloat16 [1024, 6144], P('rows')
- small_low: bfloat16 [9, 1024], P(None, 'rows')
The draws below stay inside these ranges and needn't reach their ends.
Inputs may be any that keep to these rules, and one draw needn't show every extreme that they name: `segment_ids`: along each repeat's tokens the ids never fall, are constant on aligned blocks of 128 tokens, take a new value at every multiple of 1024, and each packed row of 1024 tokens holds exactly 3 sets, numbered consecutively from 0 over all repeats; no id appears in two repeats.
All inputs are finite; a program needn't handle non-finite values.
Results may differ from the reference program's by a relative error of at most 0.001.
Values sent between devices are 32-bit elements; how exact they have to be, the bound alone decides.
A program may use at most 320 MiB of HBM per device.

```python
import math
import jax
import jax.numpy as jnp
from jax import lax

D = 1024
HEADS = 8
HEAD_DIM = 128
FF = 1024
TOK_DEV = 1024
SEG_UNIT = 128
STEP = 5
REPS = 4
TOKENS = 8192


def draw_segment_ids(key, part):
    row_total = REPS * TOKENS // TOK_DEV
    per_row = TOK_DEV // SEG_UNIT
    extra_starts = (per_row - 1) // 3
    random_part = jax.random.randint(key, (row_total, per_row), 0, 1000000).astype(jnp.int32)
    position = jnp.arange(per_row, dtype=jnp.int32)
    scores = random_part * per_row + position[None, :] + 1
    scores = jnp.where(position[None, :] == 0, 0, scores).astype(jnp.int32)
    order = jnp.argsort(scores, axis=1, stable=True)
    ranks = jnp.argsort(order, axis=1, stable=True).astype(jnp.int32)
    starts = jnp.where(ranks <= extra_starts, 1, 0).astype(jnp.int32).reshape(row_total * per_row)
    unit_ids = (jnp.cumsum(starts) - 1).astype(jnp.int32)
    return jnp.repeat(unit_ids, SEG_UNIT).reshape(REPS, TOKENS).astype(jnp.int32)


def draw_weights(key, part):
    standard = jax.random.normal(key, (D, 6 * D), jnp.float32)
    column = jnp.arange(6 * D)
    column_scale = jnp.where((column >= 3 * D) & (column < 4 * D), 4.0, 1.0) * D ** (-0.5)
    return standard * column_scale[None, :].astype(jnp.float32)


def draw_small_params(key, part):
    first_key, second_key = jax.random.split(key)
    gain_draw = jax.random.uniform(first_key, (9, D), jnp.float32, 0.5, 1.5)
    bias_draw = 0.5 * jax.random.normal(second_key, (9, D), jnp.float32)
    row_index = jnp.arange(9)
    is_gain = (row_index == 0) | (row_index == 5)
    return jnp.where(is_gain[:, None], gain_draw, bias_draw)


def levels(stream_key, shape, cuts, smallest, high):
    gain, own = 1.0, jax.random.fold_in(stream_key, 6)
    for dim, parts in cuts:
        heights = jnp.exp(jax.random.uniform(jax.random.fold_in(own, dim), (parts,), jnp.float32, smallest / len(cuts), high / len(cuts)))
        gain = gain * jnp.repeat(heights, shape[dim] // parts).reshape([-1 if axis == dim else 1 for axis in range(len(shape))])
    return gain


def noise(own_key, dims, deviation, limit, cuts=(), kind=jnp.bfloat16):
    entries = jax.random.normal(own_key, dims, jnp.float32) * deviation
    if len(cuts) > 0:
        entries = levels(own_key, dims, cuts, -0.22, 0.18) * entries
    return jnp.clip(entries, min=-limit, max=limit).astype(kind)


def setup_inputs(seed: int = 0) -> dict:
    streams_of = jax.random.split(jax.random.key(seed), 12)
    latents = noise(streams_of[0], (REPS, TOKENS, D), 1.0, 6.0, ((0, 4), (1, 8)), jnp.float32)
    cotangent = noise(streams_of[1], (REPS, TOKENS, D), 1.0, 6.0, ((0, 4), (1, 8)), jnp.float32)
    segment_ids = draw_segment_ids(jax.random.fold_in(streams_of[11], 71), 0)
    weights = draw_weights(jax.random.fold_in(streams_of[11], 71), 0)
    small_params = draw_small_params(jax.random.fold_in(streams_of[11], 71), 0)
    first_mats = noise(streams_of[5], (D, 6 * D), 0.03, 0.15, ((0, 8),), jnp.float32)
    second_mats = jnp.clip(jnp.exp(math.log(0.00025) - 1.3862944 * jax.random.uniform(streams_of[6], (D, 6 * D), jnp.float32) ** levels(streams_of[6], (D, 6 * D), ((0, 8),), -0.2, 0.2)), 6.25000029685907e-05, 0.00025)
    average_mats = noise(streams_of[7], (D, 6 * D), 0.1, 0.6, ((0, 8),), jnp.float32)
    first_small = noise(streams_of[8], (9, D), 0.03, 0.15, ((1, 8),), jnp.float32)
    second_small = jnp.clip(jnp.exp(math.log(0.00025) - 1.3862944 * jax.random.uniform(streams_of[9], (9, D), jnp.float32) ** levels(streams_of[9], (9, D), ((1, 8),), -0.2, 0.2)), 6.25000029685907e-05, 0.00025)
    average_small = noise(streams_of[10], (9, D), 0.3, 1.5, ((1, 8),), jnp.float32)
    return {"latents": latents, "cotangent": cotangent, "segment_ids": segment_ids, "weights": weights, "small_params": small_params, "first_mats": first_mats, "second_mats": second_mats, "average_mats": average_mats, "first_small": first_small, "second_small": second_small, "average_small": average_small}


@jax.custom_vjp
def low(v):
    return lax.optimization_barrier(v.astype(jnp.bfloat16)).astype(jnp.float32)

@jax.custom_vjp
def low_back(v):
    return v

def low_keep(v):
    return (low(v), None)

def low_pass(kept, grad):
    return (grad,)

def back_keep(v):
    return (v, None)

def back_low(kept, grad):
    return (low(grad),)
low.defvjp(low_keep, low_pass)
low_back.defvjp(back_keep, back_low)
highest = lax.Precision.HIGHEST

def layer_norm(values, gain_row, offset):
    center = values - lax.optimization_barrier(jnp.mean(values, axis=-1, keepdims=True))
    variance = lax.optimization_barrier(jnp.mean(center * center, axis=-1, keepdims=True))
    return center * lax.rsqrt(variance + 1e-05) * gain_row + offset

def attend(queries, keys_part, values_part, query_labels, key_labels):
    query_heads = queries.reshape(queries.shape[0], HEADS, HEAD_DIM)
    key_heads = keys_part.reshape(keys_part.shape[0], HEADS, HEAD_DIM)
    value_heads = values_part.reshape(values_part.shape[0], HEADS, HEAD_DIM)
    scores = jnp.einsum('qhd,khd->hqk', query_heads, key_heads, precision=highest) * HEAD_DIM ** (-0.5)
    allowed = query_labels[:, None] == key_labels[None, :]
    scores = jnp.where(allowed[None], scores, -1e+30)
    probs = jax.nn.softmax(scores, axis=-1)
    mixed_heads = jnp.einsum('hqk,khd->qhd', probs, value_heads, precision=highest)
    return mixed_heads.reshape(queries.shape[0], HEADS * HEAD_DIM)

def row_forward(tokens, labels, weights, small_params):
    hidden = layer_norm(tokens, small_params[0], small_params[1])
    projected = jnp.dot(hidden, weights[:, :3 * D], precision=highest)
    queries = projected[:, :D] + small_params[2]
    keys_part = projected[:, D:2 * D]
    values_part = projected[:, 2 * D:3 * D] + small_params[3]
    mixed_heads = attend(queries, keys_part, values_part, labels, labels)
    residual = tokens + jnp.dot(mixed_heads, weights[:, 3 * D:4 * D], precision=highest) + small_params[4]
    normed = layer_norm(residual, small_params[5], small_params[6])
    expanded = jax.nn.gelu(jnp.dot(normed, weights[:, 4 * D:4 * D + FF], precision=highest) + small_params[7], approximate=True)
    return residual + jnp.dot(expanded, weights[:, 4 * D + FF:], precision=highest) + small_params[8]

def adam_step(parameter, gradient, first_moment, second_moment, average):
    first_new = 0.9 * first_moment + 0.1 * gradient
    second_new = 0.999 * second_moment + 0.001 * gradient * gradient
    first_hat = first_new / (1.0 - 0.9 ** STEP)
    second_hat = second_new / (1.0 - 0.999 ** STEP)
    parameter_new = parameter - 0.05 * (first_hat / (jnp.sqrt(second_hat) + 1e-08) + 0.05 * parameter)
    average_new = 0.99 * average + 0.01 * parameter_new
    return (parameter_new, first_new, second_new, average_new)

def reference(latents, cotangent, segment_ids, weights, small_params, first_mats, second_mats, average_mats, first_small, second_small, average_small):
    row_total = REPS * TOKENS // TOK_DEV
    token_rows = latents.astype(jnp.float32).reshape(row_total, TOK_DEV, D)
    label_rows = segment_ids.reshape(row_total, TOK_DEV).astype(jnp.int32)
    cotangent_rows = cotangent.astype(jnp.float32).reshape(row_total, TOK_DEV, D)

    def forward_all(token_rows, weights, small_params):

        def one_row(row_pair):
            return row_forward(row_pair[0], row_pair[1], weights, small_params)
        return lax.map(jax.checkpoint(one_row), (token_rows, label_rows))
    output_rows, pullback = jax.vjp(forward_all, token_rows, weights, small_params)
    token_grad, weight_grad, small_grad = pullback(cotangent_rows)
    total_norm = jnp.sqrt(jnp.sum(weight_grad * weight_grad) + jnp.sum(small_grad * small_grad))
    clip_limit = 0.25 * math.sqrt(6 * D * D + 9 * D)
    factor = jnp.minimum(1.0, clip_limit / total_norm)
    clipped_mats = weight_grad * factor
    clipped_small = small_grad * factor
    new_weights, first_mats_out, second_mats_out, average_mats_out = adam_step(weights, clipped_mats, first_mats, second_mats, average_mats)
    new_small, first_small_out, second_small_out, average_small_out = adam_step(small_params, clipped_small, first_small, second_small, average_small)
    latents_out = output_rows.reshape(REPS, TOKENS, D)
    latents_grad = token_grad.reshape(REPS, TOKENS, D)
    return (latents_out, latents_grad, total_norm.reshape(1), clipped_mats, clipped_small, new_weights, new_small, first_mats_out, second_mats_out, average_mats_out, first_small_out, second_small_out, average_small_out, new_weights.astype(jnp.bfloat16), new_small.astype(jnp.bfloat16))
```

```python
import functools
import math

import jax
import jax.numpy as jnp
from jax import lax
from jax.experimental import pallas as pl
from jax.experimental.pallas import tpu as pltpu
from jax.sharding import PartitionSpec as P

D = 1024
HEADS = 8
HEAD_DIM = 128
FF = 1024
UNIT = 128
SETS = 3
STEP = 5
SCALE = HEAD_DIM ** (-0.5)

f32 = jnp.float32
bf16 = jnp.bfloat16

NN = (((1,), (0,)), ((), ()))
NT = (((1,), (1,)), ((), ()))
TN = (((0,), (0,)), ((), ()))


def params(mib=56):
    return pltpu.CompilerParams(
        vmem_limit_bytes=mib * 2**20, dimension_semantics=("arbitrary",)
    )


def mm(a, b, dims=NN):
    return lax.dot_general(a, b, dims, preferred_element_type=f32)


def split(x):
    high = x.astype(bf16)
    return high, (x - high.astype(f32)).astype(bf16)


def mm3(ah, al, bh, bl, dims=NN):
    return mm(ah, bh, dims) + (mm(al, bh, dims) + mm(ah, bl, dims))


def cost(products, mib):
    return pl.CostEstimate(
        flops=int(products * 3 * 2 * 1024**3), bytes_accessed=int(mib * 2**20), transcendentals=0
    )


def whole(shape):
    return pl.BlockSpec(shape, lambda *i: (0,) * len(shape))


def rows_of(bm, n):
    return pl.BlockSpec((bm, n), lambda i, *_: (i, 0))


def cols_of(m, bn, first=0):
    return pl.BlockSpec((m, bn), lambda i, *_: (0, first + i))


def shape_of(shape, dtype=f32):
    return jax.ShapeDtypeStruct(shape, dtype)


def norm_parts(x):
    center = x - jnp.mean(x, axis=-1, keepdims=True)
    rstd = lax.rsqrt(jnp.mean(center * center, axis=-1, keepdims=True) + 1e-05)
    return center * rstd, rstd


def norm_back(grad, normed, rstd, gain):
    scaled = grad * gain
    return rstd * (
        scaled
        - jnp.mean(scaled, axis=-1, keepdims=True)
        - normed * jnp.mean(scaled * normed, axis=-1, keepdims=True)
    )


def col_sum(x):
    return jnp.sum(x, axis=0, keepdims=True)


def add_up(ref, value):
    first = pl.program_id(0) == 0

    @pl.when(first)
    def _():
        ref[...] = value

    @pl.when(jnp.logical_not(first))
    def _():
        ref[...] += value


def prep_kernel(x, cot, s, hh, hl, ch, cl, gs8):
    normed, _ = norm_parts(x[...])
    hh[...], hl[...] = split(normed * s[0:1] + s[1:2])
    ch[...], cl[...] = split(cot[...])
    add_up(gs8, col_sum(cot[...]))


def prep(x, cot, small, bm=256):
    t = x.shape[0]
    return pl.pallas_call(
        prep_kernel,
        grid=(t // bm,),
        in_specs=[rows_of(bm, D), rows_of(bm, D), whole((9, D))],
        out_specs=[rows_of(bm, D)] * 4 + [whole((1, D))],
        out_shape=[shape_of((t, D), bf16)] * 4 + [shape_of((1, D))],
        compiler_params=params(),
        cost_estimate=cost(0, 16),
        name="prep",
    )(x, cot, small)


def pair_heads(high, low):
    parts = []
    for head in range(high.shape[1] // HEAD_DIM):
        cut = slice(head * HEAD_DIM, (head + 1) * HEAD_DIM)
        parts += [high[:, cut], low[:, cut]]
    return jnp.concatenate(parts, axis=1)


def proj_kernel(hh, hl, w, bias, out):
    wh, wl = split(w[...])
    out[...] = pair_heads(*split(mm3(hh[...], hl[...], wh, wl) + bias[...]))


def proj(hh, hl, w, bias, bn=256):
    t, n = hh.shape[0], bias.shape[1]
    return pl.pallas_call(
        proj_kernel,
        grid=(n // bn,),
        in_specs=[whole((t, D))] * 2 + [cols_of(D, bn), cols_of(1, bn)],
        out_specs=cols_of(t, 2 * bn),
        out_shape=shape_of((t, 2 * n), bf16),
        compiler_params=params(),
        cost_estimate=cost(n // D, 8 * (n // D) + 4),
        name="proj",
    )(hh, hl, w, bias)


def twice(a):
    return jnp.concatenate([a, a], axis=1)


def halves_sum(x):
    return x[:, :HEAD_DIM] + x[:, HEAD_DIM:]


def pieces(n):
    out, at = [], 0
    while at < n:
        size = min(256, n - at)
        out.append((at, size))
        at += size
    return out


def for_sets(segs, units, body):
    def one(i, carry):
        first, length = segs[2 * i], segs[2 * i + 1]
        for count in range(1, units - SETS + 2):

            @pl.when(length == count)
            def _():
                body(pl.multiple_of(first * UNIT, UNIT), count * UNIT)

        return carry

    lax.fori_loop(0, SETS, one, 0)


def attend_kernel(segs, q, k, v, oh, ol, lse):
    units = q.shape[0] // UNIT

    def body(first, n):
        rows = pl.ds(first, n)
        keys = k[rows, :]
        kh, kl = twice(keys[:, :HEAD_DIM]), twice(keys[:, HEAD_DIM:])
        vals = v[rows, :]
        for at, size in pieces(n):
            sub = pl.ds(pl.multiple_of(first + at, UNIT), size)
            qs = q[sub, :]
            scores = mm(qs, kh, NT) + mm(qs, kl, NT)
            top = jnp.max(scores, axis=-1, keepdims=True)
            p = jnp.exp((scores - top) * SCALE)
            total = jnp.sum(p, axis=-1, keepdims=True)
            ph, plow = split(p)
            o = halves_sum(mm(ph, vals) + mm(plow, vals)) / total
            oh[sub, :], ol[sub, :] = split(o)
            level = top * SCALE + jnp.log(total)
            for u in range(size // UNIT):
                tile = jnp.broadcast_to(level[u * UNIT : (u + 1) * UNIT], (UNIT, UNIT))
                lse[0, :, pl.ds(pl.multiple_of(first + at + u * UNIT, UNIT), UNIT)] = tile.T[0:8]

    for_sets(segs, units, body)


def attend(segs, qkv):
    t = qkv.shape[0]
    head = lambda first: pl.BlockSpec((t, 2 * HEAD_DIM), lambda i, *_: (0, first + i))
    return pl.pallas_call(
        attend_kernel,
        grid_spec=pltpu.PrefetchScalarGridSpec(
            num_scalar_prefetch=1,
            grid=(HEADS,),
            in_specs=[head(0), head(HEADS), head(2 * HEADS)],
            out_specs=[cols_of(t, HEAD_DIM)] * 2
            + [pl.BlockSpec((1, 8, t), lambda i, *_: (i, 0, 0))],
        ),
        out_shape=[shape_of((t, D), bf16)] * 2 + [shape_of((HEADS, 8, t))],
        compiler_params=params(),
        cost_estimate=cost(2, 16),
        name="attend",
    )(segs, qkv, qkv, qkv)


def attend_back_kernel(
    segs, q, k, v, do, oh, ol, lse, dqh, dql, dkh, dkl, dvh, dvl, gq, gv, drow, qsum, vsum
):
    units = q.shape[0] // UNIT
    for u in range(units):
        cut = slice(u * UNIT, (u + 1) * UNIT)
        grad = do[cut, :].astype(f32)
        out = oh[cut, :].astype(f32) + ol[cut, :].astype(f32)
        tile = (halves_sum(grad) * out).T
        drow[:, cut] = jnp.broadcast_to(col_sum(tile), (8, UNIT))
    qsum[...] = jnp.zeros_like(qsum)
    vsum[...] = jnp.zeros_like(vsum)

    def body(first, n):
        rows = pl.ds(first, n)
        keys, vals = k[rows, :], v[rows, :]
        dk = dv = None
        for at, size in pieces(n):
            sub = pl.ds(pl.multiple_of(first + at, UNIT), size)
            qs, grad = q[sub, :], do[sub, :]
            scores = mm(keys, twice(qs[:, :HEAD_DIM]), NT) + mm(keys, twice(qs[:, HEAD_DIM:]), NT)
            p = jnp.exp(scores * SCALE - lse[0, 0:1, sub])
            dp = mm(vals, twice(grad[:, :HEAD_DIM]), NT) + mm(vals, twice(grad[:, HEAD_DIM:]), NT)
            ds = p * (dp - drow[0:1, sub])
            ph, plow = split(p)
            dsh, dsl = split(ds)
            dv_part = mm(ph, grad) + mm(plow, grad)
            dk_part = mm(dsh, qs) + mm(dsl, qs)
            dv = dv_part if dv is None else dv + dv_part
            dk = dk_part if dk is None else dk + dk_part
            dq = halves_sum(mm(dsh, keys, TN) + mm(dsl, keys, TN)) * SCALE
            dqh[sub, :], dql[sub, :] = split(dq)
            qsum[0:1, :] += col_sum(dq)
        dk = halves_sum(dk) * SCALE
        dv = halves_sum(dv)
        dkh[rows, :], dkl[rows, :] = split(dk)
        dvh[rows, :], dvl[rows, :] = split(dv)
        vsum[0:1, :] += col_sum(dv)

    for_sets(segs, units, body)
    gq[...] = qsum[0:1, :]
    gv[...] = vsum[0:1, :]


def attend_back(segs, qkv, do, oh, ol, lse):
    t = qkv.shape[0]
    head = lambda first: pl.BlockSpec((t, 2 * HEAD_DIM), lambda i, *_: (0, first + i))
    return pl.pallas_call(
        attend_back_kernel,
        grid_spec=pltpu.PrefetchScalarGridSpec(
            num_scalar_prefetch=1,
            grid=(HEADS,),
            in_specs=[head(0), head(HEADS), head(2 * HEADS), head(0)]
            + [cols_of(t, HEAD_DIM)] * 2
            + [pl.BlockSpec((1, 8, t), lambda i, *_: (i, 0, 0))],
            out_specs=[cols_of(t, HEAD_DIM)] * 6 + [cols_of(1, HEAD_DIM)] * 2,
            scratch_shapes=[
                pltpu.VMEM((8, t), f32),
                pltpu.VMEM((8, HEAD_DIM), f32),
                pltpu.VMEM((8, HEAD_DIM), f32),
            ],
        ),
        out_shape=[shape_of((t, D), bf16)] * 6 + [shape_of((1, D))] * 2,
        compiler_params=params(),
        cost_estimate=cost(5, 36),
        name="attend_back",
    )(segs, qkv, qkv, qkv, do, oh, ol, lse)


def split_once(w, wh, wl):
    @pl.when(pl.program_id(0) == 0)
    def _():
        wh[...], wl[...] = split(w[...])


def out_proj_kernel(oh, ol, w, x, s, x1, h2h, h2l, wh, wl):
    split_once(w, wh, wl)
    value = x[...] + mm3(oh[...], ol[...], wh[...], wl[...]) + s[4:5]
    x1[...] = value
    normed, _ = norm_parts(value)
    h2h[...], h2l[...] = split(normed * s[5:6] + s[6:7])


def out_proj(oh, ol, w, x, small, bm=256):
    t = x.shape[0]
    return pl.pallas_call(
        out_proj_kernel,
        grid=(t // bm,),
        in_specs=[rows_of(bm, D)] * 2 + [whole((D, D)), rows_of(bm, D), whole((9, D))],
        out_specs=[rows_of(bm, D)] * 3,
        out_shape=[shape_of((t, D)), shape_of((t, D), bf16), shape_of((t, D), bf16)],
        scratch_shapes=[pltpu.VMEM((D, D), bf16)] * 2,
        compiler_params=params(),
        cost_estimate=cost(1, 20),
        name="out_proj",
    )(oh, ol, w, x, small)


ROOT = math.sqrt(2.0 / math.pi)


def up_kernel(hh, hl, w, s, z, uh, ul):
    wh, wl = split(w[...])
    value = mm3(hh[...], hl[...], wh, wl) + s[7:8]
    z[...] = value
    bent = jnp.tanh(ROOT * (value + 0.044715 * value * value * value))
    uh[...], ul[...] = split(0.5 * value * (1.0 + bent))


def up(hh, hl, w, small, bn=256):
    t = hh.shape[0]
    return pl.pallas_call(
        up_kernel,
        grid=(FF // bn,),
        in_specs=[whole((t, D))] * 2 + [cols_of(D, bn), cols_of(9, bn)],
        out_specs=[cols_of(t, bn)] * 3,
        out_shape=[shape_of((t, FF)), shape_of((t, FF), bf16), shape_of((t, FF), bf16)],
        compiler_params=params(),
        cost_estimate=cost(1, 16),
        name="up",
    )(hh, hl, w, small)


def down_kernel(uh, ul, w, x1, s, out):
    wh, wl = split(w[...])
    out[...] = x1[...] + mm3(uh[...], ul[...], wh, wl) + s[8:9]


def down(uh, ul, w, x1, small, bn=256):
    t = uh.shape[0]
    return pl.pallas_call(
        down_kernel,
        grid=(D // bn,),
        in_specs=[whole((t, FF))] * 2 + [cols_of(FF, bn), cols_of(t, bn), cols_of(9, bn)],
        out_specs=cols_of(t, bn),
        out_shape=shape_of((t, D)),
        compiler_params=params(),
        cost_estimate=cost(1, 16),
        name="down",
    )(uh, ul, w, x1, small)


def outer_kernel(ah, al, dh, dl, out, th, tl):
    @pl.when(pl.program_id(0) == 0)
    def _():
        th[...] = ah[...].T
        tl[...] = al[...].T

    out[...] = mm3(th[...], tl[...], dh[...], dl[...])


def outer(ah, al, dh, dl, bn=256):
    t, m = ah.shape
    n = dh.shape[1]
    return pl.pallas_call(
        outer_kernel,
        grid=(n // bn,),
        in_specs=[whole((t, m))] * 2 + [cols_of(t, bn)] * 2,
        out_specs=cols_of(m, bn),
        out_shape=shape_of((m, n)),
        scratch_shapes=[pltpu.VMEM((m, t), bf16)] * 2,
        compiler_params=params(),
        cost_estimate=cost(1, 12),
        name="outer",
    )(ah, al, dh, dl)


def down_back_kernel(ch, cl, w, z, dzh, dzl, gs7):
    wh, wl = split(w[...])
    du = mm3(ch[...], cl[...], wh, wl, NT)
    value = z[...]
    square = value * value
    bent = jnp.tanh(ROOT * (value + 0.044715 * value * square))
    slope = 0.5 * (1.0 + bent) + 0.5 * value * (1.0 - bent * bent) * (
        ROOT * (1.0 + 3.0 * 0.044715 * square)
    )
    dz = du * slope
    dzh[...], dzl[...] = split(dz)
    gs7[...] = col_sum(dz)


def down_back(ch, cl, w, z, bn=256):
    t = ch.shape[0]
    return pl.pallas_call(
        down_back_kernel,
        grid=(FF // bn,),
        in_specs=[whole((t, D))] * 2 + [rows_of(bn, D), cols_of(t, bn)],
        out_specs=[cols_of(t, bn)] * 2 + [cols_of(1, bn)],
        out_shape=[shape_of((t, FF), bf16)] * 2 + [shape_of((1, FF))],
        compiler_params=params(),
        cost_estimate=cost(1, 16),
        name="down_back",
    )(ch, cl, w, z)


def up_back_kernel(dzh, dzl, w, x1, cot, s, dx1, dxh, dxl, gs4, gs5, gs6, wh, wl):
    split_once(w, wh, wl)
    dh2 = mm3(dzh[...], dzl[...], wh[...], wl[...], NT)
    normed, rstd = norm_parts(x1[...])
    grad = cot[...] + norm_back(dh2, normed, rstd, s[5:6])
    dx1[...] = grad
    dxh[...], dxl[...] = split(grad)
    add_up(gs4, col_sum(grad))
    add_up(gs5, col_sum(dh2 * normed))
    add_up(gs6, col_sum(dh2))


def up_back(dzh, dzl, w, x1, cot, small, bm=256):
    t = x1.shape[0]
    return pl.pallas_call(
        up_back_kernel,
        grid=(t // bm,),
        in_specs=[rows_of(bm, FF)] * 2 + [whole((D, FF))] + [rows_of(bm, D)] * 2 + [whole((9, D))],
        out_specs=[rows_of(bm, D)] * 3 + [whole((1, D))] * 3,
        out_shape=[shape_of((t, D)), shape_of((t, D), bf16), shape_of((t, D), bf16)]
        + [shape_of((1, D))] * 3,
        scratch_shapes=[pltpu.VMEM((D, FF), bf16)] * 2,
        compiler_params=params(),
        cost_estimate=cost(1, 24),
        name="up_back",
    )(dzh, dzl, w, x1, cot, small)


def out_proj_back_kernel(dxh, dxl, w, do):
    wh, wl = split(w[...])
    do[...] = pair_heads(*split(mm3(dxh[...], dxl[...], wh, wl, NT)))


def out_proj_back(dxh, dxl, w, bn=256):
    t = dxh.shape[0]
    return pl.pallas_call(
        out_proj_back_kernel,
        grid=(D // bn,),
        in_specs=[whole((t, D))] * 2 + [rows_of(bn, D)],
        out_specs=cols_of(t, 2 * bn),
        out_shape=shape_of((t, 2 * D), bf16),
        compiler_params=params(),
        cost_estimate=cost(1, 12),
        name="out_proj_back",
    )(dxh, dxl, w)


def proj_back_kernel(
    dqh, dql, dkh, dkl, dvh, dvl, wq, wk, wv, x, dx1, s, out, gs0, gs1, wh, wl
):
    @pl.when(pl.program_id(0) == 0)
    def _():
        for j, w in enumerate((wq, wk, wv)):
            wh[j], wl[j] = split(w[...])

    dh = mm3(dqh[...], dql[...], wh[0], wl[0], NT)
    dh += mm3(dkh[...], dkl[...], wh[1], wl[1], NT)
    dh += mm3(dvh[...], dvl[...], wh[2], wl[2], NT)
    normed, rstd = norm_parts(x[...])
    out[...] = dx1[...] + norm_back(dh, normed, rstd, s[0:1])
    add_up(gs0, col_sum(dh * normed))
    add_up(gs1, col_sum(dh))


def proj_back(grads, wq, wk, wv, x, dx1, small, bm=256):
    t = x.shape[0]
    once = pl.BlockSpec((D, D), lambda i: (0, 0), pipeline_mode=pl.Buffered(1))
    return pl.pallas_call(
        proj_back_kernel,
        grid=(t // bm,),
        in_specs=[rows_of(bm, D)] * 6 + [once] * 3 + [rows_of(bm, D)] * 2 + [whole((9, D))],
        out_specs=[rows_of(bm, D)] + [whole((1, D))] * 2,
        out_shape=[shape_of((t, D))] + [shape_of((1, D))] * 2,
        scratch_shapes=[pltpu.VMEM((3, D, D), bf16)] * 2,
        compiler_params=params(),
        cost_estimate=cost(3, 36),
        name="proj_back",
    )(*grads, wq, wk, wv, x, dx1, small)


def adam_step(parameter, gradient, first_moment, second_moment, average):
    first_new = 0.9 * first_moment + 0.1 * gradient
    second_new = 0.999 * second_moment + 0.001 * gradient * gradient
    first_hat = first_new / (1.0 - 0.9**STEP)
    second_hat = second_new / (1.0 - 0.999**STEP)
    parameter_new = parameter - 0.05 * (
        first_hat / (jnp.sqrt(second_hat) + 1e-08) + 0.05 * parameter
    )
    average_new = 0.99 * average + 0.01 * parameter_new
    return (parameter_new, first_new, second_new, average_new)


def set_bounds(segment_ids):
    ids = segment_ids[0, ::UNIT]
    order, sets = (ids - ids[0])[None, :], jnp.arange(SETS, dtype=jnp.int32)[:, None]
    lengths = jnp.sum((order == sets).astype(jnp.int32), axis=1)
    firsts = jnp.sum((order < sets).astype(jnp.int32), axis=1)
    return jnp.stack([firsts, lengths], axis=1).reshape(-1).astype(jnp.int32)


def shards(
    latents,
    cotangent,
    segment_ids,
    weights,
    small_params,
    first_mats,
    second_mats,
    average_mats,
    first_small,
    second_small,
    average_small,
):
    full, small = (
        lax.all_gather(weights, "rows", axis=0, tiled=True),
        lax.all_gather(small_params, "rows", axis=1, tiled=True),
    )
    segs = set_bounds(segment_ids)
    x, cot = latents[0], cotangent[0]
    wq, wk, wv, wo, wup, wdown = (full[:, j * D : (j + 1) * D] for j in range(6))
    bias = jnp.concatenate([small[2], jnp.zeros((D,), f32), small[3]])[None]

    hh, hl, ch, cl, gs8 = prep(x, cot, small)
    qkv = proj(hh, hl, full, bias)
    oh, ol, lse = attend(segs, qkv)
    x1, h2h, h2l = out_proj(oh, ol, wo, x, small)
    z, uh, ul = up(h2h, h2l, wup, small)
    output = down(uh, ul, wdown, x1, small)
    g_down = outer(uh, ul, ch, cl)
    dzh, dzl, gs7 = down_back(ch, cl, wdown, z)
    g_up = outer(h2h, h2l, dzh, dzl)
    dx1, dxh, dxl, gs4, gs5, gs6 = up_back(dzh, dzl, wup, x1, cot, small)
    g_out = outer(oh, ol, dxh, dxl)
    do = out_proj_back(dxh, dxl, wo)
    *grads, gs2, gs3 = attend_back(segs, qkv, do, oh, ol, lse)
    g_qkv = [outer(hh, hl, grads[2 * j], grads[2 * j + 1]) for j in range(3)]
    token_grad, gs0, gs1 = proj_back(grads, wq, wk, wv, x, dx1, small)
    weight_grad = jnp.concatenate(g_qkv + [g_out, g_up, g_down], axis=1)
    small_grad = jnp.concatenate([gs0, gs1, gs2, gs3, gs4, gs5, gs6, gs7, gs8], axis=0)

    part_weights, part_small = (
        lax.psum_scatter(weight_grad, "rows", scatter_dimension=0, tiled=True),
        lax.psum_scatter(small_grad, "rows", scatter_dimension=1, tiled=True),
    )
    sum_weights, sum_small = lax.psum((part_weights, part_small), "rep")
    squares = lax.psum(jnp.sum(sum_weights * sum_weights) + jnp.sum(sum_small * sum_small), "rows")
    total_norm = jnp.sqrt(squares)
    clip_limit = 0.25 * math.sqrt(6 * D * D + 9 * D)
    factor = jnp.minimum(1.0, clip_limit / total_norm)
    clipped_mats = sum_weights * factor
    clipped_small = sum_small * factor
    new_weights, first_mats_out, second_mats_out, average_mats_out = adam_step(
        weights, clipped_mats, first_mats, second_mats, average_mats
    )
    new_small, first_small_out, second_small_out, average_small_out = adam_step(
        small_params, clipped_small, first_small, second_small, average_small
    )
    return (
        output[None],
        token_grad[None],
        total_norm.reshape(1),
        clipped_mats,
        clipped_small,
        new_weights,
        new_small,
        first_mats_out,
        second_mats_out,
        average_mats_out,
        first_small_out,
        second_small_out,
        average_small_out,
        new_weights.astype(bf16),
        new_small.astype(bf16),
    )


def solution(mesh):
    tokens, mats, small = P("rep", "rows", None), P("rows", None), P(None, "rows")
    in_specs = (tokens, tokens, P("rep", "rows")) + (mats, small) + (mats,) * 3 + (small,) * 3
    out_specs = (
        (tokens, tokens, P(), mats, small, mats, small) + (mats,) * 3 + (small,) * 3 + (mats, small)
    )
    return jax.shard_map(shards, mesh=mesh, in_specs=in_specs, out_specs=out_specs, check_vma=False)
```

```python
import functools
import math

import jax
import jax.numpy as jnp
from jax import lax
from jax.experimental import pallas as pl
from jax.experimental.pallas import tpu as pltpu
from jax.sharding import PartitionSpec as P

D = 1024
HEADS = 8
HEAD_DIM = 128
FF = 1024
UNIT = 128
SETS = 3
STEP = 5
SCALE = HEAD_DIM ** (-0.5)

f32 = jnp.float32
bf16 = jnp.bfloat16

NN = (((1,), (0,)), ((), ()))
NT = (((1,), (1,)), ((), ()))
TN = (((0,), (0,)), ((), ()))


def params(mib=56):
    return pltpu.CompilerParams(
        vmem_limit_bytes=mib * 2**20, dimension_semantics=("arbitrary",)
    )


def mm(a, b, dims=NN):
    return lax.dot_general(a, b, dims, preferred_element_type=f32)


def split(x):
    high = x.astype(bf16)
    return high, (x - high.astype(f32)).astype(bf16)


def mm3(ah, al, bh, bl, dims=NN):
    return mm(ah, bh, dims) + (mm(al, bh, dims) + mm(ah, bl, dims))


def cost(products, mib):
    return pl.CostEstimate(
        flops=int(products * 3 * 2 * 1024**3), bytes_accessed=int(mib * 2**20), transcendentals=0
    )


def whole(shape):
    return pl.BlockSpec(shape, lambda *i: (0,) * len(shape))


def rows_of(bm, n, column=0):
    return pl.BlockSpec((bm, n), lambda i, *_: (i, column))


def matrix(j):
    return pl.BlockSpec((D, D), lambda i: (0, j), pipeline_mode=pl.Buffered(1))


def cols_of(m, bn, first=0):
    return pl.BlockSpec((m, bn), lambda i, *_: (0, first + i))


def shape_of(shape, dtype=f32):
    return jax.ShapeDtypeStruct(shape, dtype)


def norm_parts(x):
    center = x - jnp.mean(x, axis=-1, keepdims=True)
    rstd = lax.rsqrt(jnp.mean(center * center, axis=-1, keepdims=True) + 1e-05)
    return center * rstd, rstd


def norm_back(grad, normed, rstd, gain):
    scaled = grad * gain
    return rstd * (
        scaled
        - jnp.mean(scaled, axis=-1, keepdims=True)
        - normed * jnp.mean(scaled * normed, axis=-1, keepdims=True)
    )


def col_sum(x):
    return jnp.sum(x, axis=0, keepdims=True)


def add_up(ref, value):
    first = pl.program_id(0) == 0

    @pl.when(first)
    def _():
        ref[...] = value

    @pl.when(jnp.logical_not(first))
    def _():
        ref[...] += value


def prep_kernel(x, cot, s, hh, hl, ch, cl, gs8):
    normed, _ = norm_parts(x[...])
    hh[...], hl[...] = split(normed * s[0:1] + s[1:2])
    ch[...], cl[...] = split(cot[...])
    add_up(gs8, col_sum(cot[...]))


def prep(x, cot, small, bm=256):
    t = x.shape[0]
    return pl.pallas_call(
        prep_kernel,
        grid=(t // bm,),
        in_specs=[rows_of(bm, D), rows_of(bm, D), whole((9, D))],
        out_specs=[rows_of(bm, D)] * 4 + [whole((1, D))],
        out_shape=[shape_of((t, D), bf16)] * 4 + [shape_of((1, D))],
        compiler_params=params(),
        cost_estimate=cost(0, 16),
        name="prep",
    )(x, cot, small)


def pair_heads(high, low):
    parts = []
    for head in range(high.shape[1] // HEAD_DIM):
        cut = slice(head * HEAD_DIM, (head + 1) * HEAD_DIM)
        parts += [high[:, cut], low[:, cut]]
    return jnp.concatenate(parts, axis=1)


def proj_kernel(hh, hl, w, bias, out):
    wh, wl = split(w[...])
    out[...] = pair_heads(*split(mm3(hh[...], hl[...], wh, wl) + bias[...]))


def proj(hh, hl, w, bias, bn=256):
    t, n = hh.shape[0], bias.shape[1]
    return pl.pallas_call(
        proj_kernel,
        grid=(n // bn,),
        in_specs=[whole((t, D))] * 2 + [cols_of(D, bn), cols_of(1, bn)],
        out_specs=cols_of(t, 2 * bn),
        out_shape=shape_of((t, 2 * n), bf16),
        compiler_params=params(),
        cost_estimate=cost(n // D, 8 * (n // D) + 4),
        name="proj",
    )(hh, hl, w, bias)


def twice(a):
    return jnp.concatenate([a, a], axis=1)


def halves_sum(x):
    return x[:, :HEAD_DIM] + x[:, HEAD_DIM:]


def pieces(n):
    out, at = [], 0
    while at < n:
        size = min(256, n - at)
        out.append((at, size))
        at += size
    return out


def for_sets(segs, units, body):
    def one(i, carry):
        first, length = segs[2 * i], segs[2 * i + 1]
        for count in range(1, units - SETS + 2):

            @pl.when(length == count)
            def _():
                body(pl.multiple_of(first * UNIT, UNIT), count * UNIT)

        return carry

    lax.fori_loop(0, SETS, one, 0)


def attend_kernel(segs, q, k, v, oh, ol, lse):
    units = q.shape[0] // UNIT

    def body(first, n):
        rows = pl.ds(first, n)
        keys = k[rows, :]
        kh, kl = twice(keys[:, :HEAD_DIM]), twice(keys[:, HEAD_DIM:])
        vals = v[rows, :]
        for at, size in pieces(n):
            sub = pl.ds(pl.multiple_of(first + at, UNIT), size)
            qs = q[sub, :]
            scores = mm(qs, kh, NT) + mm(qs, kl, NT)
            top = jnp.max(scores, axis=-1, keepdims=True)
            p = jnp.exp((scores - top) * SCALE)
            total = jnp.sum(p, axis=-1, keepdims=True)
            ph, plow = split(p)
            o = halves_sum(mm(ph, vals) + mm(plow, vals)) / total
            oh[sub, :], ol[sub, :] = split(o)
            level = top * SCALE + jnp.log(total)
            for u in range(size // UNIT):
                tile = jnp.broadcast_to(level[u * UNIT : (u + 1) * UNIT], (UNIT, UNIT))
                lse[0, :, pl.ds(pl.multiple_of(first + at + u * UNIT, UNIT), UNIT)] = tile.T[0:8]

    for_sets(segs, units, body)


def attend(segs, qkv):
    t = qkv.shape[0]
    head = lambda first: pl.BlockSpec((t, 2 * HEAD_DIM), lambda i, *_: (0, first + i))
    return pl.pallas_call(
        attend_kernel,
        grid_spec=pltpu.PrefetchScalarGridSpec(
            num_scalar_prefetch=1,
            grid=(HEADS,),
            in_specs=[head(0), head(HEADS), head(2 * HEADS)],
            out_specs=[cols_of(t, HEAD_DIM)] * 2
            + [pl.BlockSpec((1, 8, t), lambda i, *_: (i, 0, 0))],
        ),
        out_shape=[shape_of((t, D), bf16)] * 2 + [shape_of((HEADS, 8, t))],
        compiler_params=params(),
        cost_estimate=cost(2, 16),
        name="attend",
    )(segs, qkv, qkv, qkv)


def attend_back_kernel(
    segs, q, k, v, do, oh, ol, lse, dqh, dql, dkh, dkl, dvh, dvl, gq, gv, drow, qsum, vsum
):
    units = q.shape[0] // UNIT
    for u in range(units):
        cut = slice(u * UNIT, (u + 1) * UNIT)
        grad = do[cut, :].astype(f32)
        out = oh[cut, :].astype(f32) + ol[cut, :].astype(f32)
        tile = (halves_sum(grad) * out).T
        drow[:, cut] = jnp.broadcast_to(col_sum(tile), (8, UNIT))
    qsum[...] = jnp.zeros_like(qsum)
    vsum[...] = jnp.zeros_like(vsum)

    def body(first, n):
        rows = pl.ds(first, n)
        keys, vals = k[rows, :], v[rows, :]
        dk = dv = None
        for at, size in pieces(n):
            sub = pl.ds(pl.multiple_of(first + at, UNIT), size)
            qs, grad = q[sub, :], do[sub, :]
            scores = mm(keys, twice(qs[:, :HEAD_DIM]), NT) + mm(keys, twice(qs[:, HEAD_DIM:]), NT)
            p = jnp.exp(scores * SCALE - lse[0, 0:1, sub])
            dp = mm(vals, twice(grad[:, :HEAD_DIM]), NT) + mm(vals, twice(grad[:, HEAD_DIM:]), NT)
            ds = p * (dp - drow[0:1, sub])
            ph, plow = split(p)
            dsh, dsl = split(ds)
            dv_part = mm(ph, grad) + mm(plow, grad)
            dk_part = mm(dsh, qs) + mm(dsl, qs)
            dv = dv_part if dv is None else dv + dv_part
            dk = dk_part if dk is None else dk + dk_part
            dq = halves_sum(mm(dsh, keys, TN) + mm(dsl, keys, TN)) * SCALE
            dqh[sub, :], dql[sub, :] = split(dq)
            qsum[0:1, :] += col_sum(dq)
        dk = halves_sum(dk) * SCALE
        dv = halves_sum(dv)
        dkh[rows, :], dkl[rows, :] = split(dk)
        dvh[rows, :], dvl[rows, :] = split(dv)
        vsum[0:1, :] += col_sum(dv)

    for_sets(segs, units, body)
    gq[...] = qsum[0:1, :]
    gv[...] = vsum[0:1, :]


def attend_back(segs, qkv, do, oh, ol, lse):
    t = qkv.shape[0]
    head = lambda first: pl.BlockSpec((t, 2 * HEAD_DIM), lambda i, *_: (0, first + i))
    return pl.pallas_call(
        attend_back_kernel,
        grid_spec=pltpu.PrefetchScalarGridSpec(
            num_scalar_prefetch=1,
            grid=(HEADS,),
            in_specs=[head(0), head(HEADS), head(2 * HEADS), head(0)]
            + [cols_of(t, HEAD_DIM)] * 2
            + [pl.BlockSpec((1, 8, t), lambda i, *_: (i, 0, 0))],
            out_specs=[cols_of(t, HEAD_DIM)] * 6 + [cols_of(1, HEAD_DIM)] * 2,
            scratch_shapes=[
                pltpu.VMEM((8, t), f32),
                pltpu.VMEM((8, HEAD_DIM), f32),
                pltpu.VMEM((8, HEAD_DIM), f32),
            ],
        ),
        out_shape=[shape_of((t, D), bf16)] * 6 + [shape_of((1, D))] * 2,
        compiler_params=params(),
        cost_estimate=cost(5, 36),
        name="attend_back",
    )(segs, qkv, qkv, qkv, do, oh, ol, lse)


MESH = pl.DeviceIdType.MESH
CHUNK = 256
AHEAD, SPREAD, SWAP, USE = 4, 2, 4, 6


def wait_bytes(ref, sem):
    pltpu.make_async_copy(ref, ref, sem).wait()


def gather_kernel(
    w, own_small, x, cot,
    full, small, hh, hl, ch, cl, gs8, qkv,
    pieces, own, xbuf, cbuf, hhb, hlb, chb, clb, wbuf, obuf,
    small_send, small_recv, own_sem, send_sem, core_send, own_recv,
    z_recv, x_recv, y_recv, fx_recv, fy_recv, core_recv, in_sem, out_sem, w_sem, q_sem,
):
    rep, rows = lax.axis_index("rep"), lax.axis_index("rows")
    z, c = rows // 2, rows % 2
    x_next, y_next = rep // 2 * 2 + (1 - rep % 2), (1 - rep // 2) * 2 + rep % 2
    shard = w.shape[0]
    quarter, half = shard // 4, shard // 8
    chunks = w.shape[1] // CHUNK
    proj_chunks = 3 * D // CHUNK

    x_in = pltpu.make_async_copy(x, xbuf, in_sem.at[0])
    c_in = pltpu.make_async_copy(cot, cbuf, in_sem.at[1])
    x_in.start()
    c_in.start()
    own_in = pltpu.make_async_copy(w, own, own_sem)
    own_in.start()

    barrier = pltpu.get_barrier_semaphore()
    peers = [(rep, (rows + k) % 8) for k in range(1, 8)] + [(x_next, rows), (y_next, rows)]
    for peer in peers:
        pl.semaphore_signal(barrier, inc=1, device_id=peer, device_id_type=MESH)
    pl.semaphore_wait(barrier, len(peers))

    def send(src, dst, sem, recv, device):
        pltpu.make_async_remote_copy(
            src_ref=src, dst_ref=dst, send_sem=sem, recv_sem=recv, device_id=device,
            device_id_type=MESH,
        ).start()

    for k in range(1, 8):
        send(own_small, pieces.at[k - 1], small_send.at[k - 1], small_recv.at[k - 1], (rep, (rows + k) % 8))

    def cols(t):
        return pl.ds(pl.multiple_of(t * CHUNK, CHUNK), CHUNK)

    def place(zz, first, count, t):
        at = (zz * 2 + c) * shard + first
        return full.at[pl.ds(pl.multiple_of(at, half), count), cols(t)]

    def start_z(t):
        src = w.at[pl.ds(pl.multiple_of(rep * quarter, quarter), quarter), cols(t)]
        for k in range(1, 4):
            send(src, place(z, rep * quarter, quarter, t), send_sem, z_recv.at[t], (rep, (z + k) % 4 * 2 + c))

    for t in range(AHEAD):
        start_z(t)
    send(w, full.at[pl.ds(rows * shard, shard), :], core_send, own_recv, (rep, z * 2 + 1 - c))

    for k in range(1, 8):
        pltpu.make_async_copy(own_small, pieces.at[k - 1], small_recv.at[k - 1]).wait()
        pltpu.make_async_copy(own_small, pieces.at[k - 1], small_send.at[k - 1]).wait()
    width = own_small.shape[1]
    small[:, pl.ds(pl.multiple_of(rows * width, width), width)] = own_small[...]
    for k in range(1, 8):
        at = pl.multiple_of((rows + 8 - k) % 8 * width, width)
        small[:, pl.ds(at, width)] = pieces[k - 1]

    own_in.wait()
    own_out = pltpu.make_async_copy(own, full.at[pl.ds(rows * shard, shard), :], own_sem)
    own_out.start()
    x_in.wait()

    def norm_rows(i, carry):
        at = pl.ds(pl.multiple_of(i * 128, 128), 128)
        normed, _ = norm_parts(xbuf[at, :])
        hhb[at, :], hlb[at, :] = split(normed * small[0:1, :] + small[1:2, :])
        return carry

    lax.fori_loop(0, x.shape[0] // 128, norm_rows, 0)
    h_out = [
        pltpu.make_async_copy(hhb, hh, out_sem.at[0]),
        pltpu.make_async_copy(hlb, hl, out_sem.at[1]),
    ]
    for copy in h_out:
        copy.start()
    own_out.wait()
    wait_bytes(w, own_recv)

    def q_out(t):
        at = pl.ds(pl.multiple_of(t * 2 * CHUNK, 2 * CHUNK), 2 * CHUNK)
        return pltpu.make_async_copy(obuf.at[t % 2], qkv.at[:, at], q_sem.at[t % 2])

    def step(s, carry):
        @pl.when(s < chunks)
        def _():
            wait_bytes(w.at[0 : 3 * quarter, 0:CHUNK], z_recv.at[s])
            for k in range(1, 4):
                part = place((z + k) % 4, rep * quarter, quarter, s)
                send(part, part, send_sem, x_recv.at[s], (x_next, rows))
                send(part, part, send_sem, y_recv.at[s], (y_next, rows))

        @pl.when(s + AHEAD < chunks)
        def _():
            start_z(s + AHEAD)

        @pl.when(jnp.logical_and(s >= SPREAD, s < chunks + SPREAD))
        def _():
            t = s - SPREAD
            wait_bytes(w.at[0 : 3 * quarter, 0:CHUNK], x_recv.at[t])
            wait_bytes(w.at[0 : 3 * quarter, 0:CHUNK], y_recv.at[t])
            for k in range(1, 4):
                part = place((z + k) % 4, x_next * quarter, half, t)
                send(part, part, send_sem, fy_recv.at[t], (y_next, rows))
                part = place((z + k) % 4, y_next * quarter + half, half, t)
                send(part, part, send_sem, fx_recv.at[t], (x_next, rows))

        @pl.when(jnp.logical_and(s >= SWAP, s < chunks + SWAP))
        def _():
            t = s - SWAP
            wait_bytes(w.at[0 : 3 * half, 0:CHUNK], fx_recv.at[t])
            wait_bytes(w.at[0 : 3 * half, 0:CHUNK], fy_recv.at[t])
            for k in range(1, 4):
                part = place((z + k) % 4, 0, shard, t)
                send(part, part, core_send, core_recv.at[t], (rep, z * 2 + 1 - c))

        @pl.when(s >= USE)
        def _():
            wait_bytes(full.at[0 : 3 * shard, 0:CHUNK], core_recv.at[s - USE])

        @pl.when(jnp.logical_and(s >= USE, s < proj_chunks + USE))
        def _():
            t = s - USE
            load = pltpu.make_async_copy(full.at[:, cols(t)], wbuf, w_sem)
            load.start()

            @pl.when(t >= 2)
            def _():
                q_out(t).wait()

            load.wait()
            wh, wl = split(wbuf[...])
            kind = t // (D // CHUNK)
            at = pl.ds(pl.multiple_of(t % (D // CHUNK) * CHUNK, CHUNK), CHUNK)
            bias = jnp.where(kind == 0, small[2:3, at], jnp.where(kind == 2, small[3:4, at], 0.0))
            obuf[t % 2] = pair_heads(*split(mm3(hhb[...], hlb[...], wh, wl) + bias))
            q_out(t).start()

        @pl.when(s == proj_chunks + USE)
        def _():
            c_in.wait()

            def split_rows(i, total):
                at = pl.ds(pl.multiple_of(i * 128, 128), 128)
                value = cbuf[at, :]
                chb[at, :], clb[at, :] = split(value)
                return total + col_sum(value)

            gs8[...] = lax.fori_loop(0, cot.shape[0] // 128, split_rows, jnp.zeros((1, D), f32))
            pltpu.make_async_copy(chb, ch, out_sem.at[2]).start()
            pltpu.make_async_copy(clb, cl, out_sem.at[3]).start()

        return carry

    lax.fori_loop(0, chunks + USE, step, 0)
    q_out(proj_chunks - 2).wait()
    q_out(proj_chunks - 1).wait()
    for copy in h_out:
        copy.wait()
    pltpu.make_async_copy(chb, ch, out_sem.at[2]).wait()
    pltpu.make_async_copy(clb, cl, out_sem.at[3]).wait()
    wait_bytes(full.at[0 : 3 * quarter + 6 * quarter + 6 * half, :], send_sem)
    wait_bytes(full.at[0 : 4 * shard, :], core_send)


def gather(weights, small_params, x, cot):
    shard, width = weights.shape
    t = x.shape[0]
    chunks = width // CHUNK
    hbm = pl.BlockSpec(memory_space=pl.ANY)
    vmem = pl.BlockSpec(memory_space=pltpu.VMEM)
    dma = pltpu.SemaphoreType.DMA
    return pl.pallas_call(
        gather_kernel,
        in_specs=[hbm, vmem, hbm, hbm],
        out_specs=[hbm, vmem, hbm, hbm, hbm, hbm, vmem, hbm],
        out_shape=[shape_of((8 * shard, width)), shape_of((9, D))]
        + [shape_of((t, D), bf16)] * 4
        + [shape_of((1, D)), shape_of((t, 6 * D), bf16)],
        scratch_shapes=[pltpu.VMEM((7,) + small_params.shape, f32), pltpu.VMEM((shard, width), f32)]
        + [pltpu.VMEM((t, D), f32)] * 2
        + [pltpu.VMEM((t, D), bf16)] * 4
        + [pltpu.VMEM((D, CHUNK), f32), pltpu.VMEM((2, t, 2 * CHUNK), bf16)]
        + [dma((7,)), dma((7,)), dma, dma, dma, dma]
        + [dma((chunks,))] * 6
        + [dma((2,)), dma((4,)), dma, dma((2,))],
        compiler_params=pltpu.CompilerParams(
            vmem_limit_bytes=50 * 2**20, collective_id=0, has_side_effects=True
        ),
        cost_estimate=cost(3, 64),
        name="gather",
    )(weights, small_params, x, cot)


def split_once(w, wh, wl):
    @pl.when(pl.program_id(0) == 0)
    def _():
        wh[...], wl[...] = split(w[...])


def out_proj_kernel(oh, ol, w, x, s, x1, h2h, h2l, wh, wl):
    split_once(w, wh, wl)
    value = x[...] + mm3(oh[...], ol[...], wh[...], wl[...]) + s[4:5]
    x1[...] = value
    normed, _ = norm_parts(value)
    h2h[...], h2l[...] = split(normed * s[5:6] + s[6:7])


def out_proj(oh, ol, w, x, small, bm=256):
    t = x.shape[0]
    return pl.pallas_call(
        out_proj_kernel,
        grid=(t // bm,),
        in_specs=[rows_of(bm, D)] * 2 + [matrix(3), rows_of(bm, D), whole((9, D))],
        out_specs=[rows_of(bm, D)] * 3,
        out_shape=[shape_of((t, D)), shape_of((t, D), bf16), shape_of((t, D), bf16)],
        scratch_shapes=[pltpu.VMEM((D, D), bf16)] * 2,
        compiler_params=params(),
        cost_estimate=cost(1, 20),
        name="out_proj",
    )(oh, ol, w, x, small)


ROOT = math.sqrt(2.0 / math.pi)


def up_kernel(hh, hl, w, s, z, uh, ul):
    wh, wl = split(w[...])
    value = mm3(hh[...], hl[...], wh, wl) + s[7:8]
    z[...] = value
    bent = jnp.tanh(ROOT * (value + 0.044715 * value * value * value))
    uh[...], ul[...] = split(0.5 * value * (1.0 + bent))


def up(hh, hl, w, small, bn=256):
    t = hh.shape[0]
    return pl.pallas_call(
        up_kernel,
        grid=(FF // bn,),
        in_specs=[whole((t, D))] * 2 + [cols_of(D, bn, 4 * D // bn), cols_of(9, bn)],
        out_specs=[cols_of(t, bn)] * 3,
        out_shape=[shape_of((t, FF)), shape_of((t, FF), bf16), shape_of((t, FF), bf16)],
        compiler_params=params(),
        cost_estimate=cost(1, 16),
        name="up",
    )(hh, hl, w, small)


def down_kernel(uh, ul, w, x1, s, out):
    wh, wl = split(w[...])
    out[...] = x1[...] + mm3(uh[...], ul[...], wh, wl) + s[8:9]


def down(uh, ul, w, x1, small, bn=256):
    t = uh.shape[0]
    return pl.pallas_call(
        down_kernel,
        grid=(D // bn,),
        in_specs=[whole((t, FF))] * 2
        + [cols_of(FF, bn, 5 * D // bn), cols_of(t, bn), cols_of(9, bn)],
        out_specs=cols_of(t, bn),
        out_shape=shape_of((t, D)),
        compiler_params=params(),
        cost_estimate=cost(1, 16),
        name="down",
    )(uh, ul, w, x1, small)


def outer_kernel(ah, al, dh, dl, out, th, tl):
    @pl.when(pl.program_id(0) == 0)
    def _():
        th[...] = ah[...].T
        tl[...] = al[...].T

    out[...] = mm3(th[...], tl[...], dh[...], dl[...])


def outer(ah, al, dh, dl, bn=256):
    t, m = ah.shape
    n = dh.shape[1]
    return pl.pallas_call(
        outer_kernel,
        grid=(n // bn,),
        in_specs=[whole((t, m))] * 2 + [cols_of(t, bn)] * 2,
        out_specs=cols_of(m, bn),
        out_shape=shape_of((m, n)),
        scratch_shapes=[pltpu.VMEM((m, t), bf16)] * 2,
        compiler_params=params(),
        cost_estimate=cost(1, 12),
        name="outer",
    )(ah, al, dh, dl)


def down_back_kernel(ch, cl, w, z, dzh, dzl, gs7):
    wh, wl = split(w[...])
    du = mm3(ch[...], cl[...], wh, wl, NT)
    value = z[...]
    square = value * value
    bent = jnp.tanh(ROOT * (value + 0.044715 * value * square))
    slope = 0.5 * (1.0 + bent) + 0.5 * value * (1.0 - bent * bent) * (
        ROOT * (1.0 + 3.0 * 0.044715 * square)
    )
    dz = du * slope
    dzh[...], dzl[...] = split(dz)
    gs7[...] = col_sum(dz)


def down_back(ch, cl, w, z, bn=256):
    t = ch.shape[0]
    return pl.pallas_call(
        down_back_kernel,
        grid=(FF // bn,),
        in_specs=[whole((t, D))] * 2 + [rows_of(bn, D, 5), cols_of(t, bn)],
        out_specs=[cols_of(t, bn)] * 2 + [cols_of(1, bn)],
        out_shape=[shape_of((t, FF), bf16)] * 2 + [shape_of((1, FF))],
        compiler_params=params(),
        cost_estimate=cost(1, 16),
        name="down_back",
    )(ch, cl, w, z)


def up_back_kernel(dzh, dzl, w, x1, cot, s, dx1, dxh, dxl, gs4, gs5, gs6, wh, wl):
    split_once(w, wh, wl)
    dh2 = mm3(dzh[...], dzl[...], wh[...], wl[...], NT)
    normed, rstd = norm_parts(x1[...])
    grad = cot[...] + norm_back(dh2, normed, rstd, s[5:6])
    dx1[...] = grad
    dxh[...], dxl[...] = split(grad)
    add_up(gs4, col_sum(grad))
    add_up(gs5, col_sum(dh2 * normed))
    add_up(gs6, col_sum(dh2))


def up_back(dzh, dzl, w, x1, cot, small, bm=256):
    t = x1.shape[0]
    return pl.pallas_call(
        up_back_kernel,
        grid=(t // bm,),
        in_specs=[rows_of(bm, FF)] * 2 + [matrix(4)] + [rows_of(bm, D)] * 2 + [whole((9, D))],
        out_specs=[rows_of(bm, D)] * 3 + [whole((1, D))] * 3,
        out_shape=[shape_of((t, D)), shape_of((t, D), bf16), shape_of((t, D), bf16)]
        + [shape_of((1, D))] * 3,
        scratch_shapes=[pltpu.VMEM((D, FF), bf16)] * 2,
        compiler_params=params(),
        cost_estimate=cost(1, 24),
        name="up_back",
    )(dzh, dzl, w, x1, cot, small)


def out_proj_back_kernel(dxh, dxl, w, do):
    wh, wl = split(w[...])
    do[...] = pair_heads(*split(mm3(dxh[...], dxl[...], wh, wl, NT)))


def out_proj_back(dxh, dxl, w, bn=256):
    t = dxh.shape[0]
    return pl.pallas_call(
        out_proj_back_kernel,
        grid=(D // bn,),
        in_specs=[whole((t, D))] * 2 + [rows_of(bn, D, 3)],
        out_specs=cols_of(t, 2 * bn),
        out_shape=shape_of((t, 2 * D), bf16),
        compiler_params=params(),
        cost_estimate=cost(1, 12),
        name="out_proj_back",
    )(dxh, dxl, w)


def proj_back_kernel(
    dqh, dql, dkh, dkl, dvh, dvl, wq, wk, wv, x, dx1, s, out, gs0, gs1, wh, wl
):
    @pl.when(pl.program_id(0) == 0)
    def _():
        for j, w in enumerate((wq, wk, wv)):
            wh[j], wl[j] = split(w[...])

    dh = mm3(dqh[...], dql[...], wh[0], wl[0], NT)
    dh += mm3(dkh[...], dkl[...], wh[1], wl[1], NT)
    dh += mm3(dvh[...], dvl[...], wh[2], wl[2], NT)
    normed, rstd = norm_parts(x[...])
    out[...] = dx1[...] + norm_back(dh, normed, rstd, s[0:1])
    add_up(gs0, col_sum(dh * normed))
    add_up(gs1, col_sum(dh))


def proj_back(grads, w, x, dx1, small, bm=256):
    t = x.shape[0]
    return pl.pallas_call(
        proj_back_kernel,
        grid=(t // bm,),
        in_specs=[rows_of(bm, D)] * 6 + [matrix(j) for j in range(3)] + [rows_of(bm, D)] * 2 + [whole((9, D))],
        out_specs=[rows_of(bm, D)] + [whole((1, D))] * 2,
        out_shape=[shape_of((t, D))] + [shape_of((1, D))] * 2,
        scratch_shapes=[pltpu.VMEM((3, D, D), bf16)] * 2,
        compiler_params=params(),
        cost_estimate=cost(3, 36),
        name="proj_back",
    )(*grads, w, w, w, x, dx1, small)


def adam_step(parameter, gradient, first_moment, second_moment, average):
    first_new = 0.9 * first_moment + 0.1 * gradient
    second_new = 0.999 * second_moment + 0.001 * gradient * gradient
    first_hat = first_new / (1.0 - 0.9**STEP)
    second_hat = second_new / (1.0 - 0.999**STEP)
    parameter_new = parameter - 0.05 * (
        first_hat / (jnp.sqrt(second_hat) + 1e-08) + 0.05 * parameter
    )
    average_new = 0.99 * average + 0.01 * parameter_new
    return (parameter_new, first_new, second_new, average_new)


def set_bounds(segment_ids):
    ids = segment_ids[0, ::UNIT]
    order, sets = (ids - ids[0])[None, :], jnp.arange(SETS, dtype=jnp.int32)[:, None]
    lengths = jnp.sum((order == sets).astype(jnp.int32), axis=1)
    firsts = jnp.sum((order < sets).astype(jnp.int32), axis=1)
    return jnp.stack([firsts, lengths], axis=1).reshape(-1).astype(jnp.int32)


def shards(
    reps,
    latents,
    cotangent,
    segment_ids,
    weights,
    small_params,
    first_mats,
    second_mats,
    average_mats,
    first_small,
    second_small,
    average_small,
):
    segs = set_bounds(segment_ids)
    x, cot = latents[0], cotangent[0]
    if reps == 4 and weights.shape[0] * 8 == D:
        full, small, hh, hl, ch, cl, gs8, qkv = gather(weights, small_params, x, cot)
    else:
        full, small = (
            lax.all_gather(weights, "rows", axis=0, tiled=True),
            lax.all_gather(small_params, "rows", axis=1, tiled=True),
        )
        bias = jnp.concatenate([small[2], jnp.zeros((D,), f32), small[3]])[None]
        hh, hl, ch, cl, gs8 = prep(x, cot, small)
        qkv = proj(hh, hl, full, bias)
    oh, ol, lse = attend(segs, qkv)
    x1, h2h, h2l = out_proj(oh, ol, full, x, small)
    z, uh, ul = up(h2h, h2l, full, small)
    output = down(uh, ul, full, x1, small)
    g_down = outer(uh, ul, ch, cl)
    dzh, dzl, gs7 = down_back(ch, cl, full, z)
    g_up = outer(h2h, h2l, dzh, dzl)
    dx1, dxh, dxl, gs4, gs5, gs6 = up_back(dzh, dzl, full, x1, cot, small)
    g_out = outer(oh, ol, dxh, dxl)
    do = out_proj_back(dxh, dxl, full)
    *grads, gs2, gs3 = attend_back(segs, qkv, do, oh, ol, lse)
    g_qkv = [outer(hh, hl, grads[2 * j], grads[2 * j + 1]) for j in range(3)]
    token_grad, gs0, gs1 = proj_back(grads, full, x, dx1, small)
    weight_grad = jnp.concatenate(g_qkv + [g_out, g_up, g_down], axis=1)
    small_grad = jnp.concatenate([gs0, gs1, gs2, gs3, gs4, gs5, gs6, gs7, gs8], axis=0)

    part_weights, part_small = (
        lax.psum_scatter(weight_grad, "rows", scatter_dimension=0, tiled=True),
        lax.psum_scatter(small_grad, "rows", scatter_dimension=1, tiled=True),
    )
    sum_weights, sum_small = lax.psum((part_weights, part_small), "rep")
    squares = lax.psum(jnp.sum(sum_weights * sum_weights) + jnp.sum(sum_small * sum_small), "rows")
    total_norm = jnp.sqrt(squares)
    clip_limit = 0.25 * math.sqrt(6 * D * D + 9 * D)
    factor = jnp.minimum(1.0, clip_limit / total_norm)
    clipped_mats = sum_weights * factor
    clipped_small = sum_small * factor
    new_weights, first_mats_out, second_mats_out, average_mats_out = adam_step(
        weights, clipped_mats, first_mats, second_mats, average_mats
    )
    new_small, first_small_out, second_small_out, average_small_out = adam_step(
        small_params, clipped_small, first_small, second_small, average_small
    )
    return (
        output[None],
        token_grad[None],
        total_norm.reshape(1),
        clipped_mats,
        clipped_small,
        new_weights,
        new_small,
        first_mats_out,
        second_mats_out,
        average_mats_out,
        first_small_out,
        second_small_out,
        average_small_out,
        new_weights.astype(bf16),
        new_small.astype(bf16),
    )


def solution(mesh):
    tokens, mats, small = P("rep", "rows", None), P("rows", None), P(None, "rows")
    in_specs = (tokens, tokens, P("rep", "rows")) + (mats, small) + (mats,) * 3 + (small,) * 3
    out_specs = (
        (tokens, tokens, P(), mats, small, mats, small) + (mats,) * 3 + (small,) * 3 + (mats, small)
    )
    step = functools.partial(shards, mesh.shape["rep"])
    return jax.shard_map(step, mesh=mesh, in_specs=in_specs, out_specs=out_specs, check_vma=False)
```

```python
import functools
import math

import jax
import jax.numpy as jnp
from jax import lax
from jax.experimental import pallas as pl
from jax.experimental.pallas import tpu as pltpu
from jax.sharding import PartitionSpec as P

D = 1024
HEADS = 8
HEAD_DIM = 128
FF = 1024
UNIT = 128
SETS = 3
STEP = 5
SCALE = HEAD_DIM ** (-0.5)

f32 = jnp.float32
bf16 = jnp.bfloat16

NN = (((1,), (0,)), ((), ()))
NT = (((1,), (1,)), ((), ()))
TN = (((0,), (0,)), ((), ()))


def params(mib=56):
    return pltpu.CompilerParams(
        vmem_limit_bytes=mib * 2**20, dimension_semantics=("arbitrary",)
    )


def mm(a, b, dims=NN):
    return lax.dot_general(a, b, dims, preferred_element_type=f32)


def split(x):
    high = x.astype(bf16)
    return high, (x - high.astype(f32)).astype(bf16)


def mm3(ah, al, bh, bl, dims=NN):
    return mm(ah, bh, dims) + (mm(al, bh, dims) + mm(ah, bl, dims))


def cost(products, mib):
    return pl.CostEstimate(
        flops=int(products * 3 * 2 * 1024**3), bytes_accessed=int(mib * 2**20), transcendentals=0
    )


def whole(shape):
    return pl.BlockSpec(shape, lambda *i: (0,) * len(shape))


def rows_of(bm, n, column=0):
    return pl.BlockSpec((bm, n), lambda i, *_: (i, column))


def matrix(j):
    return pl.BlockSpec((D, D), lambda i: (0, j), pipeline_mode=pl.Buffered(1))


def cols_of(m, bn, first=0):
    return pl.BlockSpec((m, bn), lambda i, *_: (0, first + i))


def shape_of(shape, dtype=f32):
    return jax.ShapeDtypeStruct(shape, dtype)


def norm_parts(x):
    center = x - jnp.mean(x, axis=-1, keepdims=True)
    rstd = lax.rsqrt(jnp.mean(center * center, axis=-1, keepdims=True) + 1e-05)
    return center * rstd, rstd


def norm_back(grad, normed, rstd, gain):
    scaled = grad * gain
    return rstd * (
        scaled
        - jnp.mean(scaled, axis=-1, keepdims=True)
        - normed * jnp.mean(scaled * normed, axis=-1, keepdims=True)
    )


def col_sum(x):
    return jnp.sum(x, axis=0, keepdims=True)


def add_up(ref, value):
    first = pl.program_id(0) == 0

    @pl.when(first)
    def _():
        ref[...] = value

    @pl.when(jnp.logical_not(first))
    def _():
        ref[...] += value


def prep_kernel(x, cot, s, hh, hl, ch, cl, gs8):
    normed, _ = norm_parts(x[...])
    hh[...], hl[...] = split(normed * s[0:1] + s[1:2])
    ch[...], cl[...] = split(cot[...])
    add_up(gs8, col_sum(cot[...]))


def prep(x, cot, small, bm=256):
    t = x.shape[0]
    return pl.pallas_call(
        prep_kernel,
        grid=(t // bm,),
        in_specs=[rows_of(bm, D), rows_of(bm, D), whole((9, D))],
        out_specs=[rows_of(bm, D)] * 4 + [whole((1, D))],
        out_shape=[shape_of((t, D), bf16)] * 4 + [shape_of((1, D))],
        compiler_params=params(),
        cost_estimate=cost(0, 16),
        name="prep",
    )(x, cot, small)


def pair_heads(high, low):
    parts = []
    for head in range(high.shape[1] // HEAD_DIM):
        cut = slice(head * HEAD_DIM, (head + 1) * HEAD_DIM)
        parts += [high[:, cut], low[:, cut]]
    return jnp.concatenate(parts, axis=1)


def proj_kernel(hh, hl, w, bias, out):
    wh, wl = split(w[...])
    out[...] = pair_heads(*split(mm3(hh[...], hl[...], wh, wl) + bias[...]))


def proj(hh, hl, w, bias, bn=256):
    t, n = hh.shape[0], bias.shape[1]
    return pl.pallas_call(
        proj_kernel,
        grid=(n // bn,),
        in_specs=[whole((t, D))] * 2 + [cols_of(D, bn), cols_of(1, bn)],
        out_specs=cols_of(t, 2 * bn),
        out_shape=shape_of((t, 2 * n), bf16),
        compiler_params=params(),
        cost_estimate=cost(n // D, 8 * (n // D) + 4),
        name="proj",
    )(hh, hl, w, bias)


def twice(a):
    return jnp.concatenate([a, a], axis=1)


def halves_sum(x):
    return x[:, :HEAD_DIM] + x[:, HEAD_DIM:]


def pieces(n):
    out, at = [], 0
    while at < n:
        size = min(256, n - at)
        out.append((at, size))
        at += size
    return out


def for_sets(segs, units, body):
    def one(i, carry):
        first, length = segs[2 * i], segs[2 * i + 1]
        for count in range(1, units - SETS + 2):

            @pl.when(length == count)
            def _():
                body(pl.multiple_of(first * UNIT, UNIT), count * UNIT)

        return carry

    lax.fori_loop(0, SETS, one, 0)


def attend_kernel(segs, q, k, v, oh, ol, lse):
    units = q.shape[0] // UNIT

    def body(first, n):
        rows = pl.ds(first, n)
        keys = k[rows, :]
        kh, kl = twice(keys[:, :HEAD_DIM]), twice(keys[:, HEAD_DIM:])
        vals = v[rows, :]
        for at, size in pieces(n):
            sub = pl.ds(pl.multiple_of(first + at, UNIT), size)
            qs = q[sub, :]
            scores = mm(qs, kh, NT) + mm(qs, kl, NT)
            top = jnp.max(scores, axis=-1, keepdims=True)
            p = jnp.exp((scores - top) * SCALE)
            total = jnp.sum(p, axis=-1, keepdims=True)
            ph, plow = split(p)
            o = halves_sum(mm(ph, vals) + mm(plow, vals)) / total
            oh[sub, :], ol[sub, :] = split(o)
            level = top * SCALE + jnp.log(total)
            for u in range(size // UNIT):
                tile = jnp.broadcast_to(level[u * UNIT : (u + 1) * UNIT], (UNIT, UNIT))
                lse[0, :, pl.ds(pl.multiple_of(first + at + u * UNIT, UNIT), UNIT)] = tile.T[0:8]

    for_sets(segs, units, body)


def attend(segs, qkv):
    t = qkv.shape[0]
    head = lambda first: pl.BlockSpec((t, 2 * HEAD_DIM), lambda i, *_: (0, first + i))
    return pl.pallas_call(
        attend_kernel,
        grid_spec=pltpu.PrefetchScalarGridSpec(
            num_scalar_prefetch=1,
            grid=(HEADS,),
            in_specs=[head(0), head(HEADS), head(2 * HEADS)],
            out_specs=[cols_of(t, HEAD_DIM)] * 2
            + [pl.BlockSpec((1, 8, t), lambda i, *_: (i, 0, 0))],
        ),
        out_shape=[shape_of((t, D), bf16)] * 2 + [shape_of((HEADS, 8, t))],
        compiler_params=params(),
        cost_estimate=cost(2, 16),
        name="attend",
    )(segs, qkv, qkv, qkv)


def attend_back_kernel(
    segs, q, k, v, do, oh, ol, lse, dqh, dql, dkh, dkl, dvh, dvl, gq, gv, drow, qsum, vsum
):
    units = q.shape[0] // UNIT
    for u in range(units):
        cut = slice(u * UNIT, (u + 1) * UNIT)
        grad = do[cut, :].astype(f32)
        out = oh[cut, :].astype(f32) + ol[cut, :].astype(f32)
        tile = (halves_sum(grad) * out).T
        drow[:, cut] = jnp.broadcast_to(col_sum(tile), (8, UNIT))
    qsum[...] = jnp.zeros_like(qsum)
    vsum[...] = jnp.zeros_like(vsum)

    def body(first, n):
        rows = pl.ds(first, n)
        keys, vals = k[rows, :], v[rows, :]
        dk = dv = None
        for at, size in pieces(n):
            sub = pl.ds(pl.multiple_of(first + at, UNIT), size)
            qs, grad = q[sub, :], do[sub, :]
            scores = mm(keys, twice(qs[:, :HEAD_DIM]), NT) + mm(keys, twice(qs[:, HEAD_DIM:]), NT)
            p = jnp.exp(scores * SCALE - lse[0, 0:1, sub])
            dp = mm(vals, twice(grad[:, :HEAD_DIM]), NT) + mm(vals, twice(grad[:, HEAD_DIM:]), NT)
            ds = p * (dp - drow[0:1, sub])
            ph, plow = split(p)
            dsh, dsl = split(ds)
            dv_part = mm(ph, grad) + mm(plow, grad)
            dk_part = mm(dsh, qs) + mm(dsl, qs)
            dv = dv_part if dv is None else dv + dv_part
            dk = dk_part if dk is None else dk + dk_part
            dq = halves_sum(mm(dsh, keys, TN) + mm(dsl, keys, TN)) * SCALE
            dqh[sub, :], dql[sub, :] = split(dq)
            qsum[0:1, :] += col_sum(dq)
        dk = halves_sum(dk) * SCALE
        dv = halves_sum(dv)
        dkh[rows, :], dkl[rows, :] = split(dk)
        dvh[rows, :], dvl[rows, :] = split(dv)
        vsum[0:1, :] += col_sum(dv)

    for_sets(segs, units, body)
    gq[...] = qsum[0:1, :]
    gv[...] = vsum[0:1, :]


def attend_back(segs, qkv, do, oh, ol, lse):
    t = qkv.shape[0]
    head = lambda first: pl.BlockSpec((t, 2 * HEAD_DIM), lambda i, *_: (0, first + i))
    return pl.pallas_call(
        attend_back_kernel,
        grid_spec=pltpu.PrefetchScalarGridSpec(
            num_scalar_prefetch=1,
            grid=(HEADS,),
            in_specs=[head(0), head(HEADS), head(2 * HEADS), head(0)]
            + [cols_of(t, HEAD_DIM)] * 2
            + [pl.BlockSpec((1, 8, t), lambda i, *_: (i, 0, 0))],
            out_specs=[cols_of(t, HEAD_DIM)] * 6 + [cols_of(1, HEAD_DIM)] * 2,
            scratch_shapes=[
                pltpu.VMEM((8, t), f32),
                pltpu.VMEM((8, HEAD_DIM), f32),
                pltpu.VMEM((8, HEAD_DIM), f32),
            ],
        ),
        out_shape=[shape_of((t, D), bf16)] * 6 + [shape_of((1, D))] * 2,
        compiler_params=params(),
        cost_estimate=cost(5, 36),
        name="attend_back",
    )(segs, qkv, qkv, qkv, do, oh, ol, lse)


MESH = pl.DeviceIdType.MESH
CHUNK = 256
AHEAD, SPREAD, SWAP, USE = 4, 2, 4, 6


def wait_bytes(ref, sem):
    pltpu.make_async_copy(ref, ref, sem).wait()


def gather_kernel(
    w, own_small, x, cot,
    full, small, hh, hl, ch, cl, gs8, qkv,
    pieces, own, xbuf, cbuf, hhb, hlb, chb, clb, wbuf, obuf,
    small_send, small_recv, own_sem, send_sem, core_send, own_recv,
    z_recv, x_recv, y_recv, fx_recv, fy_recv, core_recv, in_sem, out_sem, w_sem, q_sem,
):
    rep, rows = lax.axis_index("rep"), lax.axis_index("rows")
    z, c = rows // 2, rows % 2
    x_next, y_next = rep // 2 * 2 + (1 - rep % 2), (1 - rep // 2) * 2 + rep % 2
    shard = w.shape[0]
    quarter, half = shard // 4, shard // 8
    chunks = w.shape[1] // CHUNK
    proj_chunks = 3 * D // CHUNK

    x_in = pltpu.make_async_copy(x, xbuf, in_sem.at[0])
    c_in = pltpu.make_async_copy(cot, cbuf, in_sem.at[1])
    x_in.start()
    c_in.start()
    own_in = pltpu.make_async_copy(w, own, own_sem)
    own_in.start()

    barrier = pltpu.get_barrier_semaphore()
    peers = [(rep, (rows + k) % 8) for k in range(1, 8)] + [(x_next, rows), (y_next, rows)]
    for peer in peers:
        pl.semaphore_signal(barrier, inc=1, device_id=peer, device_id_type=MESH)
    pl.semaphore_wait(barrier, len(peers))

    def send(src, dst, sem, recv, device):
        pltpu.make_async_remote_copy(
            src_ref=src, dst_ref=dst, send_sem=sem, recv_sem=recv, device_id=device,
            device_id_type=MESH,
        ).start()

    for k in range(1, 8):
        send(own_small, pieces.at[k - 1], small_send.at[k - 1], small_recv.at[k - 1], (rep, (rows + k) % 8))

    def cols(t):
        return pl.ds(pl.multiple_of(t * CHUNK, CHUNK), CHUNK)

    def place(zz, first, count, t):
        at = (zz * 2 + c) * shard + first
        return full.at[pl.ds(pl.multiple_of(at, half), count), cols(t)]

    def start_z(t):
        src = w.at[pl.ds(pl.multiple_of(rep * quarter, quarter), quarter), cols(t)]
        for k in range(1, 4):
            send(src, place(z, rep * quarter, quarter, t), send_sem, z_recv.at[t], (rep, (z + k) % 4 * 2 + c))

    for t in range(AHEAD):
        start_z(t)
    send(w, full.at[pl.ds(rows * shard, shard), :], core_send, own_recv, (rep, z * 2 + 1 - c))

    for k in range(1, 8):
        pltpu.make_async_copy(own_small, pieces.at[k - 1], small_recv.at[k - 1]).wait()
        pltpu.make_async_copy(own_small, pieces.at[k - 1], small_send.at[k - 1]).wait()
    width = own_small.shape[1]
    small[:, pl.ds(pl.multiple_of(rows * width, width), width)] = own_small[...]
    for k in range(1, 8):
        at = pl.multiple_of((rows + 8 - k) % 8 * width, width)
        small[:, pl.ds(at, width)] = pieces[k - 1]

    own_in.wait()
    own_out = pltpu.make_async_copy(own, full.at[pl.ds(rows * shard, shard), :], own_sem)
    own_out.start()
    x_in.wait()

    def norm_rows(i, carry):
        at = pl.ds(pl.multiple_of(i * 128, 128), 128)
        normed, _ = norm_parts(xbuf[at, :])
        hhb[at, :], hlb[at, :] = split(normed * small[0:1, :] + small[1:2, :])
        return carry

    lax.fori_loop(0, x.shape[0] // 128, norm_rows, 0)
    h_out = [
        pltpu.make_async_copy(hhb, hh, out_sem.at[0]),
        pltpu.make_async_copy(hlb, hl, out_sem.at[1]),
    ]
    for copy in h_out:
        copy.start()
    own_out.wait()
    wait_bytes(w, own_recv)

    def q_out(t):
        at = pl.ds(pl.multiple_of(t * 2 * CHUNK, 2 * CHUNK), 2 * CHUNK)
        return pltpu.make_async_copy(obuf.at[t % 2], qkv.at[:, at], q_sem.at[t % 2])

    def step(s, carry):
        @pl.when(s < chunks)
        def _():
            wait_bytes(w.at[0 : 3 * quarter, 0:CHUNK], z_recv.at[s])
            for k in range(1, 4):
                part = place((z + k) % 4, rep * quarter, quarter, s)
                send(part, part, send_sem, x_recv.at[s], (x_next, rows))
                send(part, part, send_sem, y_recv.at[s], (y_next, rows))

        @pl.when(s + AHEAD < chunks)
        def _():
            start_z(s + AHEAD)

        @pl.when(jnp.logical_and(s >= SPREAD, s < chunks + SPREAD))
        def _():
            t = s - SPREAD
            wait_bytes(w.at[0 : 3 * quarter, 0:CHUNK], x_recv.at[t])
            wait_bytes(w.at[0 : 3 * quarter, 0:CHUNK], y_recv.at[t])
            for k in range(1, 4):
                part = place((z + k) % 4, x_next * quarter, half, t)
                send(part, part, send_sem, fy_recv.at[t], (y_next, rows))
                part = place((z + k) % 4, y_next * quarter + half, half, t)
                send(part, part, send_sem, fx_recv.at[t], (x_next, rows))

        @pl.when(jnp.logical_and(s >= SWAP, s < chunks + SWAP))
        def _():
            t = s - SWAP
            wait_bytes(w.at[0 : 3 * half, 0:CHUNK], fx_recv.at[t])
            wait_bytes(w.at[0 : 3 * half, 0:CHUNK], fy_recv.at[t])
            for k in range(1, 4):
                part = place((z + k) % 4, 0, shard, t)
                send(part, part, core_send, core_recv.at[t], (rep, z * 2 + 1 - c))

        @pl.when(s >= USE)
        def _():
            wait_bytes(full.at[0 : 3 * shard, 0:CHUNK], core_recv.at[s - USE])

        @pl.when(jnp.logical_and(s >= USE, s < proj_chunks + USE))
        def _():
            t = s - USE
            load = pltpu.make_async_copy(full.at[:, cols(t)], wbuf, w_sem)
            load.start()

            @pl.when(t >= 2)
            def _():
                q_out(t).wait()

            load.wait()
            wh, wl = split(wbuf[...])
            kind = t // (D // CHUNK)
            at = pl.ds(pl.multiple_of(t % (D // CHUNK) * CHUNK, CHUNK), CHUNK)
            bias = jnp.where(kind == 0, small[2:3, at], jnp.where(kind == 2, small[3:4, at], 0.0))
            obuf[t % 2] = pair_heads(*split(mm3(hhb[...], hlb[...], wh, wl) + bias))
            q_out(t).start()

        @pl.when(s == proj_chunks + USE)
        def _():
            c_in.wait()

            def split_rows(i, total):
                at = pl.ds(pl.multiple_of(i * 128, 128), 128)
                value = cbuf[at, :]
                chb[at, :], clb[at, :] = split(value)
                return total + col_sum(value)

            gs8[...] = lax.fori_loop(0, cot.shape[0] // 128, split_rows, jnp.zeros((1, D), f32))
            pltpu.make_async_copy(chb, ch, out_sem.at[2]).start()
            pltpu.make_async_copy(clb, cl, out_sem.at[3]).start()

        return carry

    lax.fori_loop(0, chunks + USE, step, 0)
    q_out(proj_chunks - 2).wait()
    q_out(proj_chunks - 1).wait()
    for copy in h_out:
        copy.wait()
    pltpu.make_async_copy(chb, ch, out_sem.at[2]).wait()
    pltpu.make_async_copy(clb, cl, out_sem.at[3]).wait()
    wait_bytes(full.at[0 : 3 * quarter + 6 * quarter + 6 * half, :], send_sem)
    wait_bytes(full.at[0 : 4 * shard, :], core_send)


def gather(weights, small_params, x, cot):
    shard, width = weights.shape
    t = x.shape[0]
    chunks = width // CHUNK
    hbm = pl.BlockSpec(memory_space=pl.ANY)
    vmem = pl.BlockSpec(memory_space=pltpu.VMEM)
    dma = pltpu.SemaphoreType.DMA
    return pl.pallas_call(
        gather_kernel,
        in_specs=[hbm, vmem, hbm, hbm],
        out_specs=[hbm, vmem, hbm, hbm, hbm, hbm, vmem, hbm],
        out_shape=[shape_of((8 * shard, width)), shape_of((9, D))]
        + [shape_of((t, D), bf16)] * 4
        + [shape_of((1, D)), shape_of((t, 6 * D), bf16)],
        scratch_shapes=[pltpu.VMEM((7,) + small_params.shape, f32), pltpu.VMEM((shard, width), f32)]
        + [pltpu.VMEM((t, D), f32)] * 2
        + [pltpu.VMEM((t, D), bf16)] * 4
        + [pltpu.VMEM((D, CHUNK), f32), pltpu.VMEM((2, t, 2 * CHUNK), bf16)]
        + [dma((7,)), dma((7,)), dma, dma, dma, dma]
        + [dma((chunks,))] * 6
        + [dma((2,)), dma((4,)), dma, dma((2,))],
        compiler_params=pltpu.CompilerParams(
            vmem_limit_bytes=50 * 2**20, collective_id=0, has_side_effects=True
        ),
        cost_estimate=cost(3, 64),
        name="gather",
    )(weights, small_params, x, cot)


STAGES = 6


def reduce_kernel(
    hh, hl, dqh, dql, dkh, dkl, dvh, dvl, w, x, dx1, g_down, g_up, g_out, gs_rest, gain,
    out, total, small_total, norm,
    gbuf, core_in, a1, b1, a2, b2, zsrc, z_in, th, tl, dbuf, wbuf, acc, xbuf, dxbuf, obuf,
    spart, srow, srep, norm_in,
    gsend, send_sem, core_recv, a1_recv, b1_recv, a2_recv, b2_recv, z_recv,
    gx_recv, gy_recv, fx_recv, fy_recv,
    g_in, d_in, w_in, ln_in, ln_out, s_send, s_recv, r_send, r_recv, n_send, n_recv,
):
    rep, rows = lax.axis_index("rep"), lax.axis_index("rows")
    px, py, z, c = rep % 2, rep // 2, rows // 2, rows % 2
    x_peer, y_peer = (py * 2 + 1 - px, rows), ((1 - py) * 2 + px, rows)
    core_peer = (rep, z * 2 + 1 - c)
    chunks = core_in.shape[0]
    ready = chunks // 2
    per = D // CHUNK
    t_rows = x.shape[0]

    barrier = pltpu.get_barrier_semaphore()
    peers = [(rep, (rows + k) % 8) for k in range(1, 8)] + [((rep + k) % 4, rows) for k in range(1, 4)]
    for peer in peers:
        pl.semaphore_signal(barrier, inc=1, device_id=peer, device_id_type=MESH)

    def send(src, dst, sem, recv, device):
        pltpu.make_async_remote_copy(
            src_ref=src, dst_ref=dst, send_sem=sem, recv_sem=recv, device_id=device,
            device_id_type=MESH,
        ).start()

    def cols(t):
        return pl.ds(pl.multiple_of(t * CHUNK, CHUNK), CHUNK)

    def load_ready(t, start):
        for j, source in enumerate((g_down, g_up, g_out)):

            @pl.when(t // per == j)
            def _():
                copy = pltpu.make_async_copy(source.at[:, :, :, :, :, :, cols(t % per)], gbuf.at[t % 3], g_in.at[t % 3])
                copy.start() if start else copy.wait()

    def load_grad(u, start):
        for j, (high, low) in enumerate(((dqh, dql), (dkh, dkl), (dvh, dvl))):

            @pl.when(u // per == j)
            def _():
                for i, source in enumerate((high, low)):
                    copy = pltpu.make_async_copy(
                        source.at[:, cols(u % per)], dbuf.at[u % 2, i], d_in.at[u % 2, i]
                    )
                    copy.start() if start else copy.wait()

        copy = pltpu.make_async_copy(w.at[:, cols(u)], wbuf.at[u % 2], w_in.at[u % 2])
        copy.start() if start else copy.wait()

    load_ready(0, True)
    for i in range(per):
        for j, source in enumerate((hh, hl)):
            pltpu.make_async_copy(source.at[:, cols(i)], dbuf.at[i % 2, j], d_in.at[i % 2, j]).start()
        for j, turned in enumerate((th, tl)):
            pltpu.make_async_copy(dbuf.at[i % 2, j], dbuf.at[i % 2, j], d_in.at[i % 2, j]).wait()
            turned[i * CHUNK : (i + 1) * CHUNK, :] = dbuf[i % 2, j].T
    acc[...] = jnp.zeros_like(acc)
    pl.semaphore_wait(barrier, len(peers))

    def stage(s, lag, body):
        @pl.when(jnp.logical_and(s >= lag, s < chunks + lag))
        def _():
            body(s - lag)

    def halve(t):
        wait_bytes(core_in.at[t], core_recv.at[t])
        core_in[t] = core_in[t] + gbuf[t % 3, :, c]
        send(core_in.at[t, :, :, 1 - px, 0], a1.at[t], send_sem, a1_recv.at[t], x_peer)
        send(core_in.at[t, :, 1 - py, :, 1], b1.at[t], send_sem, b1_recv.at[t], y_peer)

    def quarter(t):
        wait_bytes(a1.at[t], a1_recv.at[t])
        a1[t] = a1[t] + core_in[t, :, :, px, 0]
        send(a1.at[t, :, 1 - py], a2.at[t], send_sem, a2_recv.at[t], y_peer)
        wait_bytes(b1.at[t], b1_recv.at[t])
        b1[t] = b1[t] + core_in[t, :, py, :, 1]
        send(b1.at[t, :, 1 - px], b2.at[t], send_sem, b2_recv.at[t], x_peer)

    def along_z(t):
        wait_bytes(a2.at[t], a2_recv.at[t])
        zsrc[t, :, 0] = a1[t, :, py] + a2[t]
        wait_bytes(b2.at[t], b2_recv.at[t])
        zsrc[t, :, 1] = b1[t, :, px] + b2[t]
        for k in range(1, 4):
            to = (z + k) % 4
            send(zsrc.at[t, to], z_in.at[t, k - 1], send_sem, z_recv.at[t], (rep, to * 2 + c))

    def spread(t):
        wait_bytes(z_in.at[t], z_recv.at[t])
        total[t, rep] = (zsrc[t, z] + z_in[t, 0]) + (z_in[t, 1] + z_in[t, 2])
        part = total.at[t, rep]
        send(part, part, send_sem, gx_recv.at[t], x_peer)
        send(part, part, send_sem, gy_recv.at[t], y_peer)

    def forward(t):
        wait_bytes(total.at[t, 0], gx_recv.at[t])
        part = total.at[t, x_peer[0], 0]
        send(part, part, send_sem, fy_recv.at[t], y_peer)
        wait_bytes(total.at[t, 0], gy_recv.at[t])
        part = total.at[t, y_peer[0], 1]
        send(part, part, send_sem, fx_recv.at[t], x_peer)

    def finish(t):
        wait_bytes(total.at[t, 0, 0], fx_recv.at[t])
        wait_bytes(total.at[t, 0, 0], fy_recv.at[t])

    def step(s, carry):
        for lag, body in enumerate((halve, quarter, along_z, spread, forward, finish), 1):
            stage(s, lag, body)

        @pl.when(s < chunks)
        def _():
            @pl.when(s < ready)
            def _():
                load_ready(s, False)

            @pl.when(s >= ready)
            def _():
                load_grad(s - ready, False)

            @pl.when(jnp.logical_and(s + 1 >= ready, s + 1 < chunks))
            def _():
                load_grad(s + 1 - ready, True)

            @pl.when(s >= ready)
            def _():
                wait_bytes(gbuf.at[s % 3, :, c], gsend.at[s % 3])
                u = s - ready
                gh, gl = dbuf[u % 2, 0], dbuf[u % 2, 1]
                grad = mm3(th[...], tl[...], gh, gl)
                gbuf[s % 3] = grad.reshape(gbuf.shape[1:])

            send(gbuf.at[s % 3, :, 1 - c], core_in.at[s], gsend.at[s % 3], core_recv.at[s], core_peer)

            @pl.when(s >= ready)
            def _():
                u = s - ready
                wh, wl = split(wbuf[u % 2])

                def some_rows(i, done):
                    at = pl.ds(pl.multiple_of(i * 256, 256), 256)
                    acc[at, :] += mm3(dbuf[u % 2, 0, at, :], dbuf[u % 2, 1, at, :], wh, wl, NT)
                    return done

                lax.fori_loop(0, t_rows // 256, some_rows, 0)

            @pl.when(s + 1 < ready)
            def _():
                @pl.when(s >= 2)
                def _():
                    wait_bytes(gbuf.at[(s + 1) % 3, :, c], gsend.at[(s + 1) % 3])

                load_ready(s + 1, True)

        @pl.when(jnp.logical_and(s >= chunks, s < chunks + 4))
        def _():
            size = t_rows // 4
            at = pl.ds(pl.multiple_of((s - chunks) * size, size), size)
            copies = [
                pltpu.make_async_copy(x.at[at, :], xbuf, ln_in.at[0]),
                pltpu.make_async_copy(dx1.at[at, :], dxbuf, ln_in.at[1]),
            ]
            for copy in copies:
                copy.start()
            for copy in copies:
                copy.wait()
            dh = acc[at, :]
            normed, rstd = norm_parts(xbuf[...])
            obuf[...] = dxbuf[...] + norm_back(dh, normed, rstd, gain[...])
            store = pltpu.make_async_copy(obuf, out.at[at, :], ln_out)
            store.start()
            gs = jnp.concatenate([col_sum(dh * normed), col_sum(dh)], axis=0)
            for j in range(8):
                piece = gs[:, j * 128 : (j + 1) * 128]

                @pl.when(s == chunks)
                def _():
                    spart[j, 0:2] = piece
                    spart[j, 2:9] = gs_rest[:, j * 128 : (j + 1) * 128]

                @pl.when(s > chunks)
                def _():
                    spart[j, 0:2] += piece

            store.wait()

        @pl.when(s == chunks + 4)
        def _():
            for k in range(1, 8):
                to = (rows + k) % 8
                send(spart.at[to], srow.at[k - 1], s_send.at[k - 1], s_recv.at[k - 1], (rep, to))

        @pl.when(s == chunks + 5)
        def _():
            mine = spart[rows]
            for k in range(1, 8):
                wait_bytes(srow.at[k - 1], s_recv.at[k - 1])
                mine = mine + srow[k - 1]
            srep[rep] = mine
            for k in range(1, 4):
                part = srep.at[rep]
                send(part, part, r_send.at[k - 1], r_recv.at[k - 1], ((rep + k) % 4, rows))

        return carry

    lax.fori_loop(0, chunks + STAGES + 1, step, 0)
    for k in range(1, 4):
        wait_bytes(srep.at[0], r_recv.at[k - 1])
    small = (srep[0] + srep[1]) + (srep[2] + srep[3])
    small_total[...] = small

    def squares(t, carry):
        value = total[t].reshape(128, CHUNK)
        return carry + jnp.sum((value * value).reshape(16, 8, CHUNK), axis=0)

    mats = lax.fori_loop(0, chunks, squares, jnp.zeros((8, CHUNK), f32))
    mine = jnp.sum(mats) + jnp.sum(small * small)
    norm_in[rows] = jnp.full((8, 128), mine, f32)
    for k in range(1, 8):
        part = norm_in.at[rows]
        send(part, part, n_send.at[k - 1], n_recv.at[k - 1], (rep, (rows + k) % 8))
    for k in range(1, 8):
        wait_bytes(norm_in.at[0], n_recv.at[k - 1])
    value = norm_in[0]
    for j in range(1, 8):
        value = value + norm_in[j]
    norm[...] = jnp.sqrt(value)

    def sent(t, carry):
        for ref in (a1.at[t], b1.at[t], a2.at[t], b2.at[t], z_in.at[t], total.at[t, 0:3]):
            wait_bytes(ref, send_sem)
        return carry

    lax.fori_loop(0, chunks, sent, 0)
    for i in range(3):
        wait_bytes(gbuf.at[i, :, c], gsend.at[i])
    for k in range(1, 8):
        wait_bytes(srow.at[k - 1], s_send.at[k - 1])
        wait_bytes(norm_in.at[0], n_send.at[k - 1])
    for k in range(1, 4):
        wait_bytes(srep.at[0], r_send.at[k - 1])


def reduce_all(hh, hl, grads, full, x, dx1, mats, gs_rest, gain):
    t = x.shape[0]
    chunks = 6 * D // CHUNK
    hbm = pl.BlockSpec(memory_space=pl.ANY)
    vmem = pl.BlockSpec(memory_space=pltpu.VMEM)
    dma = pltpu.SemaphoreType.DMA
    buf = lambda *shape: pltpu.VMEM(shape + (16, CHUNK), f32)
    return pl.pallas_call(
        reduce_kernel,
        in_specs=[hbm] * 14 + [vmem] * 2,
        out_specs=[hbm, vmem, vmem, vmem],
        out_shape=[
            shape_of((t, D)),
            shape_of((chunks, 4, 2, 16, CHUNK)),
            shape_of((9, 128)),
            shape_of((8, 128)),
        ],
        scratch_shapes=[
            buf(3, 4, 2, 2, 2, 2),
            buf(chunks, 4, 2, 2, 2),
            buf(chunks, 4, 2),
            buf(chunks, 4, 2),
            buf(chunks, 4),
            buf(chunks, 4),
            buf(chunks, 4, 2),
            buf(chunks, 3, 2),
            pltpu.VMEM((D, t), bf16),
            pltpu.VMEM((D, t), bf16),
            pltpu.VMEM((2, 2, t, CHUNK), bf16),
            pltpu.VMEM((2, D, CHUNK), f32),
            pltpu.VMEM((t, D), f32),
            pltpu.VMEM((t // 4, D), f32),
            pltpu.VMEM((t // 4, D), f32),
            pltpu.VMEM((t // 4, D), f32),
            pltpu.VMEM((8, 9, 128), f32),
            pltpu.VMEM((7, 9, 128), f32),
            pltpu.VMEM((4, 9, 128), f32),
            pltpu.VMEM((8, 8, 128), f32),
            dma((3,)),
            dma,
        ]
        + [dma((chunks,))] * 10
        + [dma((3,)), dma((2, 2)), dma((2,)), dma((2,)), dma]
        + [dma((7,)), dma((7,)), dma((3,)), dma((3,)), dma((7,)), dma((7,))],
        compiler_params=pltpu.CompilerParams(
            vmem_limit_bytes=60 * 2**20, collective_id=1, has_side_effects=True
        ),
        cost_estimate=cost(6, 90),
        name="reduce_all",
    )(hh, hl, *grads, full, x, dx1, *(g.reshape(4, 2, 2, 2, 2, 16, D) for g in mats), gs_rest, gain)


def adam_step(parameter, gradient, first_moment, second_moment, average):
    first_new = 0.9 * first_moment + 0.1 * gradient
    second_new = 0.999 * second_moment + 0.001 * gradient * gradient
    first_hat = first_new / (1.0 - 0.9**STEP)
    second_hat = second_new / (1.0 - 0.999**STEP)
    parameter_new = parameter - 0.05 * (
        first_hat / (jnp.sqrt(second_hat) + 1e-08) + 0.05 * parameter
    )
    average_new = 0.99 * average + 0.01 * parameter_new
    return (parameter_new, first_new, second_new, average_new)


CLIP = 0.25 * math.sqrt(6 * D * D + 9 * D)


def adam_kernel(
    grad, norm, w, first, second, average, gs, p_s, first_s, second_s, average_s,
    clipped, new_w, first_o, second_o, average_o, low,
    clipped_so, new_so, first_so, second_so, average_so, low_so,
):
    factor = jnp.minimum(1.0, CLIP / norm[0:1, 0:1])
    for j in range(D // CHUNK):
        at = slice(j * CHUNK, (j + 1) * CHUNK)
        value = grad[j].reshape(w.shape[0], CHUNK) * factor
        clipped[:, at] = value
        news = adam_step(w[:, at], value, first[:, at], second[:, at], average[:, at])
        for ref, new in zip((new_w, first_o, second_o, average_o), news):
            ref[:, at] = new
        low[:, at] = news[0].astype(bf16)

    @pl.when(pl.program_id(0) == 0)
    def _():
        value = gs[...] * factor
        clipped_so[...] = value
        news = adam_step(p_s[...], value, first_s[...], second_s[...], average_s[...])
        for ref, new in zip((new_so, first_so, second_so, average_so), news):
            ref[...] = new
        low_so[...] = news[0].astype(bf16)


def adam(total, norm, mats, gs, smalls):
    shard, width = mats[0].shape
    block = pl.BlockSpec((shard, D), lambda i: (0, jnp.where(i < 3, 5 - i, i - 3)))
    grads = pl.BlockSpec((D // CHUNK,) + total.shape[1:], lambda i: (i, 0, 0, 0, 0))
    small = whole(gs.shape)
    return pl.pallas_call(
        adam_kernel,
        grid=(width // D,),
        in_specs=[grads, whole(norm.shape)] + [block] * 4 + [small] * 5,
        out_specs=[block] * 6 + [small] * 6,
        out_shape=[shape_of((shard, width))] * 5
        + [shape_of((shard, width), bf16)]
        + [shape_of(gs.shape)] * 5
        + [shape_of(gs.shape, bf16)],
        compiler_params=params(),
        cost_estimate=cost(0, 32),
        name="adam",
    )(total, norm, *mats, gs, *smalls)


def split_once(w, wh, wl):
    @pl.when(pl.program_id(0) == 0)
    def _():
        wh[...], wl[...] = split(w[...])


def out_proj_kernel(oh, ol, w, x, s, x1, h2h, h2l, wh, wl):
    split_once(w, wh, wl)
    value = x[...] + mm3(oh[...], ol[...], wh[...], wl[...]) + s[4:5]
    x1[...] = value
    normed, _ = norm_parts(value)
    h2h[...], h2l[...] = split(normed * s[5:6] + s[6:7])


def out_proj(oh, ol, w, x, small, bm=256):
    t = x.shape[0]
    return pl.pallas_call(
        out_proj_kernel,
        grid=(t // bm,),
        in_specs=[rows_of(bm, D)] * 2 + [matrix(3), rows_of(bm, D), whole((9, D))],
        out_specs=[rows_of(bm, D)] * 3,
        out_shape=[shape_of((t, D)), shape_of((t, D), bf16), shape_of((t, D), bf16)],
        scratch_shapes=[pltpu.VMEM((D, D), bf16)] * 2,
        compiler_params=params(),
        cost_estimate=cost(1, 20),
        name="out_proj",
    )(oh, ol, w, x, small)


ROOT = math.sqrt(2.0 / math.pi)


def up_kernel(hh, hl, w, s, z, uh, ul):
    wh, wl = split(w[...])
    value = mm3(hh[...], hl[...], wh, wl) + s[7:8]
    z[...] = value
    bent = jnp.tanh(ROOT * (value + 0.044715 * value * value * value))
    uh[...], ul[...] = split(0.5 * value * (1.0 + bent))


def up(hh, hl, w, small, bn=256):
    t = hh.shape[0]
    return pl.pallas_call(
        up_kernel,
        grid=(FF // bn,),
        in_specs=[whole((t, D))] * 2 + [cols_of(D, bn, 4 * D // bn), cols_of(9, bn)],
        out_specs=[cols_of(t, bn)] * 3,
        out_shape=[shape_of((t, FF)), shape_of((t, FF), bf16), shape_of((t, FF), bf16)],
        compiler_params=params(),
        cost_estimate=cost(1, 16),
        name="up",
    )(hh, hl, w, small)


def down_kernel(uh, ul, w, x1, s, out):
    wh, wl = split(w[...])
    out[...] = x1[...] + mm3(uh[...], ul[...], wh, wl) + s[8:9]


def down(uh, ul, w, x1, small, bn=256):
    t = uh.shape[0]
    return pl.pallas_call(
        down_kernel,
        grid=(D // bn,),
        in_specs=[whole((t, FF))] * 2
        + [cols_of(FF, bn, 5 * D // bn), cols_of(t, bn), cols_of(9, bn)],
        out_specs=cols_of(t, bn),
        out_shape=shape_of((t, D)),
        compiler_params=params(),
        cost_estimate=cost(1, 16),
        name="down",
    )(uh, ul, w, x1, small)


def outer_kernel(ah, al, dh, dl, out, th, tl):
    @pl.when(pl.program_id(0) == 0)
    def _():
        th[...] = ah[...].T
        tl[...] = al[...].T

    out[...] = mm3(th[...], tl[...], dh[...], dl[...])


def outer(ah, al, dh, dl, bn=256):
    t, m = ah.shape
    n = dh.shape[1]
    return pl.pallas_call(
        outer_kernel,
        grid=(n // bn,),
        in_specs=[whole((t, m))] * 2 + [cols_of(t, bn)] * 2,
        out_specs=cols_of(m, bn),
        out_shape=shape_of((m, n)),
        scratch_shapes=[pltpu.VMEM((m, t), bf16)] * 2,
        compiler_params=params(),
        cost_estimate=cost(1, 12),
        name="outer",
    )(ah, al, dh, dl)


def down_back_kernel(ch, cl, w, z, dzh, dzl, gs7):
    wh, wl = split(w[...])
    du = mm3(ch[...], cl[...], wh, wl, NT)
    value = z[...]
    square = value * value
    bent = jnp.tanh(ROOT * (value + 0.044715 * value * square))
    slope = 0.5 * (1.0 + bent) + 0.5 * value * (1.0 - bent * bent) * (
        ROOT * (1.0 + 3.0 * 0.044715 * square)
    )
    dz = du * slope
    dzh[...], dzl[...] = split(dz)
    gs7[...] = col_sum(dz)


def down_back(ch, cl, w, z, bn=256):
    t = ch.shape[0]
    return pl.pallas_call(
        down_back_kernel,
        grid=(FF // bn,),
        in_specs=[whole((t, D))] * 2 + [rows_of(bn, D, 5), cols_of(t, bn)],
        out_specs=[cols_of(t, bn)] * 2 + [cols_of(1, bn)],
        out_shape=[shape_of((t, FF), bf16)] * 2 + [shape_of((1, FF))],
        compiler_params=params(),
        cost_estimate=cost(1, 16),
        name="down_back",
    )(ch, cl, w, z)


def up_back_kernel(dzh, dzl, w, x1, cot, s, dx1, dxh, dxl, gs4, gs5, gs6, wh, wl):
    split_once(w, wh, wl)
    dh2 = mm3(dzh[...], dzl[...], wh[...], wl[...], NT)
    normed, rstd = norm_parts(x1[...])
    grad = cot[...] + norm_back(dh2, normed, rstd, s[5:6])
    dx1[...] = grad
    dxh[...], dxl[...] = split(grad)
    add_up(gs4, col_sum(grad))
    add_up(gs5, col_sum(dh2 * normed))
    add_up(gs6, col_sum(dh2))


def up_back(dzh, dzl, w, x1, cot, small, bm=256):
    t = x1.shape[0]
    return pl.pallas_call(
        up_back_kernel,
        grid=(t // bm,),
        in_specs=[rows_of(bm, FF)] * 2 + [matrix(4)] + [rows_of(bm, D)] * 2 + [whole((9, D))],
        out_specs=[rows_of(bm, D)] * 3 + [whole((1, D))] * 3,
        out_shape=[shape_of((t, D)), shape_of((t, D), bf16), shape_of((t, D), bf16)]
        + [shape_of((1, D))] * 3,
        scratch_shapes=[pltpu.VMEM((D, FF), bf16)] * 2,
        compiler_params=params(),
        cost_estimate=cost(1, 24),
        name="up_back",
    )(dzh, dzl, w, x1, cot, small)


def out_proj_back_kernel(dxh, dxl, w, do):
    wh, wl = split(w[...])
    do[...] = pair_heads(*split(mm3(dxh[...], dxl[...], wh, wl, NT)))


def out_proj_back(dxh, dxl, w, bn=256):
    t = dxh.shape[0]
    return pl.pallas_call(
        out_proj_back_kernel,
        grid=(D // bn,),
        in_specs=[whole((t, D))] * 2 + [rows_of(bn, D, 3)],
        out_specs=cols_of(t, 2 * bn),
        out_shape=shape_of((t, 2 * D), bf16),
        compiler_params=params(),
        cost_estimate=cost(1, 12),
        name="out_proj_back",
    )(dxh, dxl, w)


def proj_back_kernel(
    dqh, dql, dkh, dkl, dvh, dvl, wq, wk, wv, x, dx1, s, out, gs0, gs1, wh, wl
):
    @pl.when(pl.program_id(0) == 0)
    def _():
        for j, w in enumerate((wq, wk, wv)):
            wh[j], wl[j] = split(w[...])

    dh = mm3(dqh[...], dql[...], wh[0], wl[0], NT)
    dh += mm3(dkh[...], dkl[...], wh[1], wl[1], NT)
    dh += mm3(dvh[...], dvl[...], wh[2], wl[2], NT)
    normed, rstd = norm_parts(x[...])
    out[...] = dx1[...] + norm_back(dh, normed, rstd, s[0:1])
    add_up(gs0, col_sum(dh * normed))
    add_up(gs1, col_sum(dh))


def proj_back(grads, w, x, dx1, small, bm=256):
    t = x.shape[0]
    return pl.pallas_call(
        proj_back_kernel,
        grid=(t // bm,),
        in_specs=[rows_of(bm, D)] * 6 + [matrix(j) for j in range(3)] + [rows_of(bm, D)] * 2 + [whole((9, D))],
        out_specs=[rows_of(bm, D)] + [whole((1, D))] * 2,
        out_shape=[shape_of((t, D))] + [shape_of((1, D))] * 2,
        scratch_shapes=[pltpu.VMEM((3, D, D), bf16)] * 2,
        compiler_params=params(),
        cost_estimate=cost(3, 36),
        name="proj_back",
    )(*grads, w, w, w, x, dx1, small)


def set_bounds(segment_ids):
    ids = segment_ids[0, ::UNIT]
    order, sets = (ids - ids[0])[None, :], jnp.arange(SETS, dtype=jnp.int32)[:, None]
    lengths = jnp.sum((order == sets).astype(jnp.int32), axis=1)
    firsts = jnp.sum((order < sets).astype(jnp.int32), axis=1)
    return jnp.stack([firsts, lengths], axis=1).reshape(-1).astype(jnp.int32)


def shards(
    reps,
    latents,
    cotangent,
    segment_ids,
    weights,
    small_params,
    first_mats,
    second_mats,
    average_mats,
    first_small,
    second_small,
    average_small,
):
    segs = set_bounds(segment_ids)
    x, cot = latents[0], cotangent[0]
    fast = reps == 4 and weights.shape[0] * 8 == D
    if fast:
        full, small, hh, hl, ch, cl, gs8, qkv = gather(weights, small_params, x, cot)
    else:
        full, small = (
            lax.all_gather(weights, "rows", axis=0, tiled=True),
            lax.all_gather(small_params, "rows", axis=1, tiled=True),
        )
        bias = jnp.concatenate([small[2], jnp.zeros((D,), f32), small[3]])[None]
        hh, hl, ch, cl, gs8 = prep(x, cot, small)
        qkv = proj(hh, hl, full, bias)
    oh, ol, lse = attend(segs, qkv)
    x1, h2h, h2l = out_proj(oh, ol, full, x, small)
    z, uh, ul = up(h2h, h2l, full, small)
    output = down(uh, ul, full, x1, small)
    g_down = outer(uh, ul, ch, cl)
    dzh, dzl, gs7 = down_back(ch, cl, full, z)
    g_up = outer(h2h, h2l, dzh, dzl)
    dx1, dxh, dxl, gs4, gs5, gs6 = up_back(dzh, dzl, full, x1, cot, small)
    g_out = outer(oh, ol, dxh, dxl)
    do = out_proj_back(dxh, dxl, full)
    *grads, gs2, gs3 = attend_back(segs, qkv, do, oh, ol, lse)
    if fast:
        gs_rest = jnp.concatenate([gs2, gs3, gs4, gs5, gs6, gs7, gs8], axis=0)
        token_grad, total, small_total, norm = reduce_all(
            hh, hl, grads, full, x, dx1, (g_down, g_up, g_out), gs_rest, small[0:1]
        )
        (
            clipped_mats, new_weights, first_mats_out, second_mats_out, average_mats_out, low_mats,
            clipped_small, new_small, first_small_out, second_small_out, average_small_out, low_small,
        ) = adam(
            total, norm, (weights, first_mats, second_mats, average_mats), small_total,
            (small_params, first_small, second_small, average_small),
        )
        norm = norm[0, 0:1]
    else:
        g_qkv = [outer(hh, hl, grads[2 * j], grads[2 * j + 1]) for j in range(3)]
        token_grad, gs0, gs1 = proj_back(grads, full, x, dx1, small)
        weight_grad = jnp.concatenate(g_qkv + [g_out, g_up, g_down], axis=1)
        small_grad = jnp.concatenate([gs0, gs1, gs2, gs3, gs4, gs5, gs6, gs7, gs8], axis=0)
        part_weights, part_small = (
            lax.psum_scatter(weight_grad, "rows", scatter_dimension=0, tiled=True),
            lax.psum_scatter(small_grad, "rows", scatter_dimension=1, tiled=True),
        )
        sum_weights, sum_small = lax.psum((part_weights, part_small), "rep")
        squares = lax.psum(
            jnp.sum(sum_weights * sum_weights) + jnp.sum(sum_small * sum_small), "rows"
        )
        norm = jnp.sqrt(squares).reshape(1)
        factor = jnp.minimum(1.0, CLIP / norm[0])
        clipped_mats = sum_weights * factor
        clipped_small = sum_small * factor
        new_weights, first_mats_out, second_mats_out, average_mats_out = adam_step(
            weights, clipped_mats, first_mats, second_mats, average_mats
        )
        new_small, first_small_out, second_small_out, average_small_out = adam_step(
            small_params, clipped_small, first_small, second_small, average_small
        )
        low_mats, low_small = new_weights.astype(bf16), new_small.astype(bf16)
    return (
        output[None],
        token_grad[None],
        norm,
        clipped_mats,
        clipped_small,
        new_weights,
        new_small,
        first_mats_out,
        second_mats_out,
        average_mats_out,
        first_small_out,
        second_small_out,
        average_small_out,
        low_mats,
        low_small,
    )


def solution(mesh):
    tokens, mats, small = P("rep", "rows", None), P("rows", None), P(None, "rows")
    in_specs = (tokens, tokens, P("rep", "rows")) + (mats, small) + (mats,) * 3 + (small,) * 3
    out_specs = (
        (tokens, tokens, P(), mats, small, mats, small) + (mats,) * 3 + (small,) * 3 + (mats, small)
    )
    step = functools.partial(shards, mesh.shape["rep"])
    return jax.shard_map(step, mesh=mesh, in_specs=in_specs, out_specs=out_specs, check_vma=False)
```

```python
import functools
import math

import jax
import jax.numpy as jnp
from jax import lax
from jax.experimental import pallas as pl
from jax.experimental.pallas import tpu as pltpu
from jax.sharding import PartitionSpec as P

D = 1024
HEADS = 8
HEAD_DIM = 128
FF = 1024
UNIT = 128
SETS = 3
STEP = 5
SCALE = HEAD_DIM ** (-0.5)
ROOT = math.sqrt(2.0 / math.pi)

f32 = jnp.float32
bf16 = jnp.bfloat16

NN = (((1,), (0,)), ((), ()))
NT = (((1,), (1,)), ((), ()))
TN = (((0,), (0,)), ((), ()))


def params(mib=56):
    return pltpu.CompilerParams(
        vmem_limit_bytes=mib * 2**20, dimension_semantics=("arbitrary",)
    )


def mm(a, b, dims=NN):
    return lax.dot_general(a, b, dims, preferred_element_type=f32)


def split(x):
    high = x.astype(bf16)
    return high, (x - high.astype(f32)).astype(bf16)


def mm3(ah, al, bh, bl, dims=NN):
    return mm(ah, bh, dims) + (mm(al, bh, dims) + mm(ah, bl, dims))


def cost(products, mib):
    return pl.CostEstimate(
        flops=int(products * 3 * 2 * 1024**3), bytes_accessed=int(mib * 2**20), transcendentals=0
    )


def whole(shape):
    return pl.BlockSpec(shape, lambda *i: (0,) * len(shape))


def rows_of(bm, n, column=0):
    return pl.BlockSpec((bm, n), lambda i, *_: (i, column))


def matrix(j):
    return pl.BlockSpec((D, D), lambda i: (0, j), pipeline_mode=pl.Buffered(1))


def cols_of(m, bn, first=0):
    return pl.BlockSpec((m, bn), lambda i, *_: (0, first + i))


def shape_of(shape, dtype=f32):
    return jax.ShapeDtypeStruct(shape, dtype)


def norm_parts(x):
    center = x - jnp.mean(x, axis=-1, keepdims=True)
    rstd = lax.rsqrt(jnp.mean(center * center, axis=-1, keepdims=True) + 1e-05)
    return center * rstd, rstd


def norm_back(grad, normed, rstd, gain):
    scaled = grad * gain
    return rstd * (
        scaled
        - jnp.mean(scaled, axis=-1, keepdims=True)
        - normed * jnp.mean(scaled * normed, axis=-1, keepdims=True)
    )


def col_sum(x):
    return jnp.sum(x, axis=0, keepdims=True)


def add_up(ref, value):
    first = pl.program_id(0) == 0

    @pl.when(first)
    def _():
        ref[...] = value

    @pl.when(jnp.logical_not(first))
    def _():
        ref[...] += value


def prep_kernel(x, cot, s, hh, hl, ch, cl, gs8):
    normed, _ = norm_parts(x[...])
    hh[...], hl[...] = split(normed * s[0:1] + s[1:2])
    ch[...], cl[...] = split(cot[...])
    add_up(gs8, col_sum(cot[...]))


def prep(x, cot, small, bm=256):
    t = x.shape[0]
    return pl.pallas_call(
        prep_kernel,
        grid=(t // bm,),
        in_specs=[rows_of(bm, D), rows_of(bm, D), whole((9, D))],
        out_specs=[rows_of(bm, D)] * 4 + [whole((1, D))],
        out_shape=[shape_of((t, D), bf16)] * 4 + [shape_of((1, D))],
        compiler_params=params(),
        cost_estimate=cost(0, 16),
        name="prep",
    )(x, cot, small)


def pair_heads(high, low):
    parts = []
    for head in range(high.shape[1] // HEAD_DIM):
        cut = slice(head * HEAD_DIM, (head + 1) * HEAD_DIM)
        parts += [high[:, cut], low[:, cut]]
    return jnp.concatenate(parts, axis=1)


def proj_kernel(hh, hl, w, bias, out):
    wh, wl = split(w[...])
    out[...] = pair_heads(*split(mm3(hh[...], hl[...], wh, wl) + bias[...]))


def proj(hh, hl, w, bias, bn=256):
    t, n = hh.shape[0], bias.shape[1]
    return pl.pallas_call(
        proj_kernel,
        grid=(n // bn,),
        in_specs=[whole((t, D))] * 2 + [cols_of(D, bn), cols_of(1, bn)],
        out_specs=cols_of(t, 2 * bn),
        out_shape=shape_of((t, 2 * n), bf16),
        compiler_params=params(),
        cost_estimate=cost(n // D, 8 * (n // D) + 4),
        name="proj",
    )(hh, hl, w, bias)


def twice(a):
    return jnp.concatenate([a, a], axis=1)


def halves_sum(x):
    return x[:, :HEAD_DIM] + x[:, HEAD_DIM:]


def pieces(n):
    out, at = [], 0
    while at < n:
        size = min(256, n - at)
        out.append((at, size))
        at += size
    return out


def for_sets(segs, units, body):
    def one(i, carry):
        first, length = segs[2 * i], segs[2 * i + 1]
        for count in range(1, units - SETS + 2):

            @pl.when(length == count)
            def _():
                body(pl.multiple_of(first * UNIT, UNIT), count * UNIT)

        return carry

    lax.fori_loop(0, SETS, one, 0)


def attend_kernel(segs, q, k, v, oh, ol, lse):
    units = q.shape[0] // UNIT

    def body(first, n):
        rows = pl.ds(first, n)
        keys = k[rows, :]
        kh, kl = twice(keys[:, :HEAD_DIM]), twice(keys[:, HEAD_DIM:])
        vals = v[rows, :]
        for at, size in pieces(n):
            sub = pl.ds(pl.multiple_of(first + at, UNIT), size)
            qs = q[sub, :]
            scores = mm(qs, kh, NT) + mm(qs, kl, NT)
            top = jnp.max(scores, axis=-1, keepdims=True)
            p = jnp.exp((scores - top) * SCALE)
            total = jnp.sum(p, axis=-1, keepdims=True)
            ph, plow = split(p)
            o = halves_sum(mm(ph, vals) + mm(plow, vals)) / total
            oh[sub, :], ol[sub, :] = split(o)
            level = top * SCALE + jnp.log(total)
            for u in range(size // UNIT):
                tile = jnp.broadcast_to(level[u * UNIT : (u + 1) * UNIT], (UNIT, UNIT))
                lse[0, :, pl.ds(pl.multiple_of(first + at + u * UNIT, UNIT), UNIT)] = tile.T[0:8]

    for_sets(segs, units, body)


def attend(segs, qkv):
    t = qkv.shape[0]
    head = lambda first: pl.BlockSpec((t, 2 * HEAD_DIM), lambda i, *_: (0, first + i))
    return pl.pallas_call(
        attend_kernel,
        grid_spec=pltpu.PrefetchScalarGridSpec(
            num_scalar_prefetch=1,
            grid=(HEADS,),
            in_specs=[head(0), head(HEADS), head(2 * HEADS)],
            out_specs=[cols_of(t, HEAD_DIM)] * 2
            + [pl.BlockSpec((1, 8, t), lambda i, *_: (i, 0, 0))],
        ),
        out_shape=[shape_of((t, D), bf16)] * 2 + [shape_of((HEADS, 8, t))],
        compiler_params=params(),
        cost_estimate=cost(2, 16),
        name="attend",
    )(segs, qkv, qkv, qkv)


def attend_back_kernel(
    segs, q, k, v, do, oh, ol, lse, dqh, dql, dkh, dkl, dvh, dvl, gq, gv, drow, qsum, vsum
):
    units = q.shape[0] // UNIT
    for u in range(units):
        cut = slice(u * UNIT, (u + 1) * UNIT)
        grad = do[cut, :].astype(f32)
        out = oh[cut, :].astype(f32) + ol[cut, :].astype(f32)
        tile = (halves_sum(grad) * out).T
        drow[:, cut] = jnp.broadcast_to(col_sum(tile), (8, UNIT))
    qsum[...] = jnp.zeros_like(qsum)
    vsum[...] = jnp.zeros_like(vsum)

    def body(first, n):
        rows = pl.ds(first, n)
        keys, vals = k[rows, :], v[rows, :]
        dk = dv = None
        for at, size in pieces(n):
            sub = pl.ds(pl.multiple_of(first + at, UNIT), size)
            qs, grad = q[sub, :], do[sub, :]
            scores = mm(keys, twice(qs[:, :HEAD_DIM]), NT) + mm(keys, twice(qs[:, HEAD_DIM:]), NT)
            p = jnp.exp(scores * SCALE - lse[0, 0:1, sub])
            dp = mm(vals, twice(grad[:, :HEAD_DIM]), NT) + mm(vals, twice(grad[:, HEAD_DIM:]), NT)
            ds = p * (dp - drow[0:1, sub])
            ph, plow = split(p)
            dsh, dsl = split(ds)
            dv_part = mm(ph, grad) + mm(plow, grad)
            dk_part = mm(dsh, qs) + mm(dsl, qs)
            dv = dv_part if dv is None else dv + dv_part
            dk = dk_part if dk is None else dk + dk_part
            dq = halves_sum(mm(dsh, keys, TN) + mm(dsl, keys, TN)) * SCALE
            dqh[sub, :], dql[sub, :] = split(dq)
            qsum[0:1, :] += col_sum(dq)
        dk = halves_sum(dk) * SCALE
        dv = halves_sum(dv)
        dkh[rows, :], dkl[rows, :] = split(dk)
        dvh[rows, :], dvl[rows, :] = split(dv)
        vsum[0:1, :] += col_sum(dv)

    for_sets(segs, units, body)
    gq[...] = qsum[0:1, :]
    gv[...] = vsum[0:1, :]


def attend_back(segs, qkv, do, oh, ol, lse):
    t = qkv.shape[0]
    head = lambda first: pl.BlockSpec((t, 2 * HEAD_DIM), lambda i, *_: (0, first + i))
    return pl.pallas_call(
        attend_back_kernel,
        grid_spec=pltpu.PrefetchScalarGridSpec(
            num_scalar_prefetch=1,
            grid=(HEADS,),
            in_specs=[head(0), head(HEADS), head(2 * HEADS), head(0)]
            + [cols_of(t, HEAD_DIM)] * 2
            + [pl.BlockSpec((1, 8, t), lambda i, *_: (i, 0, 0))],
            out_specs=[cols_of(t, HEAD_DIM)] * 6 + [cols_of(1, HEAD_DIM)] * 2,
            scratch_shapes=[
                pltpu.VMEM((8, t), f32),
                pltpu.VMEM((8, HEAD_DIM), f32),
                pltpu.VMEM((8, HEAD_DIM), f32),
            ],
        ),
        out_shape=[shape_of((t, D), bf16)] * 6 + [shape_of((1, D))] * 2,
        compiler_params=params(),
        cost_estimate=cost(5, 36),
        name="attend_back",
    )(segs, qkv, qkv, qkv, do, oh, ol, lse)


MESH = pl.DeviceIdType.MESH
CHUNK = 256
AHEAD, SPREAD, SWAP, USE = 4, 2, 4, 6


def wait_bytes(ref, sem):
    pltpu.make_async_copy(ref, ref, sem).wait()


def gather_kernel(
    w, own_small, x, cot,
    full, small, hh, hl, ch, cl, gs8, qkv,
    pieces, own, xbuf, cbuf, hhb, hlb, chb, clb, wbuf, obuf,
    small_send, small_recv, own_sem, send_sem, core_send, own_recv,
    z_recv, x_recv, y_recv, fx_recv, fy_recv, core_recv, in_sem, out_sem, w_sem, q_sem,
):
    rep, rows = lax.axis_index("rep"), lax.axis_index("rows")
    z, c = rows // 2, rows % 2
    x_next, y_next = rep // 2 * 2 + (1 - rep % 2), (1 - rep // 2) * 2 + rep % 2
    shard = w.shape[0]
    quarter, half = shard // 4, shard // 8
    chunks = w.shape[1] // CHUNK
    proj_chunks = 3 * D // CHUNK

    x_in = pltpu.make_async_copy(x, xbuf, in_sem.at[0])
    c_in = pltpu.make_async_copy(cot, cbuf, in_sem.at[1])
    x_in.start()
    c_in.start()
    own_in = pltpu.make_async_copy(w, own, own_sem)
    own_in.start()

    barrier = pltpu.get_barrier_semaphore()
    peers = [(rep, (rows + k) % 8) for k in range(1, 8)] + [(x_next, rows), (y_next, rows)]
    for peer in peers:
        pl.semaphore_signal(barrier, inc=1, device_id=peer, device_id_type=MESH)
    pl.semaphore_wait(barrier, len(peers))

    def send(src, dst, sem, recv, device):
        pltpu.make_async_remote_copy(
            src_ref=src, dst_ref=dst, send_sem=sem, recv_sem=recv, device_id=device,
            device_id_type=MESH,
        ).start()

    for k in range(1, 8):
        send(own_small, pieces.at[k - 1], small_send.at[k - 1], small_recv.at[k - 1], (rep, (rows + k) % 8))

    def cols(t):
        return pl.ds(pl.multiple_of(t * CHUNK, CHUNK), CHUNK)

    def place(zz, first, count, t):
        at = (zz * 2 + c) * shard + first
        return full.at[pl.ds(pl.multiple_of(at, half), count), cols(t)]

    def start_z(t):
        src = w.at[pl.ds(pl.multiple_of(rep * quarter, quarter), quarter), cols(t)]
        for k in range(1, 4):
            send(src, place(z, rep * quarter, quarter, t), send_sem, z_recv.at[t], (rep, (z + k) % 4 * 2 + c))

    for t in range(AHEAD):
        start_z(t)
    send(w, full.at[pl.ds(rows * shard, shard), :], core_send, own_recv, (rep, z * 2 + 1 - c))

    for k in range(1, 8):
        pltpu.make_async_copy(own_small, pieces.at[k - 1], small_recv.at[k - 1]).wait()
        pltpu.make_async_copy(own_small, pieces.at[k - 1], small_send.at[k - 1]).wait()
    width = own_small.shape[1]
    small[:, pl.ds(pl.multiple_of(rows * width, width), width)] = own_small[...]
    for k in range(1, 8):
        at = pl.multiple_of((rows + 8 - k) % 8 * width, width)
        small[:, pl.ds(at, width)] = pieces[k - 1]

    own_in.wait()
    own_out = pltpu.make_async_copy(own, full.at[pl.ds(rows * shard, shard), :], own_sem)
    own_out.start()
    x_in.wait()

    def norm_rows(i, carry):
        at = pl.ds(pl.multiple_of(i * 128, 128), 128)
        normed, _ = norm_parts(xbuf[at, :])
        hhb[at, :], hlb[at, :] = split(normed * small[0:1, :] + small[1:2, :])
        return carry

    lax.fori_loop(0, x.shape[0] // 128, norm_rows, 0)
    h_out = [
        pltpu.make_async_copy(hhb, hh, out_sem.at[0]),
        pltpu.make_async_copy(hlb, hl, out_sem.at[1]),
    ]
    for copy in h_out:
        copy.start()
    own_out.wait()
    wait_bytes(w, own_recv)

    def q_out(t):
        at = pl.ds(pl.multiple_of(t * 2 * CHUNK, 2 * CHUNK), 2 * CHUNK)
        return pltpu.make_async_copy(obuf.at[t % 2], qkv.at[:, at], q_sem.at[t % 2])

    def step(s, carry):
        @pl.when(s < chunks)
        def _():
            wait_bytes(w.at[0 : 3 * quarter, 0:CHUNK], z_recv.at[s])
            for k in range(1, 4):
                part = place((z + k) % 4, rep * quarter, quarter, s)
                send(part, part, send_sem, x_recv.at[s], (x_next, rows))
                send(part, part, send_sem, y_recv.at[s], (y_next, rows))

        @pl.when(s + AHEAD < chunks)
        def _():
            start_z(s + AHEAD)

        @pl.when(jnp.logical_and(s >= SPREAD, s < chunks + SPREAD))
        def _():
            t = s - SPREAD
            wait_bytes(w.at[0 : 3 * quarter, 0:CHUNK], x_recv.at[t])
            wait_bytes(w.at[0 : 3 * quarter, 0:CHUNK], y_recv.at[t])
            for k in range(1, 4):
                part = place((z + k) % 4, x_next * quarter, half, t)
                send(part, part, send_sem, fy_recv.at[t], (y_next, rows))
                part = place((z + k) % 4, y_next * quarter + half, half, t)
                send(part, part, send_sem, fx_recv.at[t], (x_next, rows))

        @pl.when(jnp.logical_and(s >= SWAP, s < chunks + SWAP))
        def _():
            t = s - SWAP
            wait_bytes(w.at[0 : 3 * half, 0:CHUNK], fx_recv.at[t])
            wait_bytes(w.at[0 : 3 * half, 0:CHUNK], fy_recv.at[t])
            for k in range(1, 4):
                part = place((z + k) % 4, 0, shard, t)
                send(part, part, core_send, core_recv.at[t], (rep, z * 2 + 1 - c))

        @pl.when(s >= USE)
        def _():
            wait_bytes(full.at[0 : 3 * shard, 0:CHUNK], core_recv.at[s - USE])

        @pl.when(jnp.logical_and(s >= USE, s < proj_chunks + USE))
        def _():
            t = s - USE
            load = pltpu.make_async_copy(full.at[:, cols(t)], wbuf, w_sem)
            load.start()

            @pl.when(t >= 2)
            def _():
                q_out(t).wait()

            load.wait()
            wh, wl = split(wbuf[...])
            kind = t // (D // CHUNK)
            at = pl.ds(pl.multiple_of(t % (D // CHUNK) * CHUNK, CHUNK), CHUNK)
            bias = jnp.where(kind == 0, small[2:3, at], jnp.where(kind == 2, small[3:4, at], 0.0))
            obuf[t % 2] = pair_heads(*split(mm3(hhb[...], hlb[...], wh, wl) + bias))
            q_out(t).start()

        @pl.when(s == proj_chunks + USE)
        def _():
            c_in.wait()

            def split_rows(i, total):
                at = pl.ds(pl.multiple_of(i * 128, 128), 128)
                value = cbuf[at, :]
                chb[at, :], clb[at, :] = split(value)
                return total + col_sum(value)

            gs8[...] = lax.fori_loop(0, cot.shape[0] // 128, split_rows, jnp.zeros((1, D), f32))
            pltpu.make_async_copy(chb, ch, out_sem.at[2]).start()
            pltpu.make_async_copy(clb, cl, out_sem.at[3]).start()

        return carry

    lax.fori_loop(0, chunks + USE, step, 0)
    q_out(proj_chunks - 2).wait()
    q_out(proj_chunks - 1).wait()
    for copy in h_out:
        copy.wait()
    pltpu.make_async_copy(chb, ch, out_sem.at[2]).wait()
    pltpu.make_async_copy(clb, cl, out_sem.at[3]).wait()
    wait_bytes(full.at[0 : 3 * quarter + 6 * quarter + 6 * half, :], send_sem)
    wait_bytes(full.at[0 : 4 * shard, :], core_send)


def gather(weights, small_params, x, cot):
    shard, width = weights.shape
    t = x.shape[0]
    chunks = width // CHUNK
    hbm = pl.BlockSpec(memory_space=pl.ANY)
    vmem = pl.BlockSpec(memory_space=pltpu.VMEM)
    dma = pltpu.SemaphoreType.DMA
    return pl.pallas_call(
        gather_kernel,
        in_specs=[hbm, vmem, hbm, hbm],
        out_specs=[hbm, vmem, hbm, hbm, hbm, hbm, vmem, hbm],
        out_shape=[shape_of((8 * shard, width)), shape_of((9, D))]
        + [shape_of((t, D), bf16)] * 4
        + [shape_of((1, D)), shape_of((t, 6 * D), bf16)],
        scratch_shapes=[pltpu.VMEM((7,) + small_params.shape, f32), pltpu.VMEM((shard, width), f32)]
        + [pltpu.VMEM((t, D), f32)] * 2
        + [pltpu.VMEM((t, D), bf16)] * 4
        + [pltpu.VMEM((D, CHUNK), f32), pltpu.VMEM((2, t, 2 * CHUNK), bf16)]
        + [dma((7,)), dma((7,)), dma, dma, dma, dma]
        + [dma((chunks,))] * 6
        + [dma((2,)), dma((4,)), dma, dma((2,))],
        compiler_params=pltpu.CompilerParams(
            vmem_limit_bytes=50 * 2**20, collective_id=0, has_side_effects=True
        ),
        cost_estimate=cost(3, 64),
        name="gather",
    )(weights, small_params, x, cot)


def remote(src, dst, sem, recv, device):
    pltpu.make_async_remote_copy(
        src_ref=src, dst_ref=dst, send_sem=sem, recv_sem=recv, device_id=device, device_id_type=MESH
    ).start()


def greet(peers):
    barrier = pltpu.get_barrier_semaphore()
    for peer in peers:
        pl.semaphore_signal(barrier, inc=1, device_id=peer, device_id_type=MESH)
    return lambda: pl.semaphore_wait(barrier, len(peers))


def col_chunk(t):
    return pl.ds(pl.multiple_of(t * CHUNK, CHUNK), CHUNK)


class Summing:
    def __init__(self, bufs, sems):
        self.bufs, self.sems = bufs, sems
        rep, rows = lax.axis_index("rep"), lax.axis_index("rows")
        self.rep, self.px, self.py, self.z, self.c = rep, rep % 2, rep // 2, rows // 2, rows % 2
        self.x_peer = (self.py * 2 + 1 - self.px, rows)
        self.y_peer = ((1 - self.py) * 2 + self.px, rows)

    @staticmethod
    def scratch(chunks):
        buf = lambda *shape: pltpu.VMEM(shape + (16, CHUNK), f32)
        dma = pltpu.SemaphoreType.DMA
        return [
            buf(3, 4, 2, 2, 2, 2),
            buf(chunks, 4, 2, 2, 2),
            buf(chunks, 4, 2),
            buf(chunks, 4, 2),
            buf(chunks, 4),
            buf(chunks, 4),
            buf(chunks, 4, 2),
            buf(chunks, 3, 2),
        ], [dma((3,)), dma] + [dma((chunks,))] * 6

    def free(self, t):
        wait_bytes(self.bufs[0].at[t % 3, :, self.c], self.sems[0].at[t % 3])

    def push(self, t):
        gbuf, core_in = self.bufs[:2]
        to = (self.rep, self.z * 2 + 1 - self.c)
        remote(
            gbuf.at[t % 3, :, 1 - self.c], core_in.at[t], self.sems[0].at[t % 3],
            self.sems[2].at[t], to,
        )

    def halve(self, t):
        gbuf, core_in, a1, b1 = self.bufs[:4]
        _, sent, core_recv, a1_recv, b1_recv = self.sems[:5]
        wait_bytes(core_in.at[t], core_recv.at[t])
        core_in[t] = core_in[t] + gbuf[t % 3, :, self.c]
        remote(core_in.at[t, :, :, 1 - self.px, 0], a1.at[t], sent, a1_recv.at[t], self.x_peer)
        remote(core_in.at[t, :, 1 - self.py, :, 1], b1.at[t], sent, b1_recv.at[t], self.y_peer)

    def quarter(self, t):
        _, core_in, a1, b1, a2, b2 = self.bufs[:6]
        _, sent, _, a1_recv, b1_recv, a2_recv, b2_recv = self.sems[:7]
        wait_bytes(a1.at[t], a1_recv.at[t])
        a1[t] = a1[t] + core_in[t, :, :, self.px, 0]
        remote(a1.at[t, :, 1 - self.py], a2.at[t], sent, a2_recv.at[t], self.y_peer)
        wait_bytes(b1.at[t], b1_recv.at[t])
        b1[t] = b1[t] + core_in[t, :, self.py, :, 1]
        remote(b1.at[t, :, 1 - self.px], b2.at[t], sent, b2_recv.at[t], self.x_peer)

    def along_z(self, t):
        a1, b1, a2, b2, zsrc, z_in = self.bufs[2:]
        _, sent, _, _, _, a2_recv, b2_recv, z_recv = self.sems
        wait_bytes(a2.at[t], a2_recv.at[t])
        zsrc[t, :, 0] = a1[t, :, self.py] + a2[t]
        wait_bytes(b2.at[t], b2_recv.at[t])
        zsrc[t, :, 1] = b1[t, :, self.px] + b2[t]
        for k in range(1, 4):
            to = (self.z + k) % 4
            remote(zsrc.at[t, to], z_in.at[t, k - 1], sent, z_recv.at[t], (self.rep, to * 2 + self.c))

    def z_sum(self, t):
        zsrc, z_in = self.bufs[6:]
        wait_bytes(z_in.at[t], self.sems[7].at[t])
        return (zsrc[t, self.z] + z_in[t, 0]) + (z_in[t, 1] + z_in[t, 2])

    def finish(self):
        a1, b1, a2, b2, _, z_in = self.bufs[2:]

        def sent(t, carry):
            for ref in (a1, b1, a2, b2, z_in):
                wait_bytes(ref.at[t], self.sems[1])
            return carry

        lax.fori_loop(0, a1.shape[0], sent, 0)
        for i in range(3):
            wait_bytes(self.bufs[0].at[i, :, self.c], self.sems[0].at[i])


PUSH = (0, 1, 2, 3, 8, 9, 10, 11, 16, 17, 18, 19)
HALVE = (1, 3, 5, 7, 9, 10, 11, 13, 17, 19, 21, 23)
QUARTER = (3, 5, 7, 9, 10, 11, 13, 16, 19, 21, 23, 25)
ALONG_Z = (5, 7, 9, 10, 11, 13, 16, 18, 21, 23, 25, 27)
Z_SUM = (8, 9, 11, 12, 14, 16, 19, 21, 24, 26, 28, 29)
FIRST_PUSH = 12


def mid_kernel(
    oh, ol, x, ch, cl, w, s,
    out, dx1, do, part, gs,
    x1, h2h, h2l, uh, ul, acc, chb, clb, dzh, dzl, th, tl, wcol, wrow, *rest,
):
    bufs, sems, (in_sem, w_sem, out_sem) = rest[:8], rest[8:16], rest[16:]
    summing = Summing(bufs, sems)
    gbuf = bufs[0]
    rep, rows = lax.axis_index("rep"), lax.axis_index("rows")
    c = rows % 2
    peers = [(rep, (rows // 2 + k) % 4 * 2 + c) for k in range(1, 4)]
    peers += [(rep, rows // 2 * 2 + 1 - c), summing.x_peer, summing.y_peer]
    arrived = greet(peers)

    o_in = [pltpu.make_async_copy(oh, dzh, in_sem.at[0]), pltpu.make_async_copy(ol, dzl, in_sem.at[1])]
    x_in = pltpu.make_async_copy(x, x1, in_sem.at[2])
    c_in = [pltpu.make_async_copy(ch, chb, in_sem.at[3]), pltpu.make_async_copy(cl, clb, in_sem.at[4])]

    def load(g, start):
        for phase, matrix, by_rows in (
            (0, 3, False), (2, 4, False), (4, 5, True), (5, 4, False), (8, 3, True), (9, 5, False),
        ):

            @pl.when(g // 4 == phase)
            def _():
                if by_rows:
                    src = w.at[col_chunk(g % 4), matrix * D : (matrix + 1) * D]
                    copy = pltpu.make_async_copy(src, wrow.at[g % 2], w_sem.at[g % 2])
                else:
                    src = w.at[:, col_chunk(matrix * (D // CHUNK) + g % 4)]
                    copy = pltpu.make_async_copy(src, wcol.at[g % 2], w_sem.at[g % 2])
                copy.start() if start else copy.wait()

    load(0, True)
    for copy in o_in + [x_in] + c_in:
        copy.start()
    arrived()
    for copy in o_in + [x_in]:
        copy.wait()

    def do_out(n, buf):
        target = do.at[:, pl.ds(pl.multiple_of(n * 2 * CHUNK, 2 * CHUNK), 2 * CHUNK)]
        at = pl.ds(pl.multiple_of(n % 2 * 2 * CHUNK, 2 * CHUNK), 2 * CHUNK)
        return pltpu.make_async_copy(buf.at[:, at], target, out_sem.at[8 + n])

    def step(g, carry):
        load(g + 1, True)

        for table, body in (
            (HALVE, summing.halve),
            (QUARTER, summing.quarter),
            (ALONG_Z, summing.along_z),
        ):
            t = sum(jnp.where(g == at + FIRST_PUSH, i + 1, 0) for i, at in enumerate(table)) - 1
            pl.when(t >= 0)(functools.partial(body, t))
        t = sum(jnp.where(g == at + FIRST_PUSH, i + 1, 0) for i, at in enumerate(Z_SUM)) - 1

        @pl.when(t >= 0)
        def _():
            part[t] = summing.z_sum(t)

        load(g, False)
        n = g % 4
        at = col_chunk(n)

        def phase(p):
            return pl.when(g // 4 == p)

        def gradient(t, high, low):
            @pl.when(t >= 3)
            def _():
                summing.free(t)

            gbuf[t % 3] = mm3(th[...], tl[...], high, low).reshape(gbuf.shape[1:])
            summing.push(t)

        @phase(0)
        def _():
            wh, wl = split(wcol[g % 2])
            x1[:, at] += mm3(dzh[...], dzl[...], wh, wl) + s[4:5, at]

        @phase(1)
        def _():
            normed, _ = norm_parts(x1[at, :])
            h2h[at, :], h2l[at, :] = split(normed * s[5:6, :] + s[6:7, :])

        @phase(2)
        def _():
            wh, wl = split(wcol[g % 2])
            value = mm3(h2h[...], h2l[...], wh, wl) + s[7:8, at]
            square = value * value
            bent = jnp.tanh(ROOT * (value + 0.044715 * value * square))
            uh[:, at], ul[:, at] = split(0.5 * value * (1.0 + bent))
            acc[:, at] = 0.5 * (1.0 + bent) + 0.5 * value * (1.0 - bent * bent) * (
                ROOT * (1.0 + 3.0 * 0.044715 * square)
            )

        @phase(3)
        def _():
            @pl.when(n == 0)
            def _():
                th[...] = uh[...].T
                tl[...] = ul[...].T
                for copy in c_in:
                    copy.wait()

            gradient(n, chb[:, at], clb[:, at])

        @phase(4)
        def _():
            wh, wl = split(wrow[g % 2])
            dz = mm3(chb[...], clb[...], wh, wl, NT) * acc[:, at]
            dzh[:, at], dzl[:, at] = split(dz)
            gs[3:4, at] = col_sum(dz)

        @phase(5)
        def _():
            @pl.when(n == 0)
            def _():
                th[...] = h2h[...].T
                tl[...] = h2l[...].T
                acc[...] = jnp.zeros_like(acc)

            gradient(4 + n, dzh[:, at], dzl[:, at])
            wh, wl = split(wcol[g % 2])

            def some_rows(i, done):
                r = col_chunk(i)
                acc[r, :] += mm3(dzh[r, at], dzl[r, at], wh, wl, NT)
                return done

            lax.fori_loop(0, acc.shape[0] // CHUNK, some_rows, 0)

        @phase(6)
        def _():
            @pl.when(n == 0)
            def _():
                gs[0:3, :] = jnp.zeros((3, D), f32)
                for copy in o_in:
                    copy.start()

            dh2 = acc[at, :]
            normed, rstd = norm_parts(x1[at, :])
            cot = chb[at, :].astype(f32) + clb[at, :].astype(f32)
            grad = cot + norm_back(dh2, normed, rstd, s[5:6, :])
            acc[at, :] = grad
            pltpu.make_async_copy(acc.at[at, :], dx1.at[at, :], out_sem.at[n]).start()
            h2h[at, :], h2l[at, :] = split(grad)
            gs[0:1, :] += col_sum(grad)
            gs[1:2, :] += col_sum(dh2 * normed)
            gs[2:3, :] += col_sum(dh2)

        @phase(7)
        def _():
            @pl.when(n == 0)
            def _():
                for copy in o_in:
                    copy.wait()
                th[...] = dzh[...].T
                tl[...] = dzl[...].T

            gradient(8 + n, h2h[:, at], h2l[:, at])

        @phase(8)
        def _():
            wh, wl = split(wrow[g % 2])
            value = pair_heads(*split(mm3(h2h[...], h2l[...], wh, wl, NT)))
            wide = pl.ds(pl.multiple_of(n % 2 * 2 * CHUNK, 2 * CHUNK), 2 * CHUNK)
            for i, buf in enumerate((dzh, dzl)):

                @pl.when(n // 2 == i)
                def _():
                    buf[:, wide] = value
                    do_out(n, buf).start()

        @phase(9)
        def _():
            wh, wl = split(wcol[g % 2])
            x1[:, at] += mm3(uh[...], ul[...], wh, wl) + s[8:9, at]
            pltpu.make_async_copy(x1.at[:, at], out.at[:, at], out_sem.at[4 + n]).start()

        return carry

    lax.fori_loop(0, FIRST_PUSH + Z_SUM[-1] + 1, step, 0)
    for n in range(4):
        at = col_chunk(n)
        pltpu.make_async_copy(acc.at[at, :], dx1.at[at, :], out_sem.at[n]).wait()
        pltpu.make_async_copy(x1.at[:, at], out.at[:, at], out_sem.at[4 + n]).wait()
        do_out(n, (dzh, dzl)[n // 2]).wait()
    summing.finish()


def mid(oh, ol, x, ch, cl, full, small):
    t = x.shape[0]
    hbm = pl.BlockSpec(memory_space=pl.ANY)
    vmem = pl.BlockSpec(memory_space=pltpu.VMEM)
    dma = pltpu.SemaphoreType.DMA
    chunks = len(PUSH)
    bufs, sems = Summing.scratch(chunks)
    wide, pair = pltpu.VMEM((t, D), f32), [pltpu.VMEM((t, D), bf16)] * 2
    return pl.pallas_call(
        mid_kernel,
        in_specs=[hbm] * 6 + [vmem],
        out_specs=[hbm, hbm, hbm, vmem, vmem],
        out_shape=[
            shape_of((t, D)),
            shape_of((t, D)),
            shape_of((t, 2 * D), bf16),
            shape_of((chunks, 2, 16, CHUNK)),
            shape_of((4, D)),
        ],
        scratch_shapes=[wide, *pair, *pair, wide, *pair, *pair, *pair]
        + [pltpu.VMEM((2, D, CHUNK), f32), pltpu.VMEM((2, CHUNK, D), f32)]
        + bufs
        + sems
        + [dma((5,)), dma((2,)), dma((12,))],
        compiler_params=pltpu.CompilerParams(
            vmem_limit_bytes=60 * 2**20, collective_id=2, has_side_effects=True
        ),
        cost_estimate=cost(9, 60),
        name="mid",
    )(oh, ol, x, ch, cl, full, small)


STAGES = 6


def last_kernel(
    hh, hl, dqh, dql, dkh, dkl, dvh, dvl, w, x, dx1, part, gs_rest, gain,
    out, total, small_total, norm,
    th, tl, dbuf, wbuf, acc, xbuf, dxbuf, obuf, spart, srow, srep, norm_in, *rest,
):
    bufs, sems = rest[:8], rest[8:16]
    gx_recv, gy_recv, fx_recv, fy_recv, spread_send = rest[16:21]
    d_in, w_in, ln_in, ln_out, s_send, s_recv, r_send, r_recv, n_send, n_recv = rest[21:]
    summing = Summing(bufs, sems)
    gbuf = bufs[0]
    rep, rows = lax.axis_index("rep"), lax.axis_index("rows")
    x_peer, y_peer = summing.x_peer, summing.y_peer
    before, chunks = part.shape[0], bufs[1].shape[0]
    per = D // CHUNK
    t_rows = x.shape[0]
    arrived = greet(
        [(rep, (rows + k) % 8) for k in range(1, 8)] + [((rep + k) % 4, rows) for k in range(1, 4)]
    )

    def load_grad(u, start):
        for j, (high, low) in enumerate(((dqh, dql), (dkh, dkl), (dvh, dvl))):

            @pl.when(u // per == j)
            def _():
                for i, source in enumerate((high, low)):
                    copy = pltpu.make_async_copy(
                        source.at[:, col_chunk(u % per)], dbuf.at[u % 2, i], d_in.at[u % 2, i]
                    )
                    copy.start() if start else copy.wait()

        copy = pltpu.make_async_copy(w.at[:, col_chunk(u)], wbuf.at[u % 2], w_in.at[u % 2])
        copy.start() if start else copy.wait()

    def load_h(i, start):
        for j, source in enumerate((hh, hl)):
            copy = pltpu.make_async_copy(
                source.at[:, i * CHUNK : (i + 1) * CHUNK], dbuf.at[i % 2, j], d_in.at[i % 2, j]
            )
            copy.start() if start else copy.wait()

    load_h(0, True)
    for i in range(per):
        if i + 1 < per:
            load_h(i + 1, True)
        load_h(i, False)
        for j, turned in enumerate((th, tl)):
            turned[i * CHUNK : (i + 1) * CHUNK, :] = dbuf[i % 2, j].T
    load_grad(0, True)
    acc[...] = jnp.zeros_like(acc)
    arrived()

    def stage(s, lag, count, body):
        @pl.when(jnp.logical_and(s >= lag, s < count + lag))
        def _():
            body(s - lag)

    def share(t, value):
        total[t, rep] = value
        piece = total.at[t, rep]
        remote(piece, piece, spread_send, gx_recv.at[t], x_peer)
        remote(piece, piece, spread_send, gy_recv.at[t], y_peer)

    def forward(t):
        wait_bytes(total.at[t, 0], gx_recv.at[t])
        piece = total.at[t, x_peer[0], 0]
        remote(piece, piece, spread_send, fy_recv.at[t], y_peer)
        wait_bytes(total.at[t, 0], gy_recv.at[t])
        piece = total.at[t, y_peer[0], 1]
        remote(piece, piece, spread_send, fx_recv.at[t], x_peer)

    def landed(t):
        wait_bytes(total.at[t, 0, 0], fx_recv.at[t])
        wait_bytes(total.at[t, 0, 0], fy_recv.at[t])

    def step(s, carry):
        stage(s, 1, chunks, summing.halve)
        stage(s, 2, chunks, summing.quarter)
        stage(s, 3, chunks, summing.along_z)
        stage(s, 0, before, lambda t: share(t, part[t]))
        stage(s, 1, before, forward)
        stage(s, 2, before, landed)
        stage(s, 4, chunks, lambda t: share(before + t, summing.z_sum(t)))
        stage(s, 5, chunks, lambda t: forward(before + t))
        stage(s, 6, chunks, lambda t: landed(before + t))

        @pl.when(s < chunks)
        def _():
            load_grad(s, False)

            @pl.when(s + 1 < chunks)
            def _():
                load_grad(s + 1, True)

            @pl.when(s >= 3)
            def _():
                summing.free(s)

            grad = mm3(th[...], tl[...], dbuf[s % 2, 0], dbuf[s % 2, 1])
            gbuf[s % 3] = grad.reshape(gbuf.shape[1:])
            summing.push(s)
            wh, wl = split(wbuf[s % 2])

            def some_rows(i, done):
                at = col_chunk(i)
                acc[at, :] += mm3(dbuf[s % 2, 0, at, :], dbuf[s % 2, 1, at, :], wh, wl, NT)
                return done

            lax.fori_loop(0, t_rows // CHUNK, some_rows, 0)

        @pl.when(jnp.logical_and(s >= chunks, s < chunks + 4))
        def _():
            size = t_rows // 4
            at = pl.ds(pl.multiple_of((s - chunks) * size, size), size)
            copies = [
                pltpu.make_async_copy(x.at[at, :], xbuf, ln_in.at[0]),
                pltpu.make_async_copy(dx1.at[at, :], dxbuf, ln_in.at[1]),
            ]
            for copy in copies:
                copy.start()
            for copy in copies:
                copy.wait()
            dh = acc[at, :]
            normed, rstd = norm_parts(xbuf[...])
            obuf[...] = dxbuf[...] + norm_back(dh, normed, rstd, gain[...])
            store = pltpu.make_async_copy(obuf, out.at[at, :], ln_out)
            store.start()
            gs = jnp.concatenate([col_sum(dh * normed), col_sum(dh)], axis=0)
            for j in range(8):
                piece = gs[:, j * 128 : (j + 1) * 128]

                @pl.when(s == chunks)
                def _():
                    spart[j, 0:2] = piece
                    spart[j, 2:9] = gs_rest[:, j * 128 : (j + 1) * 128]

                @pl.when(s > chunks)
                def _():
                    spart[j, 0:2] += piece

            store.wait()

        @pl.when(s == chunks + 4)
        def _():
            for k in range(1, 8):
                to = (rows + k) % 8
                remote(spart.at[to], srow.at[k - 1], s_send.at[k - 1], s_recv.at[k - 1], (rep, to))

        @pl.when(s == chunks + 5)
        def _():
            mine = spart[rows]
            for k in range(1, 8):
                wait_bytes(srow.at[k - 1], s_recv.at[k - 1])
                mine = mine + srow[k - 1]
            srep[rep] = mine
            for k in range(1, 4):
                piece = srep.at[rep]
                remote(piece, piece, r_send.at[k - 1], r_recv.at[k - 1], ((rep + k) % 4, rows))

        return carry

    lax.fori_loop(0, chunks + STAGES + 1, step, 0)
    for k in range(1, 4):
        wait_bytes(srep.at[0], r_recv.at[k - 1])
    small = (srep[0] + srep[1]) + (srep[2] + srep[3])
    small_total[...] = small

    def squares(t, carry):
        value = total[t].reshape(128, CHUNK)
        return carry + jnp.sum((value * value).reshape(16, 8, CHUNK), axis=0)

    mats = lax.fori_loop(0, before + chunks, squares, jnp.zeros((8, CHUNK), f32))
    mine = jnp.sum(mats) + jnp.sum(small * small)
    norm_in[rows] = jnp.full((8, 128), mine, f32)
    for k in range(1, 8):
        piece = norm_in.at[rows]
        remote(piece, piece, n_send.at[k - 1], n_recv.at[k - 1], (rep, (rows + k) % 8))
    for k in range(1, 8):
        wait_bytes(norm_in.at[0], n_recv.at[k - 1])
    value = norm_in[0]
    for j in range(1, 8):
        value = value + norm_in[j]
    norm[...] = jnp.sqrt(value)

    summing.finish()

    def sent(t, carry):
        wait_bytes(total.at[t, 0:3], spread_send)
        return carry

    lax.fori_loop(0, before + chunks, sent, 0)
    for k in range(1, 8):
        wait_bytes(srow.at[k - 1], s_send.at[k - 1])
        wait_bytes(norm_in.at[0], n_send.at[k - 1])
    for k in range(1, 4):
        wait_bytes(srep.at[0], r_send.at[k - 1])


def last(hh, hl, grads, full, x, dx1, part, gs_rest, gain):
    t = x.shape[0]
    chunks = 3 * D // CHUNK
    every = chunks + part.shape[0]
    hbm = pl.BlockSpec(memory_space=pl.ANY)
    vmem = pl.BlockSpec(memory_space=pltpu.VMEM)
    dma = pltpu.SemaphoreType.DMA
    bufs, sems = Summing.scratch(chunks)
    return pl.pallas_call(
        last_kernel,
        in_specs=[hbm] * 11 + [vmem] * 3,
        out_specs=[hbm, vmem, vmem, vmem],
        out_shape=[
            shape_of((t, D)),
            shape_of((every, 4, 2, 16, CHUNK)),
            shape_of((9, 128)),
            shape_of((8, 128)),
        ],
        scratch_shapes=[
            pltpu.VMEM((D, t), bf16),
            pltpu.VMEM((D, t), bf16),
            pltpu.VMEM((2, 2, t, CHUNK), bf16),
            pltpu.VMEM((2, D, CHUNK), f32),
            pltpu.VMEM((t, D), f32),
            pltpu.VMEM((t // 4, D), f32),
            pltpu.VMEM((t // 4, D), f32),
            pltpu.VMEM((t // 4, D), f32),
            pltpu.VMEM((8, 9, 128), f32),
            pltpu.VMEM((7, 9, 128), f32),
            pltpu.VMEM((4, 9, 128), f32),
            pltpu.VMEM((8, 8, 128), f32),
        ]
        + bufs
        + sems
        + [dma((every,))] * 4
        + [dma, dma((2, 2)), dma((2,)), dma((2,)), dma]
        + [dma((7,)), dma((7,)), dma((3,)), dma((3,)), dma((7,)), dma((7,))],
        compiler_params=pltpu.CompilerParams(
            vmem_limit_bytes=60 * 2**20, collective_id=1, has_side_effects=True
        ),
        cost_estimate=cost(6, 90),
        name="last",
    )(hh, hl, *grads, full, x, dx1, part, gs_rest, gain)


def adam_step(parameter, gradient, first_moment, second_moment, average):
    first_new = 0.9 * first_moment + 0.1 * gradient
    second_new = 0.999 * second_moment + 0.001 * gradient * gradient
    first_hat = first_new / (1.0 - 0.9**STEP)
    second_hat = second_new / (1.0 - 0.999**STEP)
    parameter_new = parameter - 0.05 * (
        first_hat / (jnp.sqrt(second_hat) + 1e-08) + 0.05 * parameter
    )
    average_new = 0.99 * average + 0.01 * parameter_new
    return (parameter_new, first_new, second_new, average_new)


CLIP = 0.25 * math.sqrt(6 * D * D + 9 * D)


def adam_kernel(
    grad, norm, w, first, second, average, gs, p_s, first_s, second_s, average_s,
    clipped, new_w, first_o, second_o, average_o, low,
    clipped_so, new_so, first_so, second_so, average_so, low_so,
):
    factor = jnp.minimum(1.0, CLIP / norm[0:1, 0:1])
    for j in range(D // CHUNK):
        at = slice(j * CHUNK, (j + 1) * CHUNK)
        value = grad[j].reshape(w.shape[0], CHUNK) * factor
        clipped[:, at] = value
        news = adam_step(w[:, at], value, first[:, at], second[:, at], average[:, at])
        for ref, new in zip((new_w, first_o, second_o, average_o), news):
            ref[:, at] = new
        low[:, at] = news[0].astype(bf16)

    @pl.when(pl.program_id(0) == 0)
    def _():
        value = gs[...] * factor
        clipped_so[...] = value
        news = adam_step(p_s[...], value, first_s[...], second_s[...], average_s[...])
        for ref, new in zip((new_so, first_so, second_so, average_so), news):
            ref[...] = new
        low_so[...] = news[0].astype(bf16)


def adam(total, norm, mats, gs, smalls):
    shard, width = mats[0].shape
    block = pl.BlockSpec((shard, D), lambda i: (0, jnp.where(i < 3, 5 - i, i - 3)))
    grads = pl.BlockSpec((D // CHUNK,) + total.shape[1:], lambda i: (i, 0, 0, 0, 0))
    small = whole(gs.shape)
    return pl.pallas_call(
        adam_kernel,
        grid=(width // D,),
        in_specs=[grads, whole(norm.shape)] + [block] * 4 + [small] * 5,
        out_specs=[block] * 6 + [small] * 6,
        out_shape=[shape_of((shard, width))] * 5
        + [shape_of((shard, width), bf16)]
        + [shape_of(gs.shape)] * 5
        + [shape_of(gs.shape, bf16)],
        compiler_params=params(),
        cost_estimate=cost(0, 32),
        name="adam",
    )(total, norm, *mats, gs, *smalls)


def split_once(w, wh, wl):
    @pl.when(pl.program_id(0) == 0)
    def _():
        wh[...], wl[...] = split(w[...])


def out_proj_kernel(oh, ol, w, x, s, x1, h2h, h2l, wh, wl):
    split_once(w, wh, wl)
    value = x[...] + mm3(oh[...], ol[...], wh[...], wl[...]) + s[4:5]
    x1[...] = value
    normed, _ = norm_parts(value)
    h2h[...], h2l[...] = split(normed * s[5:6] + s[6:7])


def out_proj(oh, ol, w, x, small, bm=256):
    t = x.shape[0]
    return pl.pallas_call(
        out_proj_kernel,
        grid=(t // bm,),
        in_specs=[rows_of(bm, D)] * 2 + [matrix(3), rows_of(bm, D), whole((9, D))],
        out_specs=[rows_of(bm, D)] * 3,
        out_shape=[shape_of((t, D)), shape_of((t, D), bf16), shape_of((t, D), bf16)],
        scratch_shapes=[pltpu.VMEM((D, D), bf16)] * 2,
        compiler_params=params(),
        cost_estimate=cost(1, 20),
        name="out_proj",
    )(oh, ol, w, x, small)


def up_kernel(hh, hl, w, s, z, uh, ul):
    wh, wl = split(w[...])
    value = mm3(hh[...], hl[...], wh, wl) + s[7:8]
    z[...] = value
    bent = jnp.tanh(ROOT * (value + 0.044715 * value * value * value))
    uh[...], ul[...] = split(0.5 * value * (1.0 + bent))


def up(hh, hl, w, small, bn=256):
    t = hh.shape[0]
    return pl.pallas_call(
        up_kernel,
        grid=(FF // bn,),
        in_specs=[whole((t, D))] * 2 + [cols_of(D, bn, 4 * D // bn), cols_of(9, bn)],
        out_specs=[cols_of(t, bn)] * 3,
        out_shape=[shape_of((t, FF)), shape_of((t, FF), bf16), shape_of((t, FF), bf16)],
        compiler_params=params(),
        cost_estimate=cost(1, 16),
        name="up",
    )(hh, hl, w, small)


def down_kernel(uh, ul, w, x1, s, out):
    wh, wl = split(w[...])
    out[...] = x1[...] + mm3(uh[...], ul[...], wh, wl) + s[8:9]


def down(uh, ul, w, x1, small, bn=256):
    t = uh.shape[0]
    return pl.pallas_call(
        down_kernel,
        grid=(D // bn,),
        in_specs=[whole((t, FF))] * 2
        + [cols_of(FF, bn, 5 * D // bn), cols_of(t, bn), cols_of(9, bn)],
        out_specs=cols_of(t, bn),
        out_shape=shape_of((t, D)),
        compiler_params=params(),
        cost_estimate=cost(1, 16),
        name="down",
    )(uh, ul, w, x1, small)


def outer_kernel(ah, al, dh, dl, out, th, tl):
    @pl.when(pl.program_id(0) == 0)
    def _():
        th[...] = ah[...].T
        tl[...] = al[...].T

    out[...] = mm3(th[...], tl[...], dh[...], dl[...])


def outer(ah, al, dh, dl, bn=256):
    t, m = ah.shape
    n = dh.shape[1]
    return pl.pallas_call(
        outer_kernel,
        grid=(n // bn,),
        in_specs=[whole((t, m))] * 2 + [cols_of(t, bn)] * 2,
        out_specs=cols_of(m, bn),
        out_shape=shape_of((m, n)),
        scratch_shapes=[pltpu.VMEM((m, t), bf16)] * 2,
        compiler_params=params(),
        cost_estimate=cost(1, 12),
        name="outer",
    )(ah, al, dh, dl)


def down_back_kernel(ch, cl, w, z, dzh, dzl, gs7):
    wh, wl = split(w[...])
    du = mm3(ch[...], cl[...], wh, wl, NT)
    value = z[...]
    square = value * value
    bent = jnp.tanh(ROOT * (value + 0.044715 * value * square))
    slope = 0.5 * (1.0 + bent) + 0.5 * value * (1.0 - bent * bent) * (
        ROOT * (1.0 + 3.0 * 0.044715 * square)
    )
    dz = du * slope
    dzh[...], dzl[...] = split(dz)
    gs7[...] = col_sum(dz)


def down_back(ch, cl, w, z, bn=256):
    t = ch.shape[0]
    return pl.pallas_call(
        down_back_kernel,
        grid=(FF // bn,),
        in_specs=[whole((t, D))] * 2 + [rows_of(bn, D, 5), cols_of(t, bn)],
        out_specs=[cols_of(t, bn)] * 2 + [cols_of(1, bn)],
        out_shape=[shape_of((t, FF), bf16)] * 2 + [shape_of((1, FF))],
        compiler_params=params(),
        cost_estimate=cost(1, 16),
        name="down_back",
    )(ch, cl, w, z)


def up_back_kernel(dzh, dzl, w, x1, cot, s, dx1, dxh, dxl, gs4, gs5, gs6, wh, wl):
    split_once(w, wh, wl)
    dh2 = mm3(dzh[...], dzl[...], wh[...], wl[...], NT)
    normed, rstd = norm_parts(x1[...])
    grad = cot[...] + norm_back(dh2, normed, rstd, s[5:6])
    dx1[...] = grad
    dxh[...], dxl[...] = split(grad)
    add_up(gs4, col_sum(grad))
    add_up(gs5, col_sum(dh2 * normed))
    add_up(gs6, col_sum(dh2))


def up_back(dzh, dzl, w, x1, cot, small, bm=256):
    t = x1.shape[0]
    return pl.pallas_call(
        up_back_kernel,
        grid=(t // bm,),
        in_specs=[rows_of(bm, FF)] * 2 + [matrix(4)] + [rows_of(bm, D)] * 2 + [whole((9, D))],
        out_specs=[rows_of(bm, D)] * 3 + [whole((1, D))] * 3,
        out_shape=[shape_of((t, D)), shape_of((t, D), bf16), shape_of((t, D), bf16)]
        + [shape_of((1, D))] * 3,
        scratch_shapes=[pltpu.VMEM((D, FF), bf16)] * 2,
        compiler_params=params(),
        cost_estimate=cost(1, 24),
        name="up_back",
    )(dzh, dzl, w, x1, cot, small)


def out_proj_back_kernel(dxh, dxl, w, do):
    wh, wl = split(w[...])
    do[...] = pair_heads(*split(mm3(dxh[...], dxl[...], wh, wl, NT)))


def out_proj_back(dxh, dxl, w, bn=256):
    t = dxh.shape[0]
    return pl.pallas_call(
        out_proj_back_kernel,
        grid=(D // bn,),
        in_specs=[whole((t, D))] * 2 + [rows_of(bn, D, 3)],
        out_specs=cols_of(t, 2 * bn),
        out_shape=shape_of((t, 2 * D), bf16),
        compiler_params=params(),
        cost_estimate=cost(1, 12),
        name="out_proj_back",
    )(dxh, dxl, w)


def proj_back_kernel(
    dqh, dql, dkh, dkl, dvh, dvl, wq, wk, wv, x, dx1, s, out, gs0, gs1, wh, wl
):
    @pl.when(pl.program_id(0) == 0)
    def _():
        for j, w in enumerate((wq, wk, wv)):
            wh[j], wl[j] = split(w[...])

    dh = mm3(dqh[...], dql[...], wh[0], wl[0], NT)
    dh += mm3(dkh[...], dkl[...], wh[1], wl[1], NT)
    dh += mm3(dvh[...], dvl[...], wh[2], wl[2], NT)
    normed, rstd = norm_parts(x[...])
    out[...] = dx1[...] + norm_back(dh, normed, rstd, s[0:1])
    add_up(gs0, col_sum(dh * normed))
    add_up(gs1, col_sum(dh))


def proj_back(grads, w, x, dx1, small, bm=256):
    t = x.shape[0]
    return pl.pallas_call(
        proj_back_kernel,
        grid=(t // bm,),
        in_specs=[rows_of(bm, D)] * 6 + [matrix(j) for j in range(3)] + [rows_of(bm, D)] * 2 + [whole((9, D))],
        out_specs=[rows_of(bm, D)] + [whole((1, D))] * 2,
        out_shape=[shape_of((t, D))] + [shape_of((1, D))] * 2,
        scratch_shapes=[pltpu.VMEM((3, D, D), bf16)] * 2,
        compiler_params=params(),
        cost_estimate=cost(3, 36),
        name="proj_back",
    )(*grads, w, w, w, x, dx1, small)


def set_bounds(segment_ids):
    ids = segment_ids[0, ::UNIT]
    order, sets = (ids - ids[0])[None, :], jnp.arange(SETS, dtype=jnp.int32)[:, None]
    lengths = jnp.sum((order == sets).astype(jnp.int32), axis=1)
    firsts = jnp.sum((order < sets).astype(jnp.int32), axis=1)
    return jnp.stack([firsts, lengths], axis=1).reshape(-1).astype(jnp.int32)


def shards(
    reps,
    latents,
    cotangent,
    segment_ids,
    weights,
    small_params,
    first_mats,
    second_mats,
    average_mats,
    first_small,
    second_small,
    average_small,
):
    segs = set_bounds(segment_ids)
    x, cot = latents[0], cotangent[0]
    fast = reps == 4 and weights.shape[0] * 8 == D
    if fast:
        full, small, hh, hl, ch, cl, gs8, qkv = gather(weights, small_params, x, cot)
    else:
        full, small = (
            lax.all_gather(weights, "rows", axis=0, tiled=True),
            lax.all_gather(small_params, "rows", axis=1, tiled=True),
        )
        bias = jnp.concatenate([small[2], jnp.zeros((D,), f32), small[3]])[None]
        hh, hl, ch, cl, gs8 = prep(x, cot, small)
        qkv = proj(hh, hl, full, bias)
    oh, ol, lse = attend(segs, qkv)
    if fast:
        output, dx1, do, part, gs4567 = mid(oh, ol, x, ch, cl, full, small)
    else:
        x1, h2h, h2l = out_proj(oh, ol, full, x, small)
        z, uh, ul = up(h2h, h2l, full, small)
        output = down(uh, ul, full, x1, small)
        g_down = outer(uh, ul, ch, cl)
        dzh, dzl, gs7 = down_back(ch, cl, full, z)
        g_up = outer(h2h, h2l, dzh, dzl)
        dx1, dxh, dxl, gs4, gs5, gs6 = up_back(dzh, dzl, full, x1, cot, small)
        g_out = outer(oh, ol, dxh, dxl)
        do = out_proj_back(dxh, dxl, full)
        gs4567 = jnp.concatenate([gs4, gs5, gs6, gs7], axis=0)
    *grads, gs2, gs3 = attend_back(segs, qkv, do, oh, ol, lse)
    gs_rest = jnp.concatenate([gs2, gs3, gs4567, gs8], axis=0)
    if fast:
        token_grad, total, small_total, norm = last(
            hh, hl, grads, full, x, dx1, part, gs_rest, small[0:1]
        )
        (
            clipped_mats, new_weights, first_mats_out, second_mats_out, average_mats_out, low_mats,
            clipped_small, new_small, first_small_out, second_small_out, average_small_out, low_small,
        ) = adam(
            total, norm, (weights, first_mats, second_mats, average_mats), small_total,
            (small_params, first_small, second_small, average_small),
        )
        norm = norm[0, 0:1]
    else:
        g_qkv = [outer(hh, hl, grads[2 * j], grads[2 * j + 1]) for j in range(3)]
        token_grad, gs0, gs1 = proj_back(grads, full, x, dx1, small)
        weight_grad = jnp.concatenate(g_qkv + [g_out, g_up, g_down], axis=1)
        small_grad = jnp.concatenate([gs0, gs1, gs_rest], axis=0)
        part_weights, part_small = (
            lax.psum_scatter(weight_grad, "rows", scatter_dimension=0, tiled=True),
            lax.psum_scatter(small_grad, "rows", scatter_dimension=1, tiled=True),
        )
        sum_weights, sum_small = lax.psum((part_weights, part_small), "rep")
        squares = lax.psum(
            jnp.sum(sum_weights * sum_weights) + jnp.sum(sum_small * sum_small), "rows"
        )
        norm = jnp.sqrt(squares).reshape(1)
        factor = jnp.minimum(1.0, CLIP / norm[0])
        clipped_mats = sum_weights * factor
        clipped_small = sum_small * factor
        new_weights, first_mats_out, second_mats_out, average_mats_out = adam_step(
            weights, clipped_mats, first_mats, second_mats, average_mats
        )
        new_small, first_small_out, second_small_out, average_small_out = adam_step(
            small_params, clipped_small, first_small, second_small, average_small
        )
        low_mats, low_small = new_weights.astype(bf16), new_small.astype(bf16)
    return (
        output[None],
        token_grad[None],
        norm,
        clipped_mats,
        clipped_small,
        new_weights,
        new_small,
        first_mats_out,
        second_mats_out,
        average_mats_out,
        first_small_out,
        second_small_out,
        average_small_out,
        low_mats,
        low_small,
    )


def solution(mesh):
    tokens, mats, small = P("rep", "rows", None), P("rows", None), P(None, "rows")
    in_specs = (tokens, tokens, P("rep", "rows")) + (mats, small) + (mats,) * 3 + (small,) * 3
    out_specs = (
        (tokens, tokens, P(), mats, small, mats, small) + (mats,) * 3 + (small,) * 3 + (mats, small)
    )
    step = functools.partial(shards, mesh.shape["rep"])
    return jax.shard_map(step, mesh=mesh, in_specs=in_specs, out_specs=out_specs, check_vma=False)
```

```python
import functools
import math

import jax
import jax.numpy as jnp
from jax import lax
from jax.experimental import pallas as pl
from jax.experimental.pallas import tpu as pltpu
from jax.sharding import PartitionSpec as P

D = 1024
HEADS = 8
HEAD_DIM = 128
FF = 1024
UNIT = 128
SETS = 3
STEP = 5
SCALE = HEAD_DIM ** (-0.5)
ROOT = math.sqrt(2.0 / math.pi)

f32 = jnp.float32
bf16 = jnp.bfloat16

NN = (((1,), (0,)), ((), ()))
NT = (((1,), (1,)), ((), ()))
TN = (((0,), (0,)), ((), ()))


def params(mib=56):
    return pltpu.CompilerParams(
        vmem_limit_bytes=mib * 2**20, dimension_semantics=("arbitrary",)
    )


def mm(a, b, dims=NN):
    return lax.dot_general(a, b, dims, preferred_element_type=f32)


def split(x):
    high = x.astype(bf16)
    return high, (x - high.astype(f32)).astype(bf16)


def mm3(ah, al, bh, bl, dims=NN):
    return mm(ah, bh, dims) + (mm(al, bh, dims) + mm(ah, bl, dims))


def cost(products, mib):
    return pl.CostEstimate(
        flops=int(products * 3 * 2 * 1024**3), bytes_accessed=int(mib * 2**20), transcendentals=0
    )


def whole(shape):
    return pl.BlockSpec(shape, lambda *i: (0,) * len(shape))


def rows_of(bm, n, column=0):
    return pl.BlockSpec((bm, n), lambda i, *_: (i, column))


def matrix(j):
    return pl.BlockSpec((D, D), lambda i: (0, j), pipeline_mode=pl.Buffered(1))


def cols_of(m, bn, first=0):
    return pl.BlockSpec((m, bn), lambda i, *_: (0, first + i))


def shape_of(shape, dtype=f32):
    return jax.ShapeDtypeStruct(shape, dtype)


def norm_parts(x):
    center = x - jnp.mean(x, axis=-1, keepdims=True)
    rstd = lax.rsqrt(jnp.mean(center * center, axis=-1, keepdims=True) + 1e-05)
    return center * rstd, rstd


def norm_back(grad, normed, rstd, gain):
    scaled = grad * gain
    return rstd * (
        scaled
        - jnp.mean(scaled, axis=-1, keepdims=True)
        - normed * jnp.mean(scaled * normed, axis=-1, keepdims=True)
    )


def col_sum(x):
    return jnp.sum(x, axis=0, keepdims=True)


def add_up(ref, value):
    first = pl.program_id(0) == 0

    @pl.when(first)
    def _():
        ref[...] = value

    @pl.when(jnp.logical_not(first))
    def _():
        ref[...] += value


def prep_kernel(x, cot, s, hh, hl, ch, cl, gs8):
    normed, _ = norm_parts(x[...])
    hh[...], hl[...] = split(normed * s[0:1] + s[1:2])
    ch[...], cl[...] = split(cot[...])
    add_up(gs8, col_sum(cot[...]))


def prep(x, cot, small, bm=256):
    t = x.shape[0]
    return pl.pallas_call(
        prep_kernel,
        grid=(t // bm,),
        in_specs=[rows_of(bm, D), rows_of(bm, D), whole((9, D))],
        out_specs=[rows_of(bm, D)] * 4 + [whole((1, D))],
        out_shape=[shape_of((t, D), bf16)] * 4 + [shape_of((1, D))],
        compiler_params=params(),
        cost_estimate=cost(0, 16),
        name="prep",
    )(x, cot, small)


def pair_heads(high, low):
    parts = []
    for head in range(high.shape[1] // HEAD_DIM):
        cut = slice(head * HEAD_DIM, (head + 1) * HEAD_DIM)
        parts += [high[:, cut], low[:, cut]]
    return jnp.concatenate(parts, axis=1)


def proj_kernel(hh, hl, w, bias, out):
    wh, wl = split(w[...])
    out[...] = pair_heads(*split(mm3(hh[...], hl[...], wh, wl) + bias[...]))


def proj(hh, hl, w, bias, bn=256):
    t, n = hh.shape[0], bias.shape[1]
    return pl.pallas_call(
        proj_kernel,
        grid=(n // bn,),
        in_specs=[whole((t, D))] * 2 + [cols_of(D, bn), cols_of(1, bn)],
        out_specs=cols_of(t, 2 * bn),
        out_shape=shape_of((t, 2 * n), bf16),
        compiler_params=params(),
        cost_estimate=cost(n // D, 8 * (n // D) + 4),
        name="proj",
    )(hh, hl, w, bias)


def twice(a):
    return jnp.concatenate([a, a], axis=1)


def halves_sum(x):
    return x[:, :HEAD_DIM] + x[:, HEAD_DIM:]


def pieces(n):
    out, at = [], 0
    while at < n:
        size = min(256, n - at)
        out.append((at, size))
        at += size
    return out


def for_sets(segs, units, body):
    def one(i, carry):
        first, length = segs[2 * i], segs[2 * i + 1]
        for count in range(1, units - SETS + 2):

            @pl.when(length == count)
            def _():
                body(pl.multiple_of(first * UNIT, UNIT), count * UNIT)

        return carry

    lax.fori_loop(0, SETS, one, 0)


def attend_kernel(segs, q, k, v, oh, ol, lse):
    units = q.shape[0] // UNIT

    def body(first, n):
        rows = pl.ds(first, n)
        keys = k[rows, :]
        kh, kl = twice(keys[:, :HEAD_DIM]), twice(keys[:, HEAD_DIM:])
        vals = v[rows, :]
        for at, size in pieces(n):
            sub = pl.ds(pl.multiple_of(first + at, UNIT), size)
            qs = q[sub, :]
            scores = mm(qs, kh, NT) + mm(qs, kl, NT)
            top = jnp.max(scores, axis=-1, keepdims=True)
            p = jnp.exp((scores - top) * SCALE)
            total = jnp.sum(p, axis=-1, keepdims=True)
            ph, plow = split(p)
            o = halves_sum(mm(ph, vals) + mm(plow, vals)) / total
            oh[sub, :], ol[sub, :] = split(o)
            level = top * SCALE + jnp.log(total)
            for u in range(size // UNIT):
                tile = jnp.broadcast_to(level[u * UNIT : (u + 1) * UNIT], (UNIT, UNIT))
                lse[0, :, pl.ds(pl.multiple_of(first + at + u * UNIT, UNIT), UNIT)] = tile.T[0:8]

    for_sets(segs, units, body)


def attend(segs, qkv):
    t = qkv.shape[0]
    head = lambda first: pl.BlockSpec((t, 2 * HEAD_DIM), lambda i, *_: (0, first + i))
    return pl.pallas_call(
        attend_kernel,
        grid_spec=pltpu.PrefetchScalarGridSpec(
            num_scalar_prefetch=1,
            grid=(HEADS,),
            in_specs=[head(0), head(HEADS), head(2 * HEADS)],
            out_specs=[cols_of(t, HEAD_DIM)] * 2
            + [pl.BlockSpec((1, 8, t), lambda i, *_: (i, 0, 0))],
        ),
        out_shape=[shape_of((t, D), bf16)] * 2 + [shape_of((HEADS, 8, t))],
        compiler_params=params(),
        cost_estimate=cost(2, 16),
        name="attend",
    )(segs, qkv, qkv, qkv)


def attend_back_kernel(
    segs, q, k, v, do, oh, ol, lse, dqh, dql, dkh, dkl, dvh, dvl, gq, gv, drow, qsum, vsum
):
    units = q.shape[0] // UNIT
    for u in range(units):
        cut = slice(u * UNIT, (u + 1) * UNIT)
        grad = do[cut, :].astype(f32)
        out = oh[cut, :].astype(f32) + ol[cut, :].astype(f32)
        tile = (halves_sum(grad) * out).T
        drow[:, cut] = jnp.broadcast_to(col_sum(tile), (8, UNIT))
    qsum[...] = jnp.zeros_like(qsum)
    vsum[...] = jnp.zeros_like(vsum)

    def body(first, n):
        rows = pl.ds(first, n)
        keys, vals = k[rows, :], v[rows, :]
        dk = dv = None
        for at, size in pieces(n):
            sub = pl.ds(pl.multiple_of(first + at, UNIT), size)
            qs, grad = q[sub, :], do[sub, :]
            scores = mm(keys, twice(qs[:, :HEAD_DIM]), NT) + mm(keys, twice(qs[:, HEAD_DIM:]), NT)
            p = jnp.exp(scores * SCALE - lse[0, 0:1, sub])
            dp = mm(vals, twice(grad[:, :HEAD_DIM]), NT) + mm(vals, twice(grad[:, HEAD_DIM:]), NT)
            ds = p * (dp - drow[0:1, sub])
            ph, plow = split(p)
            dsh, dsl = split(ds)
            dv_part = mm(ph, grad) + mm(plow, grad)
            dk_part = mm(dsh, qs) + mm(dsl, qs)
            dv = dv_part if dv is None else dv + dv_part
            dk = dk_part if dk is None else dk + dk_part
            dq = halves_sum(mm(dsh, keys, TN) + mm(dsl, keys, TN)) * SCALE
            dqh[sub, :], dql[sub, :] = split(dq)
            qsum[0:1, :] += col_sum(dq)
        dk = halves_sum(dk) * SCALE
        dv = halves_sum(dv)
        dkh[rows, :], dkl[rows, :] = split(dk)
        dvh[rows, :], dvl[rows, :] = split(dv)
        vsum[0:1, :] += col_sum(dv)

    for_sets(segs, units, body)
    gq[...] = qsum[0:1, :]
    gv[...] = vsum[0:1, :]


def attend_back(segs, qkv, do, oh, ol, lse):
    t = qkv.shape[0]
    head = lambda first: pl.BlockSpec((t, 2 * HEAD_DIM), lambda i, *_: (0, first + i))
    return pl.pallas_call(
        attend_back_kernel,
        grid_spec=pltpu.PrefetchScalarGridSpec(
            num_scalar_prefetch=1,
            grid=(HEADS,),
            in_specs=[head(0), head(HEADS), head(2 * HEADS), head(0)]
            + [cols_of(t, HEAD_DIM)] * 2
            + [pl.BlockSpec((1, 8, t), lambda i, *_: (i, 0, 0))],
            out_specs=[cols_of(t, HEAD_DIM)] * 6 + [cols_of(1, HEAD_DIM)] * 2,
            scratch_shapes=[
                pltpu.VMEM((8, t), f32),
                pltpu.VMEM((8, HEAD_DIM), f32),
                pltpu.VMEM((8, HEAD_DIM), f32),
            ],
        ),
        out_shape=[shape_of((t, D), bf16)] * 6 + [shape_of((1, D))] * 2,
        compiler_params=params(),
        cost_estimate=cost(5, 36),
        name="attend_back",
    )(segs, qkv, qkv, qkv, do, oh, ol, lse)


MESH = pl.DeviceIdType.MESH
CHUNK = 256
AHEAD, SPREAD, SWAP, USE = 4, 2, 4, 6


def wait_bytes(ref, sem):
    pltpu.make_async_copy(ref, ref, sem).wait()


def gather_kernel(
    w, own_small, x, cot, sets,
    full, small, th, tl, ch, cl, gs8, qkv, oh, ol, lse,
    pieces, own, xbuf, cbuf, hhb, hlb, thb, tlb, chb, clb, wbuf, qkvb, ohb, olb,
    small_send, small_recv, own_sem, send_sem, core_send, own_recv,
    z_recv, x_recv, y_recv, fx_recv, fy_recv, core_recv, in_sem, out_sem, w_sem, q_sem,
):
    rep, rows = lax.axis_index("rep"), lax.axis_index("rows")
    z, c = rows // 2, rows % 2
    x_next, y_next = rep // 2 * 2 + (1 - rep % 2), (1 - rep // 2) * 2 + rep % 2
    shard = w.shape[0]
    quarter, half = shard // 4, shard // 8
    chunks = w.shape[1] // CHUNK
    proj_chunks = 3 * D // CHUNK
    per = D // CHUNK

    x_in = pltpu.make_async_copy(x, xbuf, in_sem.at[0])
    c_in = pltpu.make_async_copy(cot, cbuf, in_sem.at[1])
    x_in.start()
    c_in.start()
    own_in = pltpu.make_async_copy(w, own, own_sem)
    own_in.start()

    barrier = pltpu.get_barrier_semaphore()
    peers = [(rep, (rows + k) % 8) for k in range(1, 8)] + [(x_next, rows), (y_next, rows)]
    for peer in peers:
        pl.semaphore_signal(barrier, inc=1, device_id=peer, device_id_type=MESH)
    pl.semaphore_wait(barrier, len(peers))

    def send(src, dst, sem, recv, device):
        pltpu.make_async_remote_copy(
            src_ref=src, dst_ref=dst, send_sem=sem, recv_sem=recv, device_id=device,
            device_id_type=MESH,
        ).start()

    for k in range(1, 8):
        send(own_small, pieces.at[k - 1], small_send.at[k - 1], small_recv.at[k - 1], (rep, (rows + k) % 8))

    def column(t):
        return jnp.where(t < proj_chunks, t % 3 * per + t // 3, t)

    def cols(t):
        return pl.ds(pl.multiple_of(column(t) * CHUNK, CHUNK), CHUNK)

    def place(zz, first, count, t):
        at = (zz * 2 + c) * shard + first
        return full.at[pl.ds(pl.multiple_of(at, half), count), cols(t)]

    def start_z(t):
        src = w.at[pl.ds(pl.multiple_of(rep * quarter, quarter), quarter), cols(t)]
        for k in range(1, 4):
            send(src, place(z, rep * quarter, quarter, t), send_sem, z_recv.at[t], (rep, (z + k) % 4 * 2 + c))

    for t in range(AHEAD):
        start_z(t)
    send(w, full.at[pl.ds(rows * shard, shard), :], core_send, own_recv, (rep, z * 2 + 1 - c))

    for k in range(1, 8):
        pltpu.make_async_copy(own_small, pieces.at[k - 1], small_recv.at[k - 1]).wait()
        pltpu.make_async_copy(own_small, pieces.at[k - 1], small_send.at[k - 1]).wait()
    width = own_small.shape[1]
    small[:, pl.ds(pl.multiple_of(rows * width, width), width)] = own_small[...]
    for k in range(1, 8):
        at = pl.multiple_of((rows + 8 - k) % 8 * width, width)
        small[:, pl.ds(at, width)] = pieces[k - 1]

    own_in.wait()
    own_out = pltpu.make_async_copy(own, full.at[pl.ds(rows * shard, shard), :], own_sem)
    own_out.start()
    x_in.wait()

    def norm_rows(i, carry):
        at = pl.ds(pl.multiple_of(i * 128, 128), 128)
        normed, _ = norm_parts(xbuf[at, :])
        hhb[at, :], hlb[at, :] = split(normed * small[0:1, :] + small[1:2, :])
        return carry

    lax.fori_loop(0, x.shape[0] // 128, norm_rows, 0)
    outs = [
        pltpu.make_async_copy(buf, ref, out_sem.at[i])
        for i, (buf, ref) in enumerate(
            ((thb, th), (tlb, tl), (chb, ch), (clb, cl), (ohb, oh), (olb, ol))
        )
    ]
    own_out.wait()
    wait_bytes(w, own_recv)

    def wide(t):
        return pl.ds(pl.multiple_of(column(t) * 2 * CHUNK, 2 * CHUNK), 2 * CHUNK)

    def q_out(t):
        return pltpu.make_async_copy(qkvb.at[:, wide(t)], qkv.at[:, wide(t)], q_sem.at[t])

    def attend_rows(a):
        head, start = a // 2, a % 2 * 512
        at = pl.ds(pl.multiple_of(start, 512), 512)

        def part(kind):
            return pl.ds(pl.multiple_of((kind * HEADS + head) * 256, 256), 256)

        keys = qkvb[:, part(1)]
        qs = qkvb[at, part(0)]
        scores = mm(qs, twice(keys[:, :HEAD_DIM]), NT) + mm(qs, twice(keys[:, HEAD_DIM:]), NT)
        parts = []
        for u in range(512 // UNIT):
            own_set = sets[:, pl.ds(pl.multiple_of(start + u * UNIT, UNIT), UNIT)][:, 0:1]
            cut = scores[u * UNIT : (u + 1) * UNIT]
            parts.append(jnp.where(own_set == sets[...], cut, -1e30))
        scores = jnp.concatenate(parts, axis=0)
        top = jnp.max(scores, axis=-1, keepdims=True)
        p = jnp.exp((scores - top) * SCALE)
        total = jnp.sum(p, axis=-1, keepdims=True)
        ph, plow = split(p)
        vals = qkvb[:, part(2)]
        out = halves_sum(mm(ph, vals) + mm(plow, vals)) / total
        lanes = pl.ds(pl.multiple_of(head * HEAD_DIM, HEAD_DIM), HEAD_DIM)
        ohb[at, lanes], olb[at, lanes] = split(out)
        level = top * SCALE + jnp.log(total)
        for u in range(512 // UNIT):
            tile = jnp.broadcast_to(level[u * UNIT : (u + 1) * UNIT], (UNIT, UNIT))
            lse[head, :, pl.ds(pl.multiple_of(start + u * UNIT, UNIT), UNIT)] = tile.T[0:8]

    def step(s, carry):
        @pl.when(s < chunks)
        def _():
            wait_bytes(w.at[0 : 3 * quarter, 0:CHUNK], z_recv.at[s])
            for k in range(1, 4):
                part = place((z + k) % 4, rep * quarter, quarter, s)
                send(part, part, send_sem, x_recv.at[s], (x_next, rows))
                send(part, part, send_sem, y_recv.at[s], (y_next, rows))

        @pl.when(s + AHEAD < chunks)
        def _():
            start_z(s + AHEAD)

        @pl.when(jnp.logical_and(s >= SPREAD, s < chunks + SPREAD))
        def _():
            t = s - SPREAD
            wait_bytes(w.at[0 : 3 * quarter, 0:CHUNK], x_recv.at[t])
            wait_bytes(w.at[0 : 3 * quarter, 0:CHUNK], y_recv.at[t])
            for k in range(1, 4):
                part = place((z + k) % 4, x_next * quarter, half, t)
                send(part, part, send_sem, fy_recv.at[t], (y_next, rows))
                part = place((z + k) % 4, y_next * quarter + half, half, t)
                send(part, part, send_sem, fx_recv.at[t], (x_next, rows))

        @pl.when(jnp.logical_and(s >= SWAP, s < chunks + SWAP))
        def _():
            t = s - SWAP
            wait_bytes(w.at[0 : 3 * half, 0:CHUNK], fx_recv.at[t])
            wait_bytes(w.at[0 : 3 * half, 0:CHUNK], fy_recv.at[t])
            for k in range(1, 4):
                part = place((z + k) % 4, 0, shard, t)
                send(part, part, core_send, core_recv.at[t], (rep, z * 2 + 1 - c))

        @pl.when(s >= USE)
        def _():
            wait_bytes(full.at[0 : 3 * shard, 0:CHUNK], core_recv.at[s - USE])

        @pl.when(jnp.logical_and(s >= USE, s < proj_chunks + USE))
        def _():
            t = s - USE
            load = pltpu.make_async_copy(full.at[:, cols(t)], wbuf, w_sem)
            load.start()
            load.wait()
            wh, wl = split(wbuf[...])
            kind = t % 3
            at = pl.ds(pl.multiple_of(t // 3 * CHUNK, CHUNK), CHUNK)
            bias = jnp.where(kind == 0, small[2:3, at], jnp.where(kind == 2, small[3:4, at], 0.0))
            qkvb[:, wide(t)] = pair_heads(*split(mm3(hhb[...], hlb[...], wh, wl) + bias))
            q_out(t).start()

        begun, later = s - USE - 3, s - USE - proj_chunks
        a = jnp.where(later < 0, begun // 2, (proj_chunks - 2) // 2 + later)
        due = jnp.logical_or(later >= 0, begun % 2 == 0)

        @pl.when(jnp.logical_and(jnp.logical_and(begun >= 0, due), a < HEADS * 2))
        def _():
            attend_rows(a)

        @pl.when(s == 1)
        def _():
            c_in.wait()

            def split_rows(i, total):
                at = pl.ds(pl.multiple_of(i * 128, 128), 128)
                value = cbuf[at, :]
                chb[at, :], clb[at, :] = split(value)
                return total + col_sum(value)

            gs8[...] = lax.fori_loop(0, cot.shape[0] // 128, split_rows, jnp.zeros((1, D), f32))
            outs[2].start()
            outs[3].start()

        @pl.when(s == 3)
        def _():
            thb[...] = hhb[...].T
            tlb[...] = hlb[...].T
            outs[0].start()
            outs[1].start()

        return carry

    lax.fori_loop(0, chunks + USE, step, 0)
    outs[4].start()
    outs[5].start()
    for t in range(proj_chunks):
        q_out(t).wait()
    for copy in outs:
        copy.wait()
    wait_bytes(full.at[0 : 3 * quarter + 6 * quarter + 6 * half, :], send_sem)
    wait_bytes(full.at[0 : 4 * shard, :], core_send)


def gather(weights, small_params, x, cot, segment_ids):
    shard, width = weights.shape
    t = x.shape[0]
    chunks = width // CHUNK
    hbm = pl.BlockSpec(memory_space=pl.ANY)
    vmem = pl.BlockSpec(memory_space=pltpu.VMEM)
    dma = pltpu.SemaphoreType.DMA
    return pl.pallas_call(
        gather_kernel,
        in_specs=[hbm, vmem, hbm, hbm, vmem],
        out_specs=[hbm, vmem, hbm, hbm, hbm, hbm, vmem, hbm, hbm, hbm, vmem],
        out_shape=[shape_of((8 * shard, width)), shape_of((9, D))]
        + [shape_of((D, t), bf16)] * 2
        + [shape_of((t, D), bf16)] * 2
        + [shape_of((1, D)), shape_of((t, 6 * D), bf16)]
        + [shape_of((t, D), bf16)] * 2
        + [shape_of((HEADS, 8, t))],
        scratch_shapes=[pltpu.VMEM((7,) + small_params.shape, f32), pltpu.VMEM((shard, width), f32)]
        + [pltpu.VMEM((t, D), f32)] * 2
        + [pltpu.VMEM((t, D), bf16)] * 2
        + [pltpu.VMEM((D, t), bf16)] * 2
        + [pltpu.VMEM((t, D), bf16)] * 2
        + [pltpu.VMEM((D, CHUNK), f32), pltpu.VMEM((t, 6 * D), bf16)]
        + [pltpu.VMEM((t, D), bf16)] * 2
        + [dma((7,)), dma((7,)), dma, dma, dma, dma]
        + [dma((chunks,))] * 6
        + [dma((2,)), dma((6,)), dma, dma((3 * D // CHUNK,))],
        compiler_params=pltpu.CompilerParams(
            vmem_limit_bytes=60 * 2**20, collective_id=0, has_side_effects=True
        ),
        cost_estimate=cost(3, 64),
        name="gather",
    )(weights, small_params, x, cot, segment_ids)


def remote(src, dst, sem, recv, device):
    pltpu.make_async_remote_copy(
        src_ref=src, dst_ref=dst, send_sem=sem, recv_sem=recv, device_id=device, device_id_type=MESH
    ).start()


def greet(peers):
    barrier = pltpu.get_barrier_semaphore()
    for peer in peers:
        pl.semaphore_signal(barrier, inc=1, device_id=peer, device_id_type=MESH)
    return lambda: pl.semaphore_wait(barrier, len(peers))


def col_chunk(t):
    return pl.ds(pl.multiple_of(t * CHUNK, CHUNK), CHUNK)


class Summing:
    def __init__(self, bufs, sems):
        self.bufs, self.sems = bufs, sems
        rep, rows = lax.axis_index("rep"), lax.axis_index("rows")
        self.rep, self.px, self.py, self.z, self.c = rep, rep % 2, rep // 2, rows // 2, rows % 2
        self.x_peer = (self.py * 2 + 1 - self.px, rows)
        self.y_peer = ((1 - self.py) * 2 + self.px, rows)

    @staticmethod
    def scratch(chunks):
        buf = lambda *shape: pltpu.VMEM(shape + (16, CHUNK), f32)
        dma = pltpu.SemaphoreType.DMA
        return [
            buf(3, 4, 2, 2, 2, 2),
            buf(chunks, 4, 2, 2, 2),
            buf(chunks, 4, 2),
            buf(chunks, 4, 2),
            buf(chunks, 4),
            buf(chunks, 4),
            buf(chunks, 4, 2),
            buf(chunks, 3, 2),
        ], [dma((3,)), dma] + [dma((chunks,))] * 6

    def free(self, t):
        wait_bytes(self.bufs[0].at[t % 3, :, self.c], self.sems[0].at[t % 3])

    def push(self, t):
        gbuf, core_in = self.bufs[:2]
        to = (self.rep, self.z * 2 + 1 - self.c)
        remote(
            gbuf.at[t % 3, :, 1 - self.c], core_in.at[t], self.sems[0].at[t % 3],
            self.sems[2].at[t], to,
        )

    def halve(self, t):
        gbuf, core_in, a1, b1 = self.bufs[:4]
        _, sent, core_recv, a1_recv, b1_recv = self.sems[:5]
        wait_bytes(core_in.at[t], core_recv.at[t])
        core_in[t] = core_in[t] + gbuf[t % 3, :, self.c]
        remote(core_in.at[t, :, :, 1 - self.px, 0], a1.at[t], sent, a1_recv.at[t], self.x_peer)
        remote(core_in.at[t, :, 1 - self.py, :, 1], b1.at[t], sent, b1_recv.at[t], self.y_peer)

    def quarter(self, t):
        _, core_in, a1, b1, a2, b2 = self.bufs[:6]
        _, sent, _, a1_recv, b1_recv, a2_recv, b2_recv = self.sems[:7]
        wait_bytes(a1.at[t], a1_recv.at[t])
        a1[t] = a1[t] + core_in[t, :, :, self.px, 0]
        remote(a1.at[t, :, 1 - self.py], a2.at[t], sent, a2_recv.at[t], self.y_peer)
        wait_bytes(b1.at[t], b1_recv.at[t])
        b1[t] = b1[t] + core_in[t, :, self.py, :, 1]
        remote(b1.at[t, :, 1 - self.px], b2.at[t], sent, b2_recv.at[t], self.x_peer)

    def along_z(self, t):
        a1, b1, a2, b2, zsrc, z_in = self.bufs[2:]
        _, sent, _, _, _, a2_recv, b2_recv, z_recv = self.sems
        wait_bytes(a2.at[t], a2_recv.at[t])
        zsrc[t, :, 0] = a1[t, :, self.py] + a2[t]
        wait_bytes(b2.at[t], b2_recv.at[t])
        zsrc[t, :, 1] = b1[t, :, self.px] + b2[t]
        for k in range(1, 4):
            to = (self.z + k) % 4
            remote(zsrc.at[t, to], z_in.at[t, k - 1], sent, z_recv.at[t], (self.rep, to * 2 + self.c))

    def z_sum(self, t):
        zsrc, z_in = self.bufs[6:]
        wait_bytes(z_in.at[t], self.sems[7].at[t])
        return (zsrc[t, self.z] + z_in[t, 0]) + (z_in[t, 1] + z_in[t, 2])

    def finish(self):
        a1, b1, a2, b2, _, z_in = self.bufs[2:]

        def sent(t, carry):
            for ref in (a1, b1, a2, b2, z_in):
                wait_bytes(ref.at[t], self.sems[1])
            return carry

        lax.fori_loop(0, a1.shape[0], sent, 0)
        for i in range(3):
            wait_bytes(self.bufs[0].at[i, :, self.c], self.sems[0].at[i])


class Spreading:
    def __init__(self, total, sems, summing):
        self.total, self.sems, self.peers = total, sems, (summing.x_peer, summing.y_peer)
        self.rep = summing.rep

    @staticmethod
    def scratch(chunks):
        dma = pltpu.SemaphoreType.DMA
        return [dma] + [dma((chunks,))] * 4

    def share(self, t, value):
        self.total[t, self.rep] = value
        piece = self.total.at[t, self.rep]
        for recv, peer in zip(self.sems[1:3], self.peers):
            remote(piece, piece, self.sems[0], recv.at[t], peer)

    def forward(self, t):
        x_peer, y_peer = self.peers
        wait_bytes(self.total.at[t, 0], self.sems[1].at[t])
        piece = self.total.at[t, x_peer[0], 0]
        remote(piece, piece, self.sems[0], self.sems[4].at[t], y_peer)
        wait_bytes(self.total.at[t, 0], self.sems[2].at[t])
        piece = self.total.at[t, y_peer[0], 1]
        remote(piece, piece, self.sems[0], self.sems[3].at[t], x_peer)

    def landed(self, t):
        wait_bytes(self.total.at[t, 0, 0], self.sems[3].at[t])
        wait_bytes(self.total.at[t, 0, 0], self.sems[4].at[t])

    def sent(self, t):
        wait_bytes(self.total.at[t, 0:3], self.sems[0])


PUSH = (0, 1, 2, 3, 8, 9, 10, 11, 16, 17, 18, 19)
HALVE = (1, 2, 3, 4, 9, 10, 11, 12, 17, 18, 19, 20)
QUARTER = (4, 5, 7, 8, 10, 11, 12, 16, 20, 21, 23, 24)
ALONG_Z = (7, 8, 9, 10, 12, 14, 16, 19, 23, 24, 26, 27)
Z_SUM = (9, 10, 11, 13, 15, 17, 19, 22, 26, 27, 28, 29)
FORWARD = (11, 12, 13, 15, 17, 19, 21, 24)
FIRST_PUSH = 12


def planned(step, table):
    return sum(jnp.where(step == at, i + 1, 0) for i, at in enumerate(table)) - 1


def mid_kernel(
    oh, ol, x, ch, cl, w, s,
    out, dx1, do, total, part, gs,
    x1, h2h, h2l, uh, ul, acc, chb, clb, dzh, dzl, th, tl, wcol, wrow, *rest,
):
    bufs, sems, (in_sem, w_sem, out_sem) = rest[:8], rest[8:16], rest[16:19]
    summing = Summing(bufs, sems)
    spreading = Spreading(total, rest[19:], summing)
    spread = total.shape[0]
    gbuf = bufs[0]
    rep, rows = lax.axis_index("rep"), lax.axis_index("rows")
    c = rows % 2
    peers = [(rep, (rows // 2 + k) % 4 * 2 + c) for k in range(1, 4)]
    peers += [(rep, rows // 2 * 2 + 1 - c), summing.x_peer, summing.y_peer]
    arrived = greet(peers)

    o_in = [pltpu.make_async_copy(oh, dzh, in_sem.at[0]), pltpu.make_async_copy(ol, dzl, in_sem.at[1])]
    x_in = pltpu.make_async_copy(x, x1, in_sem.at[2])
    c_in = [pltpu.make_async_copy(ch, chb, in_sem.at[3]), pltpu.make_async_copy(cl, clb, in_sem.at[4])]

    def load(g, start):
        for phase, matrix, by_rows in (
            (0, 3, False), (2, 4, False), (4, 5, True), (5, 4, False), (8, 3, True), (9, 5, False),
        ):

            @pl.when(g // 4 == phase)
            def _():
                if by_rows:
                    src = w.at[col_chunk(g % 4), matrix * D : (matrix + 1) * D]
                    copy = pltpu.make_async_copy(src, wrow.at[g % 2], w_sem.at[g % 2])
                else:
                    src = w.at[:, col_chunk(matrix * (D // CHUNK) + g % 4)]
                    copy = pltpu.make_async_copy(src, wcol.at[g % 2], w_sem.at[g % 2])
                copy.start() if start else copy.wait()

    load(0, True)
    for copy in o_in + [x_in] + c_in:
        copy.start()
    arrived()
    for copy in o_in + [x_in]:
        copy.wait()

    def do_out(n, buf):
        target = do.at[:, pl.ds(pl.multiple_of(n * 2 * CHUNK, 2 * CHUNK), 2 * CHUNK)]
        at = pl.ds(pl.multiple_of(n % 2 * 2 * CHUNK, 2 * CHUNK), 2 * CHUNK)
        return pltpu.make_async_copy(buf.at[:, at], target, out_sem.at[8 + n])

    def step(g, carry):
        load(g + 1, True)

        def summed(t):
            value = summing.z_sum(t)

            @pl.when(t < spread)
            def _():
                spreading.share(t, value)

            @pl.when(t >= spread)
            def _():
                part[t - spread] = value

        for table, body in (
            (HALVE, summing.halve),
            (QUARTER, summing.quarter),
            (ALONG_Z, summing.along_z),
            (Z_SUM, summed),
            (FORWARD, spreading.forward),
        ):
            t = planned(g - FIRST_PUSH, table)
            pl.when(t >= 0)(functools.partial(body, t))

        load(g, False)
        n = g % 4
        at = col_chunk(n)

        def phase(p):
            return pl.when(g // 4 == p)

        def gradient(t, high, low):
            @pl.when(t >= 3)
            def _():
                summing.free(t)

            gbuf[t % 3] = mm3(th[...], tl[...], high, low).reshape(gbuf.shape[1:])
            summing.push(t)

        @phase(0)
        def _():
            wh, wl = split(wcol[g % 2])
            x1[:, at] += mm3(dzh[...], dzl[...], wh, wl) + s[4:5, at]

        @phase(1)
        def _():
            normed, _ = norm_parts(x1[at, :])
            h2h[at, :], h2l[at, :] = split(normed * s[5:6, :] + s[6:7, :])

        @phase(2)
        def _():
            wh, wl = split(wcol[g % 2])
            value = mm3(h2h[...], h2l[...], wh, wl) + s[7:8, at]
            square = value * value
            bent = jnp.tanh(ROOT * (value + 0.044715 * value * square))
            high, low = split(0.5 * value * (1.0 + bent))
            uh[:, at], ul[:, at] = high, low
            th[at, :], tl[at, :] = high.T, low.T
            acc[:, at] = 0.5 * (1.0 + bent) + 0.5 * value * (1.0 - bent * bent) * (
                ROOT * (1.0 + 3.0 * 0.044715 * square)
            )

        @phase(3)
        def _():
            @pl.when(n == 0)
            def _():
                for copy in c_in:
                    copy.wait()

            gradient(n, chb[:, at], clb[:, at])

        @phase(4)
        def _():
            wh, wl = split(wrow[g % 2])
            dz = mm3(chb[...], clb[...], wh, wl, NT) * acc[:, at]
            dzh[:, at], dzl[:, at] = split(dz)
            gs[3:4, at] = col_sum(dz)
            th[at, :], tl[at, :] = h2h[:, at].T, h2l[:, at].T

        @phase(5)
        def _():
            @pl.when(n == 0)
            def _():
                acc[...] = jnp.zeros_like(acc)

            gradient(4 + n, dzh[:, at], dzl[:, at])
            wh, wl = split(wcol[g % 2])

            def some_rows(i, done):
                r = col_chunk(i)
                acc[r, :] += mm3(dzh[r, at], dzl[r, at], wh, wl, NT)
                return done

            lax.fori_loop(0, acc.shape[0] // CHUNK, some_rows, 0)

        @phase(6)
        def _():
            @pl.when(n == 0)
            def _():
                gs[0:3, :] = jnp.zeros((3, D), f32)
                for copy in o_in:
                    copy.start()
                for copy in o_in:
                    copy.wait()

            th[at, :], tl[at, :] = dzh[:, at].T, dzl[:, at].T
            dh2 = acc[at, :]
            normed, rstd = norm_parts(x1[at, :])
            cot = chb[at, :].astype(f32) + clb[at, :].astype(f32)
            grad = cot + norm_back(dh2, normed, rstd, s[5:6, :])
            acc[at, :] = grad
            pltpu.make_async_copy(acc.at[at, :], dx1.at[at, :], out_sem.at[n]).start()
            h2h[at, :], h2l[at, :] = split(grad)
            gs[0:1, :] += col_sum(grad)
            gs[1:2, :] += col_sum(dh2 * normed)
            gs[2:3, :] += col_sum(dh2)

        @phase(7)
        def _():
            gradient(8 + n, h2h[:, at], h2l[:, at])

        @phase(8)
        def _():
            wh, wl = split(wrow[g % 2])
            value = pair_heads(*split(mm3(h2h[...], h2l[...], wh, wl, NT)))
            wide = pl.ds(pl.multiple_of(n % 2 * 2 * CHUNK, 2 * CHUNK), 2 * CHUNK)
            for i, buf in enumerate((dzh, dzl)):

                @pl.when(n // 2 == i)
                def _():
                    buf[:, wide] = value
                    do_out(n, buf).start()

        @phase(9)
        def _():
            wh, wl = split(wcol[g % 2])
            x1[:, at] += mm3(uh[...], ul[...], wh, wl) + s[8:9, at]
            pltpu.make_async_copy(x1.at[:, at], out.at[:, at], out_sem.at[4 + n]).start()

        return carry

    lax.fori_loop(0, FIRST_PUSH + Z_SUM[-1] + 1, step, 0)
    for n in range(4):
        at = col_chunk(n)
        pltpu.make_async_copy(acc.at[at, :], dx1.at[at, :], out_sem.at[n]).wait()
        pltpu.make_async_copy(x1.at[:, at], out.at[:, at], out_sem.at[4 + n]).wait()
        do_out(n, (dzh, dzl)[n // 2]).wait()
    summing.finish()
    for t in range(spread):
        spreading.landed(t)
        spreading.sent(t)


def mid(oh, ol, x, ch, cl, full, small):
    t = x.shape[0]
    hbm = pl.BlockSpec(memory_space=pl.ANY)
    vmem = pl.BlockSpec(memory_space=pltpu.VMEM)
    dma = pltpu.SemaphoreType.DMA
    chunks, spread = len(PUSH), len(FORWARD)
    bufs, sems = Summing.scratch(chunks)
    wide, pair = pltpu.VMEM((t, D), f32), [pltpu.VMEM((t, D), bf16)] * 2
    return pl.pallas_call(
        mid_kernel,
        in_specs=[hbm] * 6 + [vmem],
        out_specs=[hbm, hbm, hbm, vmem, vmem, vmem],
        out_shape=[
            shape_of((t, D)),
            shape_of((t, D)),
            shape_of((t, 2 * D), bf16),
            shape_of((spread, 4, 2, 16, CHUNK)),
            shape_of((chunks - spread, 2, 16, CHUNK)),
            shape_of((4, D)),
        ],
        scratch_shapes=[wide, *pair, *pair, wide, *pair, *pair, *pair]
        + [pltpu.VMEM((2, D, CHUNK), f32), pltpu.VMEM((2, CHUNK, D), f32)]
        + bufs
        + sems
        + [dma((5,)), dma((2,)), dma((12,))]
        + Spreading.scratch(spread),
        compiler_params=pltpu.CompilerParams(
            vmem_limit_bytes=60 * 2**20, collective_id=2, has_side_effects=True
        ),
        cost_estimate=cost(9, 60),
        name="mid",
    )(oh, ol, x, ch, cl, full, small)


MAKE = tuple(range(12))
BACK = tuple(range(12, 24))
LAST_HALVE = tuple(range(1, 13))
LAST_QUARTER = (4, 5, 7, 8, 10, 11, 13, 14, 16, 17, 19, 20)
LAST_Z = (7, 8, 10, 11, 13, 14, 16, 17, 19, 20, 22, 23)
LAST_SUM = (10, 11, 13, 14, 16, 17, 19, 20, 22, 23, 25, 26)
LAST_FORWARD = (12, 13, 15, 16, 18, 19, 21, 22, 24, 25, 27, 28)
NORM = 24


def last_kernel(
    th_in, tl_in, dqh, dql, dkh, dkl, dvh, dvl, w, x, dx1, part, earlier, gs2, gs3, gs4567, gs8, small_in,
    out, total, small_total, norm,
    th, tl, dbuf, wbuf, acc, xbuf, dxbuf, spart, srow, srep, norm_in, *rest,
):
    bufs, sems = rest[:8], rest[8:16]
    h_sem, d_in, w_in, ln_in, ln_out, s_send, s_recv, r_send, r_recv, n_send, n_recv = rest[21:]
    summing = Summing(bufs, sems)
    spreading = Spreading(total, rest[16:21], summing)
    gbuf = bufs[0]
    rep, rows = lax.axis_index("rep"), lax.axis_index("rows")
    before, chunks = part.shape[0], bufs[1].shape[0]
    per = D // CHUNK
    t_rows = x.shape[0]
    arrived = greet(
        [(rep, (rows + k) % 8) for k in range(1, 8)] + [((rep + k) % 4, rows) for k in range(1, 4)]
    )

    h_in = [pltpu.make_async_copy(th_in, th, h_sem.at[0]), pltpu.make_async_copy(tl_in, tl, h_sem.at[1])]

    def load(step, start):
        slot = step % 2
        made, back = planned(step, MAKE), planned(step, BACK)
        u = jnp.maximum(made, back)

        def move(copy):
            copy.start() if start else copy.wait()

        for j, (high, low) in enumerate(((dqh, dql), (dkh, dkl), (dvh, dvl))):

            @pl.when(jnp.logical_and(u >= 0, u // per == j))
            def _():
                for i, source in enumerate((high, low)):
                    move(
                        pltpu.make_async_copy(
                            source.at[:, col_chunk(u % per)], dbuf.at[slot, i], d_in.at[slot, i]
                        )
                    )

        @pl.when(back >= 0)
        def _():
            move(pltpu.make_async_copy(w.at[:, col_chunk(back)], wbuf.at[slot], w_in.at[slot]))

        @pl.when(jnp.logical_and(step >= NORM, step < NORM + 4))
        def _():
            at = col_chunk(step - NORM)
            move(pltpu.make_async_copy(x.at[at, :], xbuf.at[slot], ln_in.at[slot, 0]))
            move(pltpu.make_async_copy(dx1.at[at, :], dxbuf.at[slot], ln_in.at[slot, 1]))

    for copy in h_in:
        copy.start()
    load(0, True)
    acc[...] = jnp.zeros_like(acc)
    arrived()
    for t in range(before):
        spreading.share(t, part[t])
    for copy in h_in:
        copy.wait()

    def step(s, carry):
        load(s + 1, True)
        for table, body in (
            (LAST_HALVE, summing.halve),
            (LAST_QUARTER, summing.quarter),
            (LAST_Z, summing.along_z),
            (LAST_SUM, lambda t: spreading.share(before + t, summing.z_sum(t))),
            (LAST_FORWARD, lambda t: spreading.forward(before + t)),
        ):
            t = planned(s, table)
            pl.when(t >= 0)(functools.partial(body, t))

        @pl.when(jnp.logical_and(s >= 2, s < 2 + before))
        def _():
            spreading.forward(s - 2)

        load(s, False)
        made, back = planned(s, MAKE), planned(s, BACK)

        @pl.when(made >= 3)
        def _():
            summing.free(made)

        @pl.when(made >= 0)
        def _():
            grad = mm3(th[...], tl[...], dbuf[s % 2, 0], dbuf[s % 2, 1])
            gbuf[made % 3] = grad.reshape(gbuf.shape[1:])
            summing.push(made)

        @pl.when(back >= 0)
        def _():
            wh, wl = split(wbuf[s % 2])

            def some_rows(i, done):
                at = col_chunk(i)
                acc[at, :] += mm3(dbuf[s % 2, 0, at, :], dbuf[s % 2, 1, at, :], wh, wl, NT)
                return done

            lax.fori_loop(0, t_rows // CHUNK, some_rows, 0)

        @pl.when(jnp.logical_and(s >= NORM, s < NORM + 4))
        def _():
            at = col_chunk(s - NORM)
            dh = acc[at, :]
            normed, rstd = norm_parts(xbuf[s % 2])
            acc[at, :] = dxbuf[s % 2] + norm_back(dh, normed, rstd, small_in[0:1, :])
            pltpu.make_async_copy(acc.at[at, :], out.at[at, :], ln_out.at[s - NORM]).start()
            gs = jnp.concatenate([col_sum(dh * normed), col_sum(dh)], axis=0)
            for j in range(8):
                piece = gs[:, j * 128 : (j + 1) * 128]

                @pl.when(s == NORM)
                def _():
                    spart[j, 0:2] = piece
                    for row, rest_of in ((2, gs2), (3, gs3), (4, gs4567), (8, gs8)):
                        spart[j, row : row + rest_of.shape[0]] = rest_of[:, j * 128 : (j + 1) * 128]

                @pl.when(s > NORM)
                def _():
                    spart[j, 0:2] += piece

        @pl.when(s == NORM + 4)
        def _():
            for k in range(1, 8):
                to = (rows + k) % 8
                remote(spart.at[to], srow.at[k - 1], s_send.at[k - 1], s_recv.at[k - 1], (rep, to))

        @pl.when(s == NORM + 5)
        def _():
            mine = spart[rows]
            for k in range(1, 8):
                wait_bytes(srow.at[k - 1], s_recv.at[k - 1])
                mine = mine + srow[k - 1]
            srep[rep] = mine
            for k in range(1, 4):
                piece = srep.at[rep]
                remote(piece, piece, r_send.at[k - 1], r_recv.at[k - 1], ((rep + k) % 4, rows))

        return carry

    lax.fori_loop(0, NORM + 6, step, 0)
    for k in range(1, 4):
        wait_bytes(srep.at[0], r_recv.at[k - 1])
    small = (srep[0] + srep[1]) + (srep[2] + srep[3])
    small_total[...] = small

    def squares(ref, t):
        value = ref[t].reshape(128, CHUNK)
        return jnp.sum((value * value).reshape(16, 8, CHUNK), axis=0)

    def one_earlier(t, carry):
        return carry + squares(earlier, t)

    def one(t, carry):
        spreading.landed(t)
        return carry + squares(total, t)

    mats = lax.fori_loop(0, earlier.shape[0], one_earlier, jnp.zeros((8, CHUNK), f32))
    mats = lax.fori_loop(0, before + chunks, one, mats)
    mine = jnp.sum(mats) + jnp.sum(small * small)
    norm_in[rows] = jnp.full((8, 128), mine, f32)
    for k in range(1, 8):
        piece = norm_in.at[rows]
        remote(piece, piece, n_send.at[k - 1], n_recv.at[k - 1], (rep, (rows + k) % 8))
    for k in range(1, 8):
        wait_bytes(norm_in.at[0], n_recv.at[k - 1])
    value = norm_in[0]
    for j in range(1, 8):
        value = value + norm_in[j]
    norm[...] = jnp.sqrt(value)

    summing.finish()
    for i in range(4):
        at = pl.ds(i * CHUNK, CHUNK)
        pltpu.make_async_copy(acc.at[at, :], out.at[at, :], ln_out.at[i]).wait()

    def sent(t, carry):
        spreading.sent(t)
        return carry

    lax.fori_loop(0, before + chunks, sent, 0)
    for k in range(1, 8):
        wait_bytes(srow.at[k - 1], s_send.at[k - 1])
        wait_bytes(norm_in.at[0], n_send.at[k - 1])
    for k in range(1, 4):
        wait_bytes(srep.at[0], r_send.at[k - 1])


def last(th, tl, grads, full, x, dx1, part, earlier, gs, small):
    t = x.shape[0]
    chunks = 3 * D // CHUNK
    every = chunks + part.shape[0]
    hbm = pl.BlockSpec(memory_space=pl.ANY)
    vmem = pl.BlockSpec(memory_space=pltpu.VMEM)
    dma = pltpu.SemaphoreType.DMA
    bufs, sems = Summing.scratch(chunks)
    return pl.pallas_call(
        last_kernel,
        in_specs=[hbm] * 11 + [vmem] * 7,
        out_specs=[hbm, vmem, vmem, vmem],
        out_shape=[
            shape_of((t, D)),
            shape_of((every, 4, 2, 16, CHUNK)),
            shape_of((9, 128)),
            shape_of((8, 128)),
        ],
        scratch_shapes=[
            pltpu.VMEM((D, t), bf16),
            pltpu.VMEM((D, t), bf16),
            pltpu.VMEM((2, 2, t, CHUNK), bf16),
            pltpu.VMEM((2, D, CHUNK), f32),
            pltpu.VMEM((t, D), f32),
            pltpu.VMEM((2, CHUNK, D), f32),
            pltpu.VMEM((2, CHUNK, D), f32),
            pltpu.VMEM((8, 9, 128), f32),
            pltpu.VMEM((7, 9, 128), f32),
            pltpu.VMEM((4, 9, 128), f32),
            pltpu.VMEM((8, 8, 128), f32),
        ]
        + bufs
        + sems
        + Spreading.scratch(every)
        + [dma((2,)), dma((2, 2)), dma((2,)), dma((2, 2)), dma((4,))]
        + [dma((7,)), dma((7,)), dma((3,)), dma((3,)), dma((7,)), dma((7,))],
        compiler_params=pltpu.CompilerParams(
            vmem_limit_bytes=60 * 2**20, collective_id=1, has_side_effects=True
        ),
        cost_estimate=cost(6, 90),
        name="last",
    )(th, tl, *grads, full, x, dx1, part, earlier, *gs, small)


def adam_step(parameter, gradient, first_moment, second_moment, average):
    first_new = 0.9 * first_moment + 0.1 * gradient
    second_new = 0.999 * second_moment + 0.001 * gradient * gradient
    first_hat = first_new / (1.0 - 0.9**STEP)
    second_hat = second_new / (1.0 - 0.999**STEP)
    parameter_new = parameter - 0.05 * (
        first_hat / (jnp.sqrt(second_hat) + 1e-08) + 0.05 * parameter
    )
    average_new = 0.99 * average + 0.01 * parameter_new
    return (parameter_new, first_new, second_new, average_new)


CLIP = 0.25 * math.sqrt(6 * D * D + 9 * D)


def adam_kernel(
    grad_a, grad_b, norm, w, first, second, average, gs, p_s, first_s, second_s, average_s,
    clipped, new_w, first_o, second_o, average_o, low,
    clipped_so, new_so, first_so, second_so, average_so, low_so, norm_out,
):
    norm_out[0] = jnp.max(norm[...])
    factor = jnp.minimum(1.0, CLIP / norm[0:1, 0:1])
    early = pl.program_id(0) < 2
    for j in range(D // CHUNK):
        at = slice(j * CHUNK, (j + 1) * CHUNK)
        value = jnp.where(early, grad_a[j], grad_b[j]).reshape(w.shape[0], CHUNK) * factor
        clipped[:, at] = value
        news = adam_step(w[:, at], value, first[:, at], second[:, at], average[:, at])
        for ref, new in zip((new_w, first_o, second_o, average_o), news):
            ref[:, at] = new
        low[:, at] = news[0].astype(bf16)

    @pl.when(pl.program_id(0) == 0)
    def _():
        value = gs[...] * factor
        clipped_so[...] = value
        news = adam_step(p_s[...], value, first_s[...], second_s[...], average_s[...])
        for ref, new in zip((new_so, first_so, second_so, average_so), news):
            ref[...] = new
        low_so[...] = news[0].astype(bf16)


def adam(earlier, total, norm, mats, gs, smalls):
    shard, width = mats[0].shape
    block = pl.BlockSpec((shard, D), lambda i: (0, jnp.where(i < 3, 5 - i, i - 3)))
    cut = (D // CHUNK,) + total.shape[1:]
    grads = [
        pl.BlockSpec(cut, lambda i: (jnp.minimum(i, 1), 0, 0, 0, 0)),
        pl.BlockSpec(cut, lambda i: (jnp.maximum(i - 2, 0), 0, 0, 0, 0)),
    ]
    small = whole(gs.shape)
    return pl.pallas_call(
        adam_kernel,
        grid=(width // D,),
        in_specs=grads + [whole(norm.shape)] + [block] * 4 + [small] * 5,
        out_specs=[block] * 6 + [small] * 6 + [pl.BlockSpec(memory_space=pltpu.SMEM)],
        out_shape=[shape_of((shard, width))] * 5
        + [shape_of((shard, width), bf16)]
        + [shape_of(gs.shape)] * 5
        + [shape_of(gs.shape, bf16), shape_of((1,))],
        compiler_params=params(),
        cost_estimate=cost(0, 32),
        name="adam",
    )(earlier, total, norm, *mats, gs, *smalls)


def split_once(w, wh, wl):
    @pl.when(pl.program_id(0) == 0)
    def _():
        wh[...], wl[...] = split(w[...])


def out_proj_kernel(oh, ol, w, x, s, x1, h2h, h2l, wh, wl):
    split_once(w, wh, wl)
    value = x[...] + mm3(oh[...], ol[...], wh[...], wl[...]) + s[4:5]
    x1[...] = value
    normed, _ = norm_parts(value)
    h2h[...], h2l[...] = split(normed * s[5:6] + s[6:7])


def out_proj(oh, ol, w, x, small, bm=256):
    t = x.shape[0]
    return pl.pallas_call(
        out_proj_kernel,
        grid=(t // bm,),
        in_specs=[rows_of(bm, D)] * 2 + [matrix(3), rows_of(bm, D), whole((9, D))],
        out_specs=[rows_of(bm, D)] * 3,
        out_shape=[shape_of((t, D)), shape_of((t, D), bf16), shape_of((t, D), bf16)],
        scratch_shapes=[pltpu.VMEM((D, D), bf16)] * 2,
        compiler_params=params(),
        cost_estimate=cost(1, 20),
        name="out_proj",
    )(oh, ol, w, x, small)


def up_kernel(hh, hl, w, s, z, uh, ul):
    wh, wl = split(w[...])
    value = mm3(hh[...], hl[...], wh, wl) + s[7:8]
    z[...] = value
    bent = jnp.tanh(ROOT * (value + 0.044715 * value * value * value))
    uh[...], ul[...] = split(0.5 * value * (1.0 + bent))


def up(hh, hl, w, small, bn=256):
    t = hh.shape[0]
    return pl.pallas_call(
        up_kernel,
        grid=(FF // bn,),
        in_specs=[whole((t, D))] * 2 + [cols_of(D, bn, 4 * D // bn), cols_of(9, bn)],
        out_specs=[cols_of(t, bn)] * 3,
        out_shape=[shape_of((t, FF)), shape_of((t, FF), bf16), shape_of((t, FF), bf16)],
        compiler_params=params(),
        cost_estimate=cost(1, 16),
        name="up",
    )(hh, hl, w, small)


def down_kernel(uh, ul, w, x1, s, out):
    wh, wl = split(w[...])
    out[...] = x1[...] + mm3(uh[...], ul[...], wh, wl) + s[8:9]


def down(uh, ul, w, x1, small, bn=256):
    t = uh.shape[0]
    return pl.pallas_call(
        down_kernel,
        grid=(D // bn,),
        in_specs=[whole((t, FF))] * 2
        + [cols_of(FF, bn, 5 * D // bn), cols_of(t, bn), cols_of(9, bn)],
        out_specs=cols_of(t, bn),
        out_shape=shape_of((t, D)),
        compiler_params=params(),
        cost_estimate=cost(1, 16),
        name="down",
    )(uh, ul, w, x1, small)


def outer_kernel(ah, al, dh, dl, out, th, tl):
    @pl.when(pl.program_id(0) == 0)
    def _():
        th[...] = ah[...].T
        tl[...] = al[...].T

    out[...] = mm3(th[...], tl[...], dh[...], dl[...])


def outer(ah, al, dh, dl, bn=256):
    t, m = ah.shape
    n = dh.shape[1]
    return pl.pallas_call(
        outer_kernel,
        grid=(n // bn,),
        in_specs=[whole((t, m))] * 2 + [cols_of(t, bn)] * 2,
        out_specs=cols_of(m, bn),
        out_shape=shape_of((m, n)),
        scratch_shapes=[pltpu.VMEM((m, t), bf16)] * 2,
        compiler_params=params(),
        cost_estimate=cost(1, 12),
        name="outer",
    )(ah, al, dh, dl)


def down_back_kernel(ch, cl, w, z, dzh, dzl, gs7):
    wh, wl = split(w[...])
    du = mm3(ch[...], cl[...], wh, wl, NT)
    value = z[...]
    square = value * value
    bent = jnp.tanh(ROOT * (value + 0.044715 * value * square))
    slope = 0.5 * (1.0 + bent) + 0.5 * value * (1.0 - bent * bent) * (
        ROOT * (1.0 + 3.0 * 0.044715 * square)
    )
    dz = du * slope
    dzh[...], dzl[...] = split(dz)
    gs7[...] = col_sum(dz)


def down_back(ch, cl, w, z, bn=256):
    t = ch.shape[0]
    return pl.pallas_call(
        down_back_kernel,
        grid=(FF // bn,),
        in_specs=[whole((t, D))] * 2 + [rows_of(bn, D, 5), cols_of(t, bn)],
        out_specs=[cols_of(t, bn)] * 2 + [cols_of(1, bn)],
        out_shape=[shape_of((t, FF), bf16)] * 2 + [shape_of((1, FF))],
        compiler_params=params(),
        cost_estimate=cost(1, 16),
        name="down_back",
    )(ch, cl, w, z)


def up_back_kernel(dzh, dzl, w, x1, cot, s, dx1, dxh, dxl, gs4, gs5, gs6, wh, wl):
    split_once(w, wh, wl)
    dh2 = mm3(dzh[...], dzl[...], wh[...], wl[...], NT)
    normed, rstd = norm_parts(x1[...])
    grad = cot[...] + norm_back(dh2, normed, rstd, s[5:6])
    dx1[...] = grad
    dxh[...], dxl[...] = split(grad)
    add_up(gs4, col_sum(grad))
    add_up(gs5, col_sum(dh2 * normed))
    add_up(gs6, col_sum(dh2))


def up_back(dzh, dzl, w, x1, cot, small, bm=256):
    t = x1.shape[0]
    return pl.pallas_call(
        up_back_kernel,
        grid=(t // bm,),
        in_specs=[rows_of(bm, FF)] * 2 + [matrix(4)] + [rows_of(bm, D)] * 2 + [whole((9, D))],
        out_specs=[rows_of(bm, D)] * 3 + [whole((1, D))] * 3,
        out_shape=[shape_of((t, D)), shape_of((t, D), bf16), shape_of((t, D), bf16)]
        + [shape_of((1, D))] * 3,
        scratch_shapes=[pltpu.VMEM((D, FF), bf16)] * 2,
        compiler_params=params(),
        cost_estimate=cost(1, 24),
        name="up_back",
    )(dzh, dzl, w, x1, cot, small)


def out_proj_back_kernel(dxh, dxl, w, do):
    wh, wl = split(w[...])
    do[...] = pair_heads(*split(mm3(dxh[...], dxl[...], wh, wl, NT)))


def out_proj_back(dxh, dxl, w, bn=256):
    t = dxh.shape[0]
    return pl.pallas_call(
        out_proj_back_kernel,
        grid=(D // bn,),
        in_specs=[whole((t, D))] * 2 + [rows_of(bn, D, 3)],
        out_specs=cols_of(t, 2 * bn),
        out_shape=shape_of((t, 2 * D), bf16),
        compiler_params=params(),
        cost_estimate=cost(1, 12),
        name="out_proj_back",
    )(dxh, dxl, w)


def proj_back_kernel(
    dqh, dql, dkh, dkl, dvh, dvl, wq, wk, wv, x, dx1, s, out, gs0, gs1, wh, wl
):
    @pl.when(pl.program_id(0) == 0)
    def _():
        for j, w in enumerate((wq, wk, wv)):
            wh[j], wl[j] = split(w[...])

    dh = mm3(dqh[...], dql[...], wh[0], wl[0], NT)
    dh += mm3(dkh[...], dkl[...], wh[1], wl[1], NT)
    dh += mm3(dvh[...], dvl[...], wh[2], wl[2], NT)
    normed, rstd = norm_parts(x[...])
    out[...] = dx1[...] + norm_back(dh, normed, rstd, s[0:1])
    add_up(gs0, col_sum(dh * normed))
    add_up(gs1, col_sum(dh))


def proj_back(grads, w, x, dx1, small, bm=256):
    t = x.shape[0]
    return pl.pallas_call(
        proj_back_kernel,
        grid=(t // bm,),
        in_specs=[rows_of(bm, D)] * 6 + [matrix(j) for j in range(3)] + [rows_of(bm, D)] * 2 + [whole((9, D))],
        out_specs=[rows_of(bm, D)] + [whole((1, D))] * 2,
        out_shape=[shape_of((t, D))] + [shape_of((1, D))] * 2,
        scratch_shapes=[pltpu.VMEM((3, D, D), bf16)] * 2,
        compiler_params=params(),
        cost_estimate=cost(3, 36),
        name="proj_back",
    )(*grads, w, w, w, x, dx1, small)


def set_bounds(segment_ids):
    ids = segment_ids[0, ::UNIT]
    order, sets = (ids - ids[0])[None, :], jnp.arange(SETS, dtype=jnp.int32)[:, None]
    lengths = jnp.sum((order == sets).astype(jnp.int32), axis=1)
    firsts = jnp.sum((order < sets).astype(jnp.int32), axis=1)
    return jnp.stack([firsts, lengths], axis=1).reshape(-1).astype(jnp.int32)


def shards(
    reps,
    latents,
    cotangent,
    segment_ids,
    weights,
    small_params,
    first_mats,
    second_mats,
    average_mats,
    first_small,
    second_small,
    average_small,
):
    segs = set_bounds(segment_ids)
    x, cot = latents[0], cotangent[0]
    fast = reps == 4 and weights.shape[0] * 8 == D and x.shape[0] == D
    if fast:
        full, small, th, tl, ch, cl, gs8, qkv, oh, ol, lse = gather(
            weights, small_params, x, cot, segment_ids
        )
    else:
        full, small = (
            lax.all_gather(weights, "rows", axis=0, tiled=True),
            lax.all_gather(small_params, "rows", axis=1, tiled=True),
        )
        bias = jnp.concatenate([small[2], jnp.zeros((D,), f32), small[3]])[None]
        hh, hl, ch, cl, gs8 = prep(x, cot, small)
        qkv = proj(hh, hl, full, bias)
        oh, ol, lse = attend(segs, qkv)
    if fast:
        output, dx1, do, earlier, part, gs4567 = mid(oh, ol, x, ch, cl, full, small)
    else:
        x1, h2h, h2l = out_proj(oh, ol, full, x, small)
        z, uh, ul = up(h2h, h2l, full, small)
        output = down(uh, ul, full, x1, small)
        g_down = outer(uh, ul, ch, cl)
        dzh, dzl, gs7 = down_back(ch, cl, full, z)
        g_up = outer(h2h, h2l, dzh, dzl)
        dx1, dxh, dxl, gs4, gs5, gs6 = up_back(dzh, dzl, full, x1, cot, small)
        g_out = outer(oh, ol, dxh, dxl)
        do = out_proj_back(dxh, dxl, full)
        gs4567 = jnp.concatenate([gs4, gs5, gs6, gs7], axis=0)
    *grads, gs2, gs3 = attend_back(segs, qkv, do, oh, ol, lse)
    gs_rest = (gs2, gs3, gs4567, gs8)
    if fast:
        token_grad, total, small_total, norm = last(
            th, tl, grads, full, x, dx1, part, earlier, gs_rest, small
        )
        (
            clipped_mats, new_weights, first_mats_out, second_mats_out, average_mats_out, low_mats,
            clipped_small, new_small, first_small_out, second_small_out, average_small_out, low_small,
            norm,
        ) = adam(
            earlier, total, norm, (weights, first_mats, second_mats, average_mats), small_total,
            (small_params, first_small, second_small, average_small),
        )
    else:
        g_qkv = [outer(hh, hl, grads[2 * j], grads[2 * j + 1]) for j in range(3)]
        token_grad, gs0, gs1 = proj_back(grads, full, x, dx1, small)
        weight_grad = jnp.concatenate(g_qkv + [g_out, g_up, g_down], axis=1)
        small_grad = jnp.concatenate([gs0, gs1, *gs_rest], axis=0)
        part_weights, part_small = (
            lax.psum_scatter(weight_grad, "rows", scatter_dimension=0, tiled=True),
            lax.psum_scatter(small_grad, "rows", scatter_dimension=1, tiled=True),
        )
        sum_weights, sum_small = lax.psum((part_weights, part_small), "rep")
        squares = lax.psum(
            jnp.sum(sum_weights * sum_weights) + jnp.sum(sum_small * sum_small), "rows"
        )
        norm = jnp.sqrt(squares).reshape(1)
        factor = jnp.minimum(1.0, CLIP / norm[0])
        clipped_mats = sum_weights * factor
        clipped_small = sum_small * factor
        new_weights, first_mats_out, second_mats_out, average_mats_out = adam_step(
            weights, clipped_mats, first_mats, second_mats, average_mats
        )
        new_small, first_small_out, second_small_out, average_small_out = adam_step(
            small_params, clipped_small, first_small, second_small, average_small
        )
        low_mats, low_small = new_weights.astype(bf16), new_small.astype(bf16)
    return (
        output[None],
        token_grad[None],
        norm,
        clipped_mats,
        clipped_small,
        new_weights,
        new_small,
        first_mats_out,
        second_mats_out,
        average_mats_out,
        first_small_out,
        second_small_out,
        average_small_out,
        low_mats,
        low_small,
    )


def solution(mesh):
    tokens, mats, small = P("rep", "rows", None), P("rows", None), P(None, "rows")
    in_specs = (tokens, tokens, P("rep", "rows")) + (mats, small) + (mats,) * 3 + (small,) * 3
    out_specs = (
        (tokens, tokens, P(), mats, small, mats, small) + (mats,) * 3 + (small,) * 3 + (mats, small)
    )
    step = functools.partial(shards, mesh.shape["rep"])
    return jax.shard_map(step, mesh=mesh, in_specs=in_specs, out_specs=out_specs, check_vma=False)
```

```python
import functools
import math

import jax
import jax.numpy as jnp
from jax import lax
from jax.experimental import pallas as pl
from jax.experimental.pallas import tpu as pltpu
from jax.sharding import PartitionSpec as P

D = 1024
HEADS = 8
HEAD_DIM = 128
FF = 1024
UNIT = 128
SETS = 3
STEP = 5
SCALE = HEAD_DIM ** (-0.5)
SCALE2 = SCALE / math.log(2.0)
ROOT = math.sqrt(2.0 / math.pi)

f32 = jnp.float32
bf16 = jnp.bfloat16

NN = (((1,), (0,)), ((), ()))
NT = (((1,), (1,)), ((), ()))
TN = (((0,), (0,)), ((), ()))


def params(mib=56):
    return pltpu.CompilerParams(
        vmem_limit_bytes=mib * 2**20, dimension_semantics=("arbitrary",)
    )


def mm(a, b, dims=NN):
    return lax.dot_general(a, b, dims, preferred_element_type=f32)


def split(x):
    high = x.astype(bf16)
    return high, (x - high.astype(f32)).astype(bf16)


def mm3(ah, al, bh, bl, dims=NN):
    return mm(ah, bh, dims) + (mm(al, bh, dims) + mm(ah, bl, dims))


def cost(products, mib):
    return pl.CostEstimate(
        flops=int(products * 3 * 2 * 1024**3), bytes_accessed=int(mib * 2**20), transcendentals=0
    )


def whole(shape):
    return pl.BlockSpec(shape, lambda *i: (0,) * len(shape))


def rows_of(bm, n, column=0):
    return pl.BlockSpec((bm, n), lambda i, *_: (i, column))


def matrix(j):
    return pl.BlockSpec((D, D), lambda i: (0, j), pipeline_mode=pl.Buffered(1))


def cols_of(m, bn, first=0):
    return pl.BlockSpec((m, bn), lambda i, *_: (0, first + i))


def shape_of(shape, dtype=f32):
    return jax.ShapeDtypeStruct(shape, dtype)


def norm_parts(x):
    center = x - jnp.mean(x, axis=-1, keepdims=True)
    rstd = lax.rsqrt(jnp.mean(center * center, axis=-1, keepdims=True) + 1e-05)
    return center * rstd, rstd


def norm_back(grad, normed, rstd, gain):
    scaled = grad * gain
    return rstd * (
        scaled
        - jnp.mean(scaled, axis=-1, keepdims=True)
        - normed * jnp.mean(scaled * normed, axis=-1, keepdims=True)
    )


def col_sum(x):
    return jnp.sum(x, axis=0, keepdims=True)


def add_up(ref, value):
    first = pl.program_id(0) == 0

    @pl.when(first)
    def _():
        ref[...] = value

    @pl.when(jnp.logical_not(first))
    def _():
        ref[...] += value


def prep_kernel(x, cot, s, hh, hl, ch, cl, gs8):
    normed, _ = norm_parts(x[...])
    hh[...], hl[...] = split(normed * s[0:1] + s[1:2])
    ch[...], cl[...] = split(cot[...])
    add_up(gs8, col_sum(cot[...]))


def prep(x, cot, small, bm=256):
    t = x.shape[0]
    return pl.pallas_call(
        prep_kernel,
        grid=(t // bm,),
        in_specs=[rows_of(bm, D), rows_of(bm, D), whole((9, D))],
        out_specs=[rows_of(bm, D)] * 4 + [whole((1, D))],
        out_shape=[shape_of((t, D), bf16)] * 4 + [shape_of((1, D))],
        compiler_params=params(),
        cost_estimate=cost(0, 16),
        name="prep",
    )(x, cot, small)


def pair_heads(high, low):
    parts = []
    for head in range(high.shape[1] // HEAD_DIM):
        cut = slice(head * HEAD_DIM, (head + 1) * HEAD_DIM)
        parts += [high[:, cut], low[:, cut]]
    return jnp.concatenate(parts, axis=1)


def proj_kernel(hh, hl, w, bias, out):
    wh, wl = split(w[...])
    out[...] = pair_heads(*split(mm3(hh[...], hl[...], wh, wl) + bias[...]))


def proj(hh, hl, w, bias, bn=256):
    t, n = hh.shape[0], bias.shape[1]
    return pl.pallas_call(
        proj_kernel,
        grid=(n // bn,),
        in_specs=[whole((t, D))] * 2 + [cols_of(D, bn), cols_of(1, bn)],
        out_specs=cols_of(t, 2 * bn),
        out_shape=shape_of((t, 2 * n), bf16),
        compiler_params=params(),
        cost_estimate=cost(n // D, 8 * (n // D) + 4),
        name="proj",
    )(hh, hl, w, bias)


def twice(a):
    return jnp.concatenate([a, a], axis=1)


def halves_sum(x):
    return x[:, :HEAD_DIM] + x[:, HEAD_DIM:]


def pieces(n):
    out, at = [], 0
    while at < n:
        size = min(256, n - at)
        out.append((at, size))
        at += size
    return out


def for_sets(segs, units, body):
    def one(i, carry):
        first, length = segs[2 * i], segs[2 * i + 1]
        for count in range(1, units - SETS + 2):

            @pl.when(length == count)
            def _():
                body(pl.multiple_of(first * UNIT, UNIT), count * UNIT)

        return carry

    lax.fori_loop(0, SETS, one, 0)


def attend_kernel(segs, q, k, v, oh, ol, lse):
    units = q.shape[0] // UNIT

    def body(first, n):
        rows = pl.ds(first, n)
        keys = k[rows, :]
        kh, kl = twice(keys[:, :HEAD_DIM]), twice(keys[:, HEAD_DIM:])
        vals = v[rows, :]
        for at, size in pieces(n):
            sub = pl.ds(pl.multiple_of(first + at, UNIT), size)
            qs = q[sub, :]
            scores = mm(qs, kh, NT) + mm(qs, kl, NT)
            top = jnp.max(scores, axis=-1, keepdims=True)
            p = jnp.exp2((scores - top) * SCALE2)
            total = jnp.sum(p, axis=-1, keepdims=True)
            ph, plow = split(p)
            o = halves_sum(mm(ph, vals) + mm(plow, vals)) / total
            oh[sub, :], ol[sub, :] = split(o)
            level = top * SCALE2 + jnp.log2(total)
            for u in range(size // UNIT):
                tile = jnp.broadcast_to(level[u * UNIT : (u + 1) * UNIT], (UNIT, UNIT))
                lse[0, :, pl.ds(pl.multiple_of(first + at + u * UNIT, UNIT), UNIT)] = tile.T[0:8]

    for_sets(segs, units, body)


def attend(segs, qkv):
    t = qkv.shape[0]
    head = lambda first: pl.BlockSpec((t, 2 * HEAD_DIM), lambda i, *_: (0, first + i))
    return pl.pallas_call(
        attend_kernel,
        grid_spec=pltpu.PrefetchScalarGridSpec(
            num_scalar_prefetch=1,
            grid=(HEADS,),
            in_specs=[head(0), head(HEADS), head(2 * HEADS)],
            out_specs=[cols_of(t, HEAD_DIM)] * 2
            + [pl.BlockSpec((1, 8, t), lambda i, *_: (i, 0, 0))],
        ),
        out_shape=[shape_of((t, D), bf16)] * 2 + [shape_of((HEADS, 8, t))],
        compiler_params=params(),
        cost_estimate=cost(2, 16),
        name="attend",
    )(segs, qkv, qkv, qkv)


def attend_back_kernel(
    segs, q, k, v, do, oh, ol, lse, done, dqh, dql, dkh, dkl, dvh, dvl, gq, gv, done_out, drow, qsum, vsum
):
    units = q.shape[0] // UNIT
    for u in range(units):
        cut = slice(u * UNIT, (u + 1) * UNIT)
        grad = do[cut, :].astype(f32)
        out = oh[cut, :].astype(f32) + ol[cut, :].astype(f32)
        tile = (halves_sum(grad) * out).T
        drow[:, cut] = jnp.broadcast_to(col_sum(tile), (8, UNIT))
    done_out[...] = done[...]
    qsum[...] = jnp.zeros_like(qsum)
    vsum[...] = jnp.zeros_like(vsum)

    def body(first, n):
        rows = pl.ds(first, n)
        keys, vals = k[rows, :], v[rows, :]
        dk = dv = None
        for at, size in pieces(n):
            sub = pl.ds(pl.multiple_of(first + at, UNIT), size)
            qs, grad = q[sub, :], do[sub, :]
            scores = mm(keys, twice(qs[:, :HEAD_DIM]), NT) + mm(keys, twice(qs[:, HEAD_DIM:]), NT)
            p = jnp.exp2(scores * SCALE2 - lse[0, 0:1, sub])
            dp = mm(vals, twice(grad[:, :HEAD_DIM]), NT) + mm(vals, twice(grad[:, HEAD_DIM:]), NT)
            ds = p * (dp - drow[0:1, sub])
            ph, plow = split(p)
            dsh, dsl = split(ds)
            dv_part = mm(ph, grad) + mm(plow, grad)
            dk_part = mm(dsh, qs) + mm(dsl, qs)
            dv = dv_part if dv is None else dv + dv_part
            dk = dk_part if dk is None else dk + dk_part
            dq = halves_sum(mm(dsh, keys, TN) + mm(dsl, keys, TN)) * SCALE
            dqh[sub, :], dql[sub, :] = split(dq)
            qsum[0:1, :] += col_sum(dq)
        dk = halves_sum(dk) * SCALE
        dv = halves_sum(dv)
        dkh[rows, :], dkl[rows, :] = split(dk)
        dvh[rows, :], dvl[rows, :] = split(dv)
        vsum[0:1, :] += col_sum(dv)

    for_sets(segs, units, body)
    gq[...] = qsum[0:1, :]
    gv[...] = vsum[0:1, :]


def attend_back(segs, qkv, do, oh, ol, lse, done):
    t = qkv.shape[0]
    head = lambda first: pl.BlockSpec((t, 2 * HEAD_DIM), lambda i, *_: (0, first + i))
    return pl.pallas_call(
        attend_back_kernel,
        grid_spec=pltpu.PrefetchScalarGridSpec(
            num_scalar_prefetch=1,
            grid=(HEADS,),
            in_specs=[head(0), head(HEADS), head(2 * HEADS), head(0)]
            + [cols_of(t, HEAD_DIM)] * 2
            + [pl.BlockSpec((1, 8, t), lambda i, *_: (i, 0, 0)), rows_of(t // HEADS, D)],
            out_specs=[cols_of(t, HEAD_DIM)] * 6
            + [cols_of(1, HEAD_DIM)] * 2
            + [rows_of(t // HEADS, D)],
            scratch_shapes=[
                pltpu.VMEM((8, t), f32),
                pltpu.VMEM((8, HEAD_DIM), f32),
                pltpu.VMEM((8, HEAD_DIM), f32),
            ],
        ),
        out_shape=[shape_of((t, D), bf16)] * 6 + [shape_of((1, D))] * 2 + [shape_of((t, D))],
        compiler_params=params(),
        cost_estimate=cost(5, 36),
        name="attend_back",
    )(segs, qkv, qkv, qkv, do, oh, ol, lse, done)


MESH = pl.DeviceIdType.MESH
CHUNK = 256
AHEAD, SPREAD, SWAP, USE = 4, 2, 5, 7


def wait_bytes(ref, sem):
    pltpu.make_async_copy(ref, ref, sem).wait()


def gather_kernel(
    w, own_small, x, cot, sets,
    full, small, th, tl, ch, cl, gs8, qkv, oh, ol, lse,
    pieces, own, xbuf, cbuf, hhb, hlb, thb, tlb, chb, clb, wbuf, qkvb, ohb, olb,
    small_send, small_recv, own_sem, send_sem, core_send, own_recv,
    z_recv, x_recv, y_recv, fx_recv, fy_recv, core_recv, in_sem, out_sem, w_sem, q_sem,
):
    rep, rows = lax.axis_index("rep"), lax.axis_index("rows")
    z, c = rows // 2, rows % 2
    x_next, y_next = rep // 2 * 2 + (1 - rep % 2), (1 - rep // 2) * 2 + rep % 2
    shard = w.shape[0]
    quarter, half = shard // 4, shard // 8
    chunks = w.shape[1] // CHUNK
    proj_chunks = 3 * D // CHUNK
    per = D // CHUNK

    x_in = pltpu.make_async_copy(x, xbuf, in_sem.at[0])
    c_in = pltpu.make_async_copy(cot, cbuf, in_sem.at[1])
    x_in.start()
    c_in.start()
    own_in = pltpu.make_async_copy(w, own, own_sem)
    own_in.start()

    barrier = pltpu.get_barrier_semaphore()
    peers = [(rep, (rows + k) % 8) for k in range(1, 8)] + [(x_next, rows), (y_next, rows)]
    for peer in peers:
        pl.semaphore_signal(barrier, inc=1, device_id=peer, device_id_type=MESH)
    pl.semaphore_wait(barrier, len(peers))

    def send(src, dst, sem, recv, device):
        pltpu.make_async_remote_copy(
            src_ref=src, dst_ref=dst, send_sem=sem, recv_sem=recv, device_id=device,
            device_id_type=MESH,
        ).start()

    for k in range(1, 8):
        send(own_small, pieces.at[k - 1], small_send.at[k - 1], small_recv.at[k - 1], (rep, (rows + k) % 8))

    def column(t):
        return jnp.where(t < proj_chunks, t % 3 * per + t // 3, t)

    def cols(t):
        return pl.ds(pl.multiple_of(column(t) * CHUNK, CHUNK), CHUNK)

    def place(zz, first, count, t):
        at = (zz * 2 + c) * shard + first
        return full.at[pl.ds(pl.multiple_of(at, half), count), cols(t)]

    def start_z(t):
        src = w.at[pl.ds(pl.multiple_of(rep * quarter, quarter), quarter), cols(t)]
        for k in range(1, 4):
            send(src, place(z, rep * quarter, quarter, t), send_sem, z_recv.at[t], (rep, (z + k) % 4 * 2 + c))

    for t in range(AHEAD):
        start_z(t)
    send(w, full.at[pl.ds(rows * shard, shard), :], core_send, own_recv, (rep, z * 2 + 1 - c))

    for k in range(1, 8):
        pltpu.make_async_copy(own_small, pieces.at[k - 1], small_recv.at[k - 1]).wait()
        pltpu.make_async_copy(own_small, pieces.at[k - 1], small_send.at[k - 1]).wait()
    width = own_small.shape[1]
    small[:, pl.ds(pl.multiple_of(rows * width, width), width)] = own_small[...]
    for k in range(1, 8):
        at = pl.multiple_of((rows + 8 - k) % 8 * width, width)
        small[:, pl.ds(at, width)] = pieces[k - 1]

    own_in.wait()
    own_out = pltpu.make_async_copy(own, full.at[pl.ds(rows * shard, shard), :], own_sem)
    own_out.start()
    x_in.wait()

    def norm_rows(i, carry):
        at = pl.ds(pl.multiple_of(i * 128, 128), 128)
        normed, _ = norm_parts(xbuf[at, :])
        hhb[at, :], hlb[at, :] = split(normed * small[0:1, :] + small[1:2, :])
        return carry

    lax.fori_loop(0, x.shape[0] // 128, norm_rows, 0)
    outs = [
        pltpu.make_async_copy(buf, ref, out_sem.at[i])
        for i, (buf, ref) in enumerate(
            ((thb, th), (tlb, tl), (chb, ch), (clb, cl), (ohb, oh), (olb, ol))
        )
    ]
    own_out.wait()
    wait_bytes(w, own_recv)

    def wide(t):
        return pl.ds(pl.multiple_of(column(t) * 2 * CHUNK, 2 * CHUNK), 2 * CHUNK)

    def q_out(t):
        return pltpu.make_async_copy(qkvb.at[:, wide(t)], qkv.at[:, wide(t)], q_sem.at[t])

    def attend_rows(a):
        head, start = a // 2, a % 2 * 512
        at = pl.ds(pl.multiple_of(start, 512), 512)

        def part(kind):
            return pl.ds(pl.multiple_of((kind * HEADS + head) * 256, 256), 256)

        keys = qkvb[:, part(1)]
        qs = qkvb[at, part(0)]
        scores = mm(qs, twice(keys[:, :HEAD_DIM]), NT) + mm(qs, twice(keys[:, HEAD_DIM:]), NT)
        parts = []
        for u in range(512 // UNIT):
            own_set = sets[:, pl.ds(pl.multiple_of(start + u * UNIT, UNIT), UNIT)][:, 0:1]
            cut = scores[u * UNIT : (u + 1) * UNIT]
            parts.append(jnp.where(own_set == sets[...], cut, -1e30))
        scores = jnp.concatenate(parts, axis=0)
        top = jnp.max(scores, axis=-1, keepdims=True)
        p = jnp.exp2((scores - top) * SCALE2)
        total = jnp.sum(p, axis=-1, keepdims=True)
        ph, plow = split(p)
        vals = qkvb[:, part(2)]
        out = halves_sum(mm(ph, vals) + mm(plow, vals)) / total
        lanes = pl.ds(pl.multiple_of(head * HEAD_DIM, HEAD_DIM), HEAD_DIM)
        ohb[at, lanes], olb[at, lanes] = split(out)
        level = top * SCALE2 + jnp.log2(total)
        for u in range(512 // UNIT):
            tile = jnp.broadcast_to(level[u * UNIT : (u + 1) * UNIT], (UNIT, UNIT))
            lse[head, :, pl.ds(pl.multiple_of(start + u * UNIT, UNIT), UNIT)] = tile.T[0:8]

    def step(s, carry):
        @pl.when(s < chunks)
        def _():
            wait_bytes(w.at[0 : 3 * quarter, 0:CHUNK], z_recv.at[s])
            for k in range(1, 4):
                part = place((z + k) % 4, rep * quarter, quarter, s)
                send(part, part, send_sem, x_recv.at[s], (x_next, rows))
                send(part, part, send_sem, y_recv.at[s], (y_next, rows))

        @pl.when(s + AHEAD < chunks)
        def _():
            start_z(s + AHEAD)

        @pl.when(jnp.logical_and(s >= SPREAD, s < chunks + SPREAD))
        def _():
            t = s - SPREAD
            wait_bytes(w.at[0 : 3 * quarter, 0:CHUNK], x_recv.at[t])
            wait_bytes(w.at[0 : 3 * quarter, 0:CHUNK], y_recv.at[t])
            for k in range(1, 4):
                part = place((z + k) % 4, x_next * quarter, half, t)
                send(part, part, send_sem, fy_recv.at[t], (y_next, rows))
                part = place((z + k) % 4, y_next * quarter + half, half, t)
                send(part, part, send_sem, fx_recv.at[t], (x_next, rows))

        @pl.when(jnp.logical_and(s >= SWAP, s < chunks + SWAP))
        def _():
            t = s - SWAP
            wait_bytes(w.at[0 : 3 * half, 0:CHUNK], fx_recv.at[t])
            wait_bytes(w.at[0 : 3 * half, 0:CHUNK], fy_recv.at[t])
            for k in range(1, 4):
                part = place((z + k) % 4, 0, shard, t)
                send(part, part, core_send, core_recv.at[t], (rep, z * 2 + 1 - c))

        @pl.when(s >= USE)
        def _():
            wait_bytes(full.at[0 : 3 * shard, 0:CHUNK], core_recv.at[s - USE])

        @pl.when(jnp.logical_and(s >= USE, s < proj_chunks + USE))
        def _():
            t = s - USE
            load = pltpu.make_async_copy(full.at[:, cols(t)], wbuf, w_sem)
            load.start()
            load.wait()
            wh, wl = split(wbuf[...])
            kind = t % 3
            at = pl.ds(pl.multiple_of(t // 3 * CHUNK, CHUNK), CHUNK)
            bias = jnp.where(kind == 0, small[2:3, at], jnp.where(kind == 2, small[3:4, at], 0.0))
            qkvb[:, wide(t)] = pair_heads(*split(mm3(hhb[...], hlb[...], wh, wl) + bias))
            q_out(t).start()

        begun, later = s - USE - 3, s - USE - proj_chunks
        a = jnp.where(later < 0, begun // 2, (proj_chunks - 2) // 2 + later)
        due = jnp.logical_or(later >= 0, begun % 2 == 0)

        @pl.when(jnp.logical_and(jnp.logical_and(begun >= 0, due), a < HEADS * 2))
        def _():
            attend_rows(a)

        @pl.when(s == 1)
        def _():
            c_in.wait()

            def split_rows(i, total):
                at = pl.ds(pl.multiple_of(i * 128, 128), 128)
                value = cbuf[at, :]
                chb[at, :], clb[at, :] = split(value)
                return total + col_sum(value)

            gs8[...] = lax.fori_loop(0, cot.shape[0] // 128, split_rows, jnp.zeros((1, D), f32))
            outs[2].start()
            outs[3].start()

        @pl.when(s == 3)
        def _():
            thb[...] = hhb[...].T
            tlb[...] = hlb[...].T
            outs[0].start()
            outs[1].start()

        return carry

    lax.fori_loop(0, chunks + USE, step, 0)
    outs[4].start()
    outs[5].start()
    for t in range(proj_chunks):
        q_out(t).wait()
    for copy in outs:
        copy.wait()
    wait_bytes(full.at[0 : 3 * quarter + 6 * quarter + 6 * half, :], send_sem)
    wait_bytes(full.at[0 : 4 * shard, :], core_send)


def gather(weights, small_params, x, cot, segment_ids):
    shard, width = weights.shape
    t = x.shape[0]
    chunks = width // CHUNK
    hbm = pl.BlockSpec(memory_space=pl.ANY)
    vmem = pl.BlockSpec(memory_space=pltpu.VMEM)
    dma = pltpu.SemaphoreType.DMA
    return pl.pallas_call(
        gather_kernel,
        in_specs=[hbm, vmem, hbm, hbm, vmem],
        out_specs=[hbm, vmem, hbm, hbm, hbm, hbm, vmem, hbm, hbm, hbm, vmem],
        out_shape=[shape_of((8 * shard, width)), shape_of((9, D))]
        + [shape_of((D, t), bf16)] * 2
        + [shape_of((t, D), bf16)] * 2
        + [shape_of((1, D)), shape_of((t, 6 * D), bf16)]
        + [shape_of((t, D), bf16)] * 2
        + [shape_of((HEADS, 8, t))],
        scratch_shapes=[pltpu.VMEM((7,) + small_params.shape, f32), pltpu.VMEM((shard, width), f32)]
        + [pltpu.VMEM((t, D), f32)] * 2
        + [pltpu.VMEM((t, D), bf16)] * 2
        + [pltpu.VMEM((D, t), bf16)] * 2
        + [pltpu.VMEM((t, D), bf16)] * 2
        + [pltpu.VMEM((D, CHUNK), f32), pltpu.VMEM((t, 6 * D), bf16)]
        + [pltpu.VMEM((t, D), bf16)] * 2
        + [dma((7,)), dma((7,)), dma, dma, dma, dma]
        + [dma((chunks,))] * 6
        + [dma((2,)), dma((6,)), dma, dma((3 * D // CHUNK,))],
        compiler_params=pltpu.CompilerParams(
            vmem_limit_bytes=60 * 2**20, collective_id=0, has_side_effects=True
        ),
        cost_estimate=cost(3, 64),
        name="gather",
    )(weights, small_params, x, cot, segment_ids)


def remote(src, dst, sem, recv, device):
    pltpu.make_async_remote_copy(
        src_ref=src, dst_ref=dst, send_sem=sem, recv_sem=recv, device_id=device, device_id_type=MESH
    ).start()


def greet(peers):
    barrier = pltpu.get_barrier_semaphore()
    for peer in peers:
        pl.semaphore_signal(barrier, inc=1, device_id=peer, device_id_type=MESH)
    return lambda: pl.semaphore_wait(barrier, len(peers))


def col_chunk(t):
    return pl.ds(pl.multiple_of(t * CHUNK, CHUNK), CHUNK)


class Summing:
    def __init__(self, bufs, sems):
        self.bufs, self.sems = bufs, sems
        rep, rows = lax.axis_index("rep"), lax.axis_index("rows")
        self.rep, self.px, self.py, self.z, self.c = rep, rep % 2, rep // 2, rows // 2, rows % 2
        self.x_peer = (self.py * 2 + 1 - self.px, rows)
        self.y_peer = ((1 - self.py) * 2 + self.px, rows)

    @staticmethod
    def scratch(chunks):
        buf = lambda *shape: pltpu.VMEM(shape + (16, CHUNK), f32)
        dma = pltpu.SemaphoreType.DMA
        return [
            buf(3, 4, 2, 2, 2, 2),
            buf(chunks, 4, 2, 2, 2),
            buf(chunks, 4, 2),
            buf(chunks, 4, 2),
            buf(chunks, 4),
            buf(chunks, 4),
            buf(chunks, 4, 2),
            buf(chunks, 3, 2),
        ], [dma((3,)), dma] + [dma((chunks,))] * 6

    def free(self, t):
        wait_bytes(self.bufs[0].at[t % 3, :, self.c], self.sems[0].at[t % 3])

    def push(self, t):
        gbuf, core_in = self.bufs[:2]
        to = (self.rep, self.z * 2 + 1 - self.c)
        remote(
            gbuf.at[t % 3, :, 1 - self.c], core_in.at[t], self.sems[0].at[t % 3],
            self.sems[2].at[t], to,
        )

    def halve(self, t):
        gbuf, core_in, a1, b1 = self.bufs[:4]
        _, sent, core_recv, a1_recv, b1_recv = self.sems[:5]
        wait_bytes(core_in.at[t], core_recv.at[t])
        core_in[t] = core_in[t] + gbuf[t % 3, :, self.c]
        remote(core_in.at[t, :, :, 1 - self.px, 0], a1.at[t], sent, a1_recv.at[t], self.x_peer)
        remote(core_in.at[t, :, 1 - self.py, :, 1], b1.at[t], sent, b1_recv.at[t], self.y_peer)

    def quarter(self, t):
        _, core_in, a1, b1, a2, b2 = self.bufs[:6]
        _, sent, _, a1_recv, b1_recv, a2_recv, b2_recv = self.sems[:7]
        wait_bytes(a1.at[t], a1_recv.at[t])
        a1[t] = a1[t] + core_in[t, :, :, self.px, 0]
        remote(a1.at[t, :, 1 - self.py], a2.at[t], sent, a2_recv.at[t], self.y_peer)
        wait_bytes(b1.at[t], b1_recv.at[t])
        b1[t] = b1[t] + core_in[t, :, self.py, :, 1]
        remote(b1.at[t, :, 1 - self.px], b2.at[t], sent, b2_recv.at[t], self.x_peer)

    def along_z(self, t):
        a1, b1, a2, b2, zsrc, z_in = self.bufs[2:]
        _, sent, _, _, _, a2_recv, b2_recv, z_recv = self.sems
        wait_bytes(a2.at[t], a2_recv.at[t])
        zsrc[t, :, 0] = a1[t, :, self.py] + a2[t]
        wait_bytes(b2.at[t], b2_recv.at[t])
        zsrc[t, :, 1] = b1[t, :, self.px] + b2[t]
        for k in range(1, 4):
            to = (self.z + k) % 4
            remote(zsrc.at[t, to], z_in.at[t, k - 1], sent, z_recv.at[t], (self.rep, to * 2 + self.c))

    def z_sum(self, t):
        zsrc, z_in = self.bufs[6:]
        wait_bytes(z_in.at[t], self.sems[7].at[t])
        return (zsrc[t, self.z] + z_in[t, 0]) + (z_in[t, 1] + z_in[t, 2])

    def finish(self):
        a1, b1, a2, b2, _, z_in = self.bufs[2:]

        def sent(t, carry):
            for ref in (a1, b1, a2, b2, z_in):
                wait_bytes(ref.at[t], self.sems[1])
            return carry

        lax.fori_loop(0, a1.shape[0], sent, 0)
        for i in range(3):
            wait_bytes(self.bufs[0].at[i, :, self.c], self.sems[0].at[i])


class Spreading:
    def __init__(self, total, sems, summing):
        self.total, self.sems, self.peers = total, sems, (summing.x_peer, summing.y_peer)
        self.rep = summing.rep

    @staticmethod
    def scratch(chunks):
        dma = pltpu.SemaphoreType.DMA
        return [dma] + [dma((chunks,))] * 4

    def share(self, t, value):
        self.total[t, self.rep] = value
        piece = self.total.at[t, self.rep]
        for recv, peer in zip(self.sems[1:3], self.peers):
            remote(piece, piece, self.sems[0], recv.at[t], peer)

    def forward(self, t):
        x_peer, y_peer = self.peers
        wait_bytes(self.total.at[t, 0], self.sems[1].at[t])
        piece = self.total.at[t, x_peer[0], 0]
        remote(piece, piece, self.sems[0], self.sems[4].at[t], y_peer)
        wait_bytes(self.total.at[t, 0], self.sems[2].at[t])
        piece = self.total.at[t, y_peer[0], 1]
        remote(piece, piece, self.sems[0], self.sems[3].at[t], x_peer)

    def landed(self, t):
        wait_bytes(self.total.at[t, 0, 0], self.sems[3].at[t])
        wait_bytes(self.total.at[t, 0, 0], self.sems[4].at[t])

    def sent(self, t):
        wait_bytes(self.total.at[t, 0:3], self.sems[0])


PUSH = (0, 1, 2, 3, 8, 9, 10, 11, 16, 17, 18, 19)
HALVE = (2, 3, 4, 5, 9, 10, 11, 12, 18, 19, 20, 21)
QUARTER = (5, 7, 8, 9, 10, 11, 12, 15, 21, 22, 23, 25)
ALONG_Z = (8, 9, 10, 11, 12, 13, 15, 18, 23, 24, 26, 27)
Z_SUM = (10, 11, 12, 13, 16, 17, 18, 20, 26, 27, 28, 29)
FORWARD = (12, 13, 16, 17, 18, 19, 20, 22)
FIRST_PUSH = 12


def planned(step, table):
    return sum(jnp.where(step == at, i + 1, 0) for i, at in enumerate(table)) - 1


def mid_kernel(
    oh, ol, x, ch, cl, w, s,
    out, dx1, do, total, part, gs,
    x1, h2h, h2l, uh, ul, acc, chb, clb, dzh, dzl, th, tl, wcol, wrow, *rest,
):
    bufs, sems, (in_sem, w_sem, out_sem) = rest[:8], rest[8:16], rest[16:19]
    summing = Summing(bufs, sems)
    spreading = Spreading(total, rest[19:], summing)
    spread = total.shape[0]
    gbuf = bufs[0]
    rep, rows = lax.axis_index("rep"), lax.axis_index("rows")
    c = rows % 2
    peers = [(rep, (rows // 2 + k) % 4 * 2 + c) for k in range(1, 4)]
    peers += [(rep, rows // 2 * 2 + 1 - c), summing.x_peer, summing.y_peer]
    arrived = greet(peers)

    o_in = [pltpu.make_async_copy(oh, dzh, in_sem.at[0]), pltpu.make_async_copy(ol, dzl, in_sem.at[1])]
    x_in = pltpu.make_async_copy(x, x1, in_sem.at[2])
    c_in = [pltpu.make_async_copy(ch, chb, in_sem.at[3]), pltpu.make_async_copy(cl, clb, in_sem.at[4])]

    def load(g, start):
        for phase, matrix, by_rows in (
            (0, 3, False), (2, 4, False), (4, 5, True), (5, 4, False), (8, 3, True), (9, 5, False),
        ):

            @pl.when(g // 4 == phase)
            def _():
                if by_rows:
                    src = w.at[col_chunk(g % 4), matrix * D : (matrix + 1) * D]
                    copy = pltpu.make_async_copy(src, wrow.at[g % 2], w_sem.at[g % 2])
                else:
                    src = w.at[:, col_chunk(matrix * (D // CHUNK) + g % 4)]
                    copy = pltpu.make_async_copy(src, wcol.at[g % 2], w_sem.at[g % 2])
                copy.start() if start else copy.wait()

    load(0, True)
    for copy in o_in + [x_in] + c_in:
        copy.start()
    arrived()
    for copy in o_in + [x_in]:
        copy.wait()

    def do_out(n, buf):
        target = do.at[:, pl.ds(pl.multiple_of(n * 2 * CHUNK, 2 * CHUNK), 2 * CHUNK)]
        at = pl.ds(pl.multiple_of(n % 2 * 2 * CHUNK, 2 * CHUNK), 2 * CHUNK)
        return pltpu.make_async_copy(buf.at[:, at], target, out_sem.at[8 + n])

    def step(g, carry):
        load(g + 1, True)

        def summed(t):
            value = summing.z_sum(t)

            @pl.when(t < spread)
            def _():
                spreading.share(t, value)

            @pl.when(t >= spread)
            def _():
                part[t - spread] = value

        for table, body in (
            (HALVE, summing.halve),
            (QUARTER, summing.quarter),
            (ALONG_Z, summing.along_z),
            (Z_SUM, summed),
            (FORWARD, spreading.forward),
        ):
            t = planned(g - FIRST_PUSH, table)
            pl.when(t >= 0)(functools.partial(body, t))

        load(g, False)
        n = g % 4
        at = col_chunk(n)

        def phase(p):
            return pl.when(g // 4 == p)

        def gradient(t, high, low):
            @pl.when(t >= 3)
            def _():
                summing.free(t)

            gbuf[t % 3] = mm3(th[...], tl[...], high, low).reshape(gbuf.shape[1:])
            summing.push(t)

        @phase(0)
        def _():
            wh, wl = split(wcol[g % 2])
            x1[:, at] += mm3(dzh[...], dzl[...], wh, wl) + s[4:5, at]

        @phase(1)
        def _():
            normed, _ = norm_parts(x1[at, :])
            h2h[at, :], h2l[at, :] = split(normed * s[5:6, :] + s[6:7, :])

        @phase(2)
        def _():
            wh, wl = split(wcol[g % 2])
            value = mm3(h2h[...], h2l[...], wh, wl) + s[7:8, at]
            square = value * value
            bent = jnp.tanh(ROOT * (value + 0.044715 * value * square))
            high, low = split(0.5 * value * (1.0 + bent))
            uh[:, at], ul[:, at] = high, low
            th[at, :], tl[at, :] = high.T, low.T
            acc[:, at] = 0.5 * (1.0 + bent) + 0.5 * value * (1.0 - bent * bent) * (
                ROOT * (1.0 + 3.0 * 0.044715 * square)
            )

        @phase(3)
        def _():
            @pl.when(n == 0)
            def _():
                for copy in c_in:
                    copy.wait()

            gradient(n, chb[:, at], clb[:, at])

        @phase(4)
        def _():
            wh, wl = split(wrow[g % 2])
            dz = mm3(chb[...], clb[...], wh, wl, NT) * acc[:, at]
            dzh[:, at], dzl[:, at] = split(dz)
            gs[3:4, at] = col_sum(dz)
            th[at, :], tl[at, :] = h2h[:, at].T, h2l[:, at].T

        @phase(5)
        def _():
            @pl.when(n == 0)
            def _():
                acc[...] = jnp.zeros_like(acc)

            gradient(4 + n, dzh[:, at], dzl[:, at])
            wh, wl = split(wcol[g % 2])

            def some_rows(i, done):
                r = col_chunk(i)
                acc[r, :] += mm3(dzh[r, at], dzl[r, at], wh, wl, NT)
                return done

            lax.fori_loop(0, acc.shape[0] // CHUNK, some_rows, 0)

        @phase(6)
        def _():
            @pl.when(n == 0)
            def _():
                gs[0:3, :] = jnp.zeros((3, D), f32)
                for copy in o_in:
                    copy.start()
                for copy in o_in:
                    copy.wait()

            th[at, :], tl[at, :] = dzh[:, at].T, dzl[:, at].T
            dh2 = acc[at, :]
            normed, rstd = norm_parts(x1[at, :])
            cot = chb[at, :].astype(f32) + clb[at, :].astype(f32)
            grad = cot + norm_back(dh2, normed, rstd, s[5:6, :])
            acc[at, :] = grad
            pltpu.make_async_copy(acc.at[at, :], dx1.at[at, :], out_sem.at[n]).start()
            h2h[at, :], h2l[at, :] = split(grad)
            gs[0:1, :] += col_sum(grad)
            gs[1:2, :] += col_sum(dh2 * normed)
            gs[2:3, :] += col_sum(dh2)

        @phase(7)
        def _():
            gradient(8 + n, h2h[:, at], h2l[:, at])

        @phase(8)
        def _():
            wh, wl = split(wrow[g % 2])
            value = pair_heads(*split(mm3(h2h[...], h2l[...], wh, wl, NT)))
            wide = pl.ds(pl.multiple_of(n % 2 * 2 * CHUNK, 2 * CHUNK), 2 * CHUNK)
            for i, buf in enumerate((dzh, dzl)):

                @pl.when(n // 2 == i)
                def _():
                    buf[:, wide] = value
                    do_out(n, buf).start()

        @phase(9)
        def _():
            wh, wl = split(wcol[g % 2])
            x1[:, at] += mm3(uh[...], ul[...], wh, wl) + s[8:9, at]
            pltpu.make_async_copy(x1.at[:, at], out.at[:, at], out_sem.at[4 + n]).start()

        return carry

    lax.fori_loop(0, FIRST_PUSH + Z_SUM[-1] + 1, step, 0)
    for n in range(4):
        at = col_chunk(n)
        pltpu.make_async_copy(acc.at[at, :], dx1.at[at, :], out_sem.at[n]).wait()
        pltpu.make_async_copy(x1.at[:, at], out.at[:, at], out_sem.at[4 + n]).wait()
        do_out(n, (dzh, dzl)[n // 2]).wait()
    summing.finish()
    for t in range(spread):
        spreading.landed(t)
        spreading.sent(t)


def mid(oh, ol, x, ch, cl, full, small):
    t = x.shape[0]
    hbm = pl.BlockSpec(memory_space=pl.ANY)
    vmem = pl.BlockSpec(memory_space=pltpu.VMEM)
    dma = pltpu.SemaphoreType.DMA
    chunks, spread = len(PUSH), len(FORWARD)
    bufs, sems = Summing.scratch(chunks)
    wide, pair = pltpu.VMEM((t, D), f32), [pltpu.VMEM((t, D), bf16)] * 2
    return pl.pallas_call(
        mid_kernel,
        in_specs=[hbm] * 6 + [vmem],
        out_specs=[hbm, hbm, hbm, vmem, vmem, vmem],
        out_shape=[
            shape_of((t, D)),
            shape_of((t, D)),
            shape_of((t, 2 * D), bf16),
            shape_of((spread, 4, 2, 16, CHUNK)),
            shape_of((chunks - spread, 2, 16, CHUNK)),
            shape_of((4, D)),
        ],
        scratch_shapes=[wide, *pair, *pair, wide, *pair, *pair, *pair]
        + [pltpu.VMEM((2, D, CHUNK), f32), pltpu.VMEM((2, CHUNK, D), f32)]
        + bufs
        + sems
        + [dma((5,)), dma((2,)), dma((12,))]
        + Spreading.scratch(spread),
        compiler_params=pltpu.CompilerParams(
            vmem_limit_bytes=60 * 2**20, collective_id=2, has_side_effects=True
        ),
        cost_estimate=cost(9, 60),
        name="mid",
    )(oh, ol, x, ch, cl, full, small)


MAKE = tuple(range(12))
BACK = tuple(range(12, 24))
LAST_HALVE = (2, 3, 4, 5, 6, 7, 8, 9, 10, 11, 12, 13)
LAST_QUARTER = (6, 8, 9, 10, 12, 13, 15, 16, 18, 19, 21, 22)
LAST_Z = (9, 11, 12, 13, 15, 16, 18, 19, 21, 22, 24, 25)
LAST_SUM = (12, 14, 15, 16, 18, 19, 21, 22, 24, 25, 26, 27)
LAST_FORWARD = (14, 16, 17, 18, 20, 21, 23, 24, 26, 27, 28, 29)
NORM = 24


def last_kernel(
    th_in, tl_in, dqh, dql, dkh, dkl, dvh, dvl, w, x, dx1, part, earlier, gs2, gs3, gs4567, gs8, small_in,
    out, total, small_total, norm,
    th, tl, dbuf, wbuf, acc, xbuf, dxbuf, spart, srow, srep, norm_in, *rest,
):
    bufs, sems = rest[:8], rest[8:16]
    h_sem, d_in, w_in, ln_in, ln_out, s_send, s_recv, r_send, r_recv, n_send, n_recv = rest[21:]
    summing = Summing(bufs, sems)
    spreading = Spreading(total, rest[16:21], summing)
    gbuf = bufs[0]
    rep, rows = lax.axis_index("rep"), lax.axis_index("rows")
    before, chunks = part.shape[0], bufs[1].shape[0]
    per = D // CHUNK
    t_rows = x.shape[0]
    arrived = greet(
        [(rep, (rows + k) % 8) for k in range(1, 8)] + [((rep + k) % 4, rows) for k in range(1, 4)]
    )

    h_in = [pltpu.make_async_copy(th_in, th, h_sem.at[0]), pltpu.make_async_copy(tl_in, tl, h_sem.at[1])]

    def load(step, start):
        slot = step % 2
        made, back = planned(step, MAKE), planned(step, BACK)
        u = jnp.maximum(made, back)

        def move(copy):
            copy.start() if start else copy.wait()

        for j, (high, low) in enumerate(((dqh, dql), (dkh, dkl), (dvh, dvl))):

            @pl.when(jnp.logical_and(u >= 0, u // per == j))
            def _():
                for i, source in enumerate((high, low)):
                    move(
                        pltpu.make_async_copy(
                            source.at[:, col_chunk(u % per)], dbuf.at[slot, i], d_in.at[slot, i]
                        )
                    )

        @pl.when(back >= 0)
        def _():
            move(pltpu.make_async_copy(w.at[:, col_chunk(back)], wbuf.at[slot], w_in.at[slot]))

        @pl.when(jnp.logical_and(step >= NORM, step < NORM + 4))
        def _():
            at = col_chunk(step - NORM)
            move(pltpu.make_async_copy(x.at[at, :], xbuf.at[slot], ln_in.at[slot, 0]))
            move(pltpu.make_async_copy(dx1.at[at, :], dxbuf.at[slot], ln_in.at[slot, 1]))

    for copy in h_in:
        copy.start()
    load(0, True)
    acc[...] = jnp.zeros_like(acc)
    arrived()
    for t in range(before):
        spreading.share(t, part[t])
    for copy in h_in:
        copy.wait()

    def step(s, carry):
        load(s + 1, True)
        for table, body in (
            (LAST_HALVE, summing.halve),
            (LAST_QUARTER, summing.quarter),
            (LAST_Z, summing.along_z),
            (LAST_SUM, lambda t: spreading.share(before + t, summing.z_sum(t))),
            (LAST_FORWARD, lambda t: spreading.forward(before + t)),
        ):
            t = planned(s, table)
            pl.when(t >= 0)(functools.partial(body, t))

        @pl.when(jnp.logical_and(s >= 2, s < 2 + before))
        def _():
            spreading.forward(s - 2)

        load(s, False)
        made, back = planned(s, MAKE), planned(s, BACK)

        @pl.when(made >= 3)
        def _():
            summing.free(made)

        @pl.when(made >= 0)
        def _():
            grad = mm3(th[...], tl[...], dbuf[s % 2, 0], dbuf[s % 2, 1])
            gbuf[made % 3] = grad.reshape(gbuf.shape[1:])
            summing.push(made)

        @pl.when(back >= 0)
        def _():
            wh, wl = split(wbuf[s % 2])

            def some_rows(i, done):
                at = col_chunk(i)
                acc[at, :] += mm3(dbuf[s % 2, 0, at, :], dbuf[s % 2, 1, at, :], wh, wl, NT)
                return done

            lax.fori_loop(0, t_rows // CHUNK, some_rows, 0)

        @pl.when(jnp.logical_and(s >= NORM, s < NORM + 4))
        def _():
            at = col_chunk(s - NORM)
            dh = acc[at, :]
            normed, rstd = norm_parts(xbuf[s % 2])
            acc[at, :] = dxbuf[s % 2] + norm_back(dh, normed, rstd, small_in[0:1, :])
            pltpu.make_async_copy(acc.at[at, :], out.at[at, :], ln_out.at[s - NORM]).start()
            gs = jnp.concatenate([col_sum(dh * normed), col_sum(dh)], axis=0)
            for j in range(8):
                piece = gs[:, j * 128 : (j + 1) * 128]

                @pl.when(s == NORM)
                def _():
                    spart[j, 0:2] = piece
                    for row, rest_of in ((2, gs2), (3, gs3), (4, gs4567), (8, gs8)):
                        spart[j, row : row + rest_of.shape[0]] = rest_of[:, j * 128 : (j + 1) * 128]

                @pl.when(s > NORM)
                def _():
                    spart[j, 0:2] += piece

        @pl.when(s == NORM + 4)
        def _():
            for k in range(1, 8):
                to = (rows + k) % 8
                remote(spart.at[to], srow.at[k - 1], s_send.at[k - 1], s_recv.at[k - 1], (rep, to))

        @pl.when(s == NORM + 5)
        def _():
            mine = spart[rows]
            for k in range(1, 8):
                wait_bytes(srow.at[k - 1], s_recv.at[k - 1])
                mine = mine + srow[k - 1]
            srep[rep] = mine
            for k in range(1, 4):
                piece = srep.at[rep]
                remote(piece, piece, r_send.at[k - 1], r_recv.at[k - 1], ((rep + k) % 4, rows))

        return carry

    lax.fori_loop(0, NORM + 6, step, 0)
    for k in range(1, 4):
        wait_bytes(srep.at[0], r_recv.at[k - 1])
    small = (srep[0] + srep[1]) + (srep[2] + srep[3])
    small_total[...] = small

    def squares(ref, t):
        value = ref[t].reshape(128, CHUNK)
        return jnp.sum((value * value).reshape(16, 8, CHUNK), axis=0)

    def one_earlier(t, carry):
        return carry + squares(earlier, t)

    def one(t, carry):
        spreading.landed(t)
        return carry + squares(total, t)

    mats = lax.fori_loop(0, earlier.shape[0], one_earlier, jnp.zeros((8, CHUNK), f32))
    mats = lax.fori_loop(0, before + chunks, one, mats)
    mine = jnp.sum(mats) + jnp.sum(small * small)
    norm_in[rows] = jnp.full((8, 128), mine, f32)
    for k in range(1, 8):
        piece = norm_in.at[rows]
        remote(piece, piece, n_send.at[k - 1], n_recv.at[k - 1], (rep, (rows + k) % 8))
    for k in range(1, 8):
        wait_bytes(norm_in.at[0], n_recv.at[k - 1])
    value = norm_in[0]
    for j in range(1, 8):
        value = value + norm_in[j]
    norm[...] = jnp.sqrt(value)

    summing.finish()
    for i in range(4):
        at = pl.ds(i * CHUNK, CHUNK)
        pltpu.make_async_copy(acc.at[at, :], out.at[at, :], ln_out.at[i]).wait()

    def sent(t, carry):
        spreading.sent(t)
        return carry

    lax.fori_loop(0, before + chunks, sent, 0)
    for k in range(1, 8):
        wait_bytes(srow.at[k - 1], s_send.at[k - 1])
        wait_bytes(norm_in.at[0], n_send.at[k - 1])
    for k in range(1, 4):
        wait_bytes(srep.at[0], r_send.at[k - 1])


def last(th, tl, grads, full, x, dx1, part, earlier, gs, small):
    t = x.shape[0]
    chunks = 3 * D // CHUNK
    every = chunks + part.shape[0]
    hbm = pl.BlockSpec(memory_space=pl.ANY)
    vmem = pl.BlockSpec(memory_space=pltpu.VMEM)
    dma = pltpu.SemaphoreType.DMA
    bufs, sems = Summing.scratch(chunks)
    return pl.pallas_call(
        last_kernel,
        in_specs=[hbm] * 11 + [vmem] * 7,
        out_specs=[hbm, vmem, vmem, vmem],
        out_shape=[
            shape_of((t, D)),
            shape_of((every, 4, 2, 16, CHUNK)),
            shape_of((9, 128)),
            shape_of((8, 128)),
        ],
        scratch_shapes=[
            pltpu.VMEM((D, t), bf16),
            pltpu.VMEM((D, t), bf16),
            pltpu.VMEM((2, 2, t, CHUNK), bf16),
            pltpu.VMEM((2, D, CHUNK), f32),
            pltpu.VMEM((t, D), f32),
            pltpu.VMEM((2, CHUNK, D), f32),
            pltpu.VMEM((2, CHUNK, D), f32),
            pltpu.VMEM((8, 9, 128), f32),
            pltpu.VMEM((7, 9, 128), f32),
            pltpu.VMEM((4, 9, 128), f32),
            pltpu.VMEM((8, 8, 128), f32),
        ]
        + bufs
        + sems
        + Spreading.scratch(every)
        + [dma((2,)), dma((2, 2)), dma((2,)), dma((2, 2)), dma((4,))]
        + [dma((7,)), dma((7,)), dma((3,)), dma((3,)), dma((7,)), dma((7,))],
        compiler_params=pltpu.CompilerParams(
            vmem_limit_bytes=60 * 2**20, collective_id=1, has_side_effects=True
        ),
        cost_estimate=cost(6, 90),
        name="last",
    )(th, tl, *grads, full, x, dx1, part, earlier, *gs, small)


def adam_step(parameter, gradient, first_moment, second_moment, average):
    first_new = 0.9 * first_moment + 0.1 * gradient
    second_new = 0.999 * second_moment + 0.001 * gradient * gradient
    first_hat = first_new * (1.0 / (1.0 - 0.9**STEP))
    second_hat = second_new * (1.0 / (1.0 - 0.999**STEP))
    parameter_new = parameter - 0.05 * (
        first_hat / (jnp.sqrt(second_hat) + 1e-08) + 0.05 * parameter
    )
    average_new = 0.99 * average + 0.01 * parameter_new
    return (parameter_new, first_new, second_new, average_new)


CLIP = 0.25 * math.sqrt(6 * D * D + 9 * D)


def adam_kernel(
    grad_a, grad_b, norm, w, first, second, average, gs, p_s, first_s, second_s, average_s,
    clipped, new_w, first_o, second_o, average_o, low,
    clipped_so, new_so, first_so, second_so, average_so, low_so, norm_out,
):
    norm_out[0] = jnp.max(norm[...])
    factor = jnp.minimum(1.0, CLIP / norm[0:1, 0:1])
    early = pl.program_id(0) < 2
    for j in range(D // CHUNK):
        at = slice(j * CHUNK, (j + 1) * CHUNK)
        value = jnp.where(early, grad_a[j], grad_b[j]).reshape(w.shape[0], CHUNK) * factor
        clipped[:, at] = value
        news = adam_step(w[:, at], value, first[:, at], second[:, at], average[:, at])
        for ref, new in zip((new_w, first_o, second_o, average_o), news):
            ref[:, at] = new
        low[:, at] = news[0].astype(bf16)

    @pl.when(pl.program_id(0) == 0)
    def _():
        value = gs[...] * factor
        clipped_so[...] = value
        news = adam_step(p_s[...], value, first_s[...], second_s[...], average_s[...])
        for ref, new in zip((new_so, first_so, second_so, average_so), news):
            ref[...] = new
        low_so[...] = news[0].astype(bf16)


def adam(earlier, total, norm, mats, gs, smalls):
    shard, width = mats[0].shape
    block = pl.BlockSpec((shard, D), lambda i: (0, jnp.where(i < 3, 5 - i, i - 3)))
    cut = (D // CHUNK,) + total.shape[1:]
    grads = [
        pl.BlockSpec(cut, lambda i: (jnp.minimum(i, 1), 0, 0, 0, 0)),
        pl.BlockSpec(cut, lambda i: (jnp.maximum(i - 2, 0), 0, 0, 0, 0)),
    ]
    small = whole(gs.shape)
    return pl.pallas_call(
        adam_kernel,
        grid=(width // D,),
        in_specs=grads + [whole(norm.shape)] + [block] * 4 + [small] * 5,
        out_specs=[block] * 6 + [small] * 6 + [pl.BlockSpec(memory_space=pltpu.SMEM)],
        out_shape=[shape_of((shard, width))] * 5
        + [shape_of((shard, width), bf16)]
        + [shape_of(gs.shape)] * 5
        + [shape_of(gs.shape, bf16), shape_of((1,))],
        compiler_params=params(),
        cost_estimate=cost(0, 32),
        name="adam",
    )(earlier, total, norm, *mats, gs, *smalls)


def split_once(w, wh, wl):
    @pl.when(pl.program_id(0) == 0)
    def _():
        wh[...], wl[...] = split(w[...])


def out_proj_kernel(oh, ol, w, x, s, x1, h2h, h2l, wh, wl):
    split_once(w, wh, wl)
    value = x[...] + mm3(oh[...], ol[...], wh[...], wl[...]) + s[4:5]
    x1[...] = value
    normed, _ = norm_parts(value)
    h2h[...], h2l[...] = split(normed * s[5:6] + s[6:7])


def out_proj(oh, ol, w, x, small, bm=256):
    t = x.shape[0]
    return pl.pallas_call(
        out_proj_kernel,
        grid=(t // bm,),
        in_specs=[rows_of(bm, D)] * 2 + [matrix(3), rows_of(bm, D), whole((9, D))],
        out_specs=[rows_of(bm, D)] * 3,
        out_shape=[shape_of((t, D)), shape_of((t, D), bf16), shape_of((t, D), bf16)],
        scratch_shapes=[pltpu.VMEM((D, D), bf16)] * 2,
        compiler_params=params(),
        cost_estimate=cost(1, 20),
        name="out_proj",
    )(oh, ol, w, x, small)


def up_kernel(hh, hl, w, s, z, uh, ul):
    wh, wl = split(w[...])
    value = mm3(hh[...], hl[...], wh, wl) + s[7:8]
    z[...] = value
    bent = jnp.tanh(ROOT * (value + 0.044715 * value * value * value))
    uh[...], ul[...] = split(0.5 * value * (1.0 + bent))


def up(hh, hl, w, small, bn=256):
    t = hh.shape[0]
    return pl.pallas_call(
        up_kernel,
        grid=(FF // bn,),
        in_specs=[whole((t, D))] * 2 + [cols_of(D, bn, 4 * D // bn), cols_of(9, bn)],
        out_specs=[cols_of(t, bn)] * 3,
        out_shape=[shape_of((t, FF)), shape_of((t, FF), bf16), shape_of((t, FF), bf16)],
        compiler_params=params(),
        cost_estimate=cost(1, 16),
        name="up",
    )(hh, hl, w, small)


def down_kernel(uh, ul, w, x1, s, out):
    wh, wl = split(w[...])
    out[...] = x1[...] + mm3(uh[...], ul[...], wh, wl) + s[8:9]


def down(uh, ul, w, x1, small, bn=256):
    t = uh.shape[0]
    return pl.pallas_call(
        down_kernel,
        grid=(D // bn,),
        in_specs=[whole((t, FF))] * 2
        + [cols_of(FF, bn, 5 * D // bn), cols_of(t, bn), cols_of(9, bn)],
        out_specs=cols_of(t, bn),
        out_shape=shape_of((t, D)),
        compiler_params=params(),
        cost_estimate=cost(1, 16),
        name="down",
    )(uh, ul, w, x1, small)


def outer_kernel(ah, al, dh, dl, out, th, tl):
    @pl.when(pl.program_id(0) == 0)
    def _():
        th[...] = ah[...].T
        tl[...] = al[...].T

    out[...] = mm3(th[...], tl[...], dh[...], dl[...])


def outer(ah, al, dh, dl, bn=256):
    t, m = ah.shape
    n = dh.shape[1]
    return pl.pallas_call(
        outer_kernel,
        grid=(n // bn,),
        in_specs=[whole((t, m))] * 2 + [cols_of(t, bn)] * 2,
        out_specs=cols_of(m, bn),
        out_shape=shape_of((m, n)),
        scratch_shapes=[pltpu.VMEM((m, t), bf16)] * 2,
        compiler_params=params(),
        cost_estimate=cost(1, 12),
        name="outer",
    )(ah, al, dh, dl)


def down_back_kernel(ch, cl, w, z, dzh, dzl, gs7):
    wh, wl = split(w[...])
    du = mm3(ch[...], cl[...], wh, wl, NT)
    value = z[...]
    square = value * value
    bent = jnp.tanh(ROOT * (value + 0.044715 * value * square))
    slope = 0.5 * (1.0 + bent) + 0.5 * value * (1.0 - bent * bent) * (
        ROOT * (1.0 + 3.0 * 0.044715 * square)
    )
    dz = du * slope
    dzh[...], dzl[...] = split(dz)
    gs7[...] = col_sum(dz)


def down_back(ch, cl, w, z, bn=256):
    t = ch.shape[0]
    return pl.pallas_call(
        down_back_kernel,
        grid=(FF // bn,),
        in_specs=[whole((t, D))] * 2 + [rows_of(bn, D, 5), cols_of(t, bn)],
        out_specs=[cols_of(t, bn)] * 2 + [cols_of(1, bn)],
        out_shape=[shape_of((t, FF), bf16)] * 2 + [shape_of((1, FF))],
        compiler_params=params(),
        cost_estimate=cost(1, 16),
        name="down_back",
    )(ch, cl, w, z)


def up_back_kernel(dzh, dzl, w, x1, cot, s, dx1, dxh, dxl, gs4, gs5, gs6, wh, wl):
    split_once(w, wh, wl)
    dh2 = mm3(dzh[...], dzl[...], wh[...], wl[...], NT)
    normed, rstd = norm_parts(x1[...])
    grad = cot[...] + norm_back(dh2, normed, rstd, s[5:6])
    dx1[...] = grad
    dxh[...], dxl[...] = split(grad)
    add_up(gs4, col_sum(grad))
    add_up(gs5, col_sum(dh2 * normed))
    add_up(gs6, col_sum(dh2))


def up_back(dzh, dzl, w, x1, cot, small, bm=256):
    t = x1.shape[0]
    return pl.pallas_call(
        up_back_kernel,
        grid=(t // bm,),
        in_specs=[rows_of(bm, FF)] * 2 + [matrix(4)] + [rows_of(bm, D)] * 2 + [whole((9, D))],
        out_specs=[rows_of(bm, D)] * 3 + [whole((1, D))] * 3,
        out_shape=[shape_of((t, D)), shape_of((t, D), bf16), shape_of((t, D), bf16)]
        + [shape_of((1, D))] * 3,
        scratch_shapes=[pltpu.VMEM((D, FF), bf16)] * 2,
        compiler_params=params(),
        cost_estimate=cost(1, 24),
        name="up_back",
    )(dzh, dzl, w, x1, cot, small)


def out_proj_back_kernel(dxh, dxl, w, do):
    wh, wl = split(w[...])
    do[...] = pair_heads(*split(mm3(dxh[...], dxl[...], wh, wl, NT)))


def out_proj_back(dxh, dxl, w, bn=256):
    t = dxh.shape[0]
    return pl.pallas_call(
        out_proj_back_kernel,
        grid=(D // bn,),
        in_specs=[whole((t, D))] * 2 + [rows_of(bn, D, 3)],
        out_specs=cols_of(t, 2 * bn),
        out_shape=shape_of((t, 2 * D), bf16),
        compiler_params=params(),
        cost_estimate=cost(1, 12),
        name="out_proj_back",
    )(dxh, dxl, w)


def proj_back_kernel(
    dqh, dql, dkh, dkl, dvh, dvl, wq, wk, wv, x, dx1, s, out, gs0, gs1, wh, wl
):
    @pl.when(pl.program_id(0) == 0)
    def _():
        for j, w in enumerate((wq, wk, wv)):
            wh[j], wl[j] = split(w[...])

    dh = mm3(dqh[...], dql[...], wh[0], wl[0], NT)
    dh += mm3(dkh[...], dkl[...], wh[1], wl[1], NT)
    dh += mm3(dvh[...], dvl[...], wh[2], wl[2], NT)
    normed, rstd = norm_parts(x[...])
    out[...] = dx1[...] + norm_back(dh, normed, rstd, s[0:1])
    add_up(gs0, col_sum(dh * normed))
    add_up(gs1, col_sum(dh))


def proj_back(grads, w, x, dx1, small, bm=256):
    t = x.shape[0]
    return pl.pallas_call(
        proj_back_kernel,
        grid=(t // bm,),
        in_specs=[rows_of(bm, D)] * 6 + [matrix(j) for j in range(3)] + [rows_of(bm, D)] * 2 + [whole((9, D))],
        out_specs=[rows_of(bm, D)] + [whole((1, D))] * 2,
        out_shape=[shape_of((t, D))] + [shape_of((1, D))] * 2,
        scratch_shapes=[pltpu.VMEM((3, D, D), bf16)] * 2,
        compiler_params=params(),
        cost_estimate=cost(3, 36),
        name="proj_back",
    )(*grads, w, w, w, x, dx1, small)


def set_bounds(segment_ids):
    ids = segment_ids[0, ::UNIT]
    order, sets = (ids - ids[0])[None, :], jnp.arange(SETS, dtype=jnp.int32)[:, None]
    lengths = jnp.sum((order == sets).astype(jnp.int32), axis=1)
    firsts = jnp.sum((order < sets).astype(jnp.int32), axis=1)
    return jnp.stack([firsts, lengths], axis=1).reshape(-1).astype(jnp.int32)


def shards(
    reps,
    latents,
    cotangent,
    segment_ids,
    weights,
    small_params,
    first_mats,
    second_mats,
    average_mats,
    first_small,
    second_small,
    average_small,
):
    segs = set_bounds(segment_ids)
    x, cot = latents[0], cotangent[0]
    fast = reps == 4 and weights.shape[0] * 8 == D and x.shape[0] == D
    if fast:
        full, small, th, tl, ch, cl, gs8, qkv, oh, ol, lse = gather(
            weights, small_params, x, cot, segment_ids
        )
    else:
        full, small = (
            lax.all_gather(weights, "rows", axis=0, tiled=True),
            lax.all_gather(small_params, "rows", axis=1, tiled=True),
        )
        bias = jnp.concatenate([small[2], jnp.zeros((D,), f32), small[3]])[None]
        hh, hl, ch, cl, gs8 = prep(x, cot, small)
        qkv = proj(hh, hl, full, bias)
        oh, ol, lse = attend(segs, qkv)
    if fast:
        output, dx1, do, earlier, part, gs4567 = mid(oh, ol, x, ch, cl, full, small)
    else:
        x1, h2h, h2l = out_proj(oh, ol, full, x, small)
        z, uh, ul = up(h2h, h2l, full, small)
        output = down(uh, ul, full, x1, small)
        g_down = outer(uh, ul, ch, cl)
        dzh, dzl, gs7 = down_back(ch, cl, full, z)
        g_up = outer(h2h, h2l, dzh, dzl)
        dx1, dxh, dxl, gs4, gs5, gs6 = up_back(dzh, dzl, full, x1, cot, small)
        g_out = outer(oh, ol, dxh, dxl)
        do = out_proj_back(dxh, dxl, full)
        gs4567 = jnp.concatenate([gs4, gs5, gs6, gs7], axis=0)
    *grads, gs2, gs3, output = attend_back(segs, qkv, do, oh, ol, lse, output)
    gs_rest = (gs2, gs3, gs4567, gs8)
    if fast:
        token_grad, total, small_total, norm = last(
            th, tl, grads, full, x, dx1, part, earlier, gs_rest, small
        )
        (
            clipped_mats, new_weights, first_mats_out, second_mats_out, average_mats_out, low_mats,
            clipped_small, new_small, first_small_out, second_small_out, average_small_out, low_small,
            norm,
        ) = adam(
            earlier, total, norm, (weights, first_mats, second_mats, average_mats), small_total,
            (small_params, first_small, second_small, average_small),
        )
    else:
        g_qkv = [outer(hh, hl, grads[2 * j], grads[2 * j + 1]) for j in range(3)]
        token_grad, gs0, gs1 = proj_back(grads, full, x, dx1, small)
        weight_grad = jnp.concatenate(g_qkv + [g_out, g_up, g_down], axis=1)
        small_grad = jnp.concatenate([gs0, gs1, *gs_rest], axis=0)
        part_weights, part_small = (
            lax.psum_scatter(weight_grad, "rows", scatter_dimension=0, tiled=True),
            lax.psum_scatter(small_grad, "rows", scatter_dimension=1, tiled=True),
        )
        sum_weights, sum_small = lax.psum((part_weights, part_small), "rep")
        squares = lax.psum(
            jnp.sum(sum_weights * sum_weights) + jnp.sum(sum_small * sum_small), "rows"
        )
        norm = jnp.sqrt(squares).reshape(1)
        factor = jnp.minimum(1.0, CLIP / norm[0])
        clipped_mats = sum_weights * factor
        clipped_small = sum_small * factor
        new_weights, first_mats_out, second_mats_out, average_mats_out = adam_step(
            weights, clipped_mats, first_mats, second_mats, average_mats
        )
        new_small, first_small_out, second_small_out, average_small_out = adam_step(
            small_params, clipped_small, first_small, second_small, average_small
        )
        low_mats, low_small = new_weights.astype(bf16), new_small.astype(bf16)
    return (
        output[None],
        token_grad[None],
        norm,
        clipped_mats,
        clipped_small,
        new_weights,
        new_small,
        first_mats_out,
        second_mats_out,
        average_mats_out,
        first_small_out,
        second_small_out,
        average_small_out,
        low_mats,
        low_small,
    )


def solution(mesh):
    tokens, mats, small = P("rep", "rows", None), P("rows", None), P(None, "rows")
    in_specs = (tokens, tokens, P("rep", "rows")) + (mats, small) + (mats,) * 3 + (small,) * 3
    out_specs = (
        (tokens, tokens, P(), mats, small, mats, small) + (mats,) * 3 + (small,) * 3 + (mats, small)
    )
    step = functools.partial(shards, mesh.shape["rep"])
    return jax.shard_map(step, mesh=mesh, in_specs=in_specs, out_specs=out_specs, check_vma=False)
```

```python
import functools
import math

import jax
import jax.numpy as jnp
from jax import lax
from jax.experimental import pallas as pl
from jax.experimental.pallas import tpu as pltpu
from jax.sharding import PartitionSpec as P

D = 1024
HEADS = 8
HEAD_DIM = 128
FF = 1024
UNIT = 128
SETS = 3
STEP = 5
SCALE = HEAD_DIM ** (-0.5)
SCALE2 = SCALE / math.log(2.0)
ROOT = math.sqrt(2.0 / math.pi)

f32 = jnp.float32
bf16 = jnp.bfloat16

NN = (((1,), (0,)), ((), ()))
NT = (((1,), (1,)), ((), ()))
TN = (((0,), (0,)), ((), ()))


def params(mib=56):
    return pltpu.CompilerParams(
        vmem_limit_bytes=mib * 2**20, dimension_semantics=("arbitrary",)
    )


def mm(a, b, dims=NN):
    return lax.dot_general(a, b, dims, preferred_element_type=f32)


def split(x):
    high = x.astype(bf16)
    return high, (x - high.astype(f32)).astype(bf16)


def mm3(ah, al, bh, bl, dims=NN):
    return mm(ah, bh, dims) + (mm(al, bh, dims) + mm(ah, bl, dims))


def cost(products, mib):
    return pl.CostEstimate(
        flops=int(products * 3 * 2 * 1024**3), bytes_accessed=int(mib * 2**20), transcendentals=0
    )


def whole(shape):
    return pl.BlockSpec(shape, lambda *i: (0,) * len(shape))


def rows_of(bm, n, column=0):
    return pl.BlockSpec((bm, n), lambda i, *_: (i, column))


def matrix(j):
    return pl.BlockSpec((D, D), lambda i: (0, j), pipeline_mode=pl.Buffered(1))


def cols_of(m, bn, first=0):
    return pl.BlockSpec((m, bn), lambda i, *_: (0, first + i))


def shape_of(shape, dtype=f32):
    return jax.ShapeDtypeStruct(shape, dtype)


def norm_parts(x):
    center = x - jnp.mean(x, axis=-1, keepdims=True)
    rstd = lax.rsqrt(jnp.mean(center * center, axis=-1, keepdims=True) + 1e-05)
    return center * rstd, rstd


def norm_back(grad, normed, rstd, gain):
    scaled = grad * gain
    return rstd * (
        scaled
        - jnp.mean(scaled, axis=-1, keepdims=True)
        - normed * jnp.mean(scaled * normed, axis=-1, keepdims=True)
    )


def col_sum(x):
    return jnp.sum(x, axis=0, keepdims=True)


def add_up(ref, value):
    first = pl.program_id(0) == 0

    @pl.when(first)
    def _():
        ref[...] = value

    @pl.when(jnp.logical_not(first))
    def _():
        ref[...] += value


def prep_kernel(x, cot, s, hh, hl, ch, cl, gs8):
    normed, _ = norm_parts(x[...])
    hh[...], hl[...] = split(normed * s[0:1] + s[1:2])
    ch[...], cl[...] = split(cot[...])
    add_up(gs8, col_sum(cot[...]))


def prep(x, cot, small, bm=256):
    t = x.shape[0]
    return pl.pallas_call(
        prep_kernel,
        grid=(t // bm,),
        in_specs=[rows_of(bm, D), rows_of(bm, D), whole((9, D))],
        out_specs=[rows_of(bm, D)] * 4 + [whole((1, D))],
        out_shape=[shape_of((t, D), bf16)] * 4 + [shape_of((1, D))],
        compiler_params=params(),
        cost_estimate=cost(0, 16),
        name="prep",
    )(x, cot, small)


def pair_heads(high, low):
    parts = []
    for head in range(high.shape[1] // HEAD_DIM):
        cut = slice(head * HEAD_DIM, (head + 1) * HEAD_DIM)
        parts += [high[:, cut], low[:, cut]]
    return jnp.concatenate(parts, axis=1)


def proj_kernel(hh, hl, w, bias, out):
    wh, wl = split(w[...])
    out[...] = pair_heads(*split(mm3(hh[...], hl[...], wh, wl) + bias[...]))


def proj(hh, hl, w, bias, bn=256):
    t, n = hh.shape[0], bias.shape[1]
    return pl.pallas_call(
        proj_kernel,
        grid=(n // bn,),
        in_specs=[whole((t, D))] * 2 + [cols_of(D, bn), cols_of(1, bn)],
        out_specs=cols_of(t, 2 * bn),
        out_shape=shape_of((t, 2 * n), bf16),
        compiler_params=params(),
        cost_estimate=cost(n // D, 8 * (n // D) + 4),
        name="proj",
    )(hh, hl, w, bias)


def twice(a):
    return jnp.concatenate([a, a], axis=1)


def halves_sum(x):
    return x[:, :HEAD_DIM] + x[:, HEAD_DIM:]


def pieces(n):
    out, at = [], 0
    while at < n:
        size = min(256, n - at)
        out.append((at, size))
        at += size
    return out


def for_sets(segs, units, body):
    def one(i, carry):
        first, length = segs[2 * i], segs[2 * i + 1]
        for count in range(1, units - SETS + 2):

            @pl.when(length == count)
            def _():
                body(pl.multiple_of(first * UNIT, UNIT), count * UNIT)

        return carry

    lax.fori_loop(0, SETS, one, 0)


def attend_kernel(segs, q, k, v, oh, ol, lse):
    units = q.shape[0] // UNIT

    def body(first, n):
        rows = pl.ds(first, n)
        keys = k[rows, :]
        kh, kl = twice(keys[:, :HEAD_DIM]), twice(keys[:, HEAD_DIM:])
        vals = v[rows, :]
        for at, size in pieces(n):
            sub = pl.ds(pl.multiple_of(first + at, UNIT), size)
            qs = q[sub, :]
            scores = mm(qs, kh, NT) + mm(qs, kl, NT)
            top = jnp.max(scores, axis=-1, keepdims=True)
            p = jnp.exp2((scores - top) * SCALE2)
            total = jnp.sum(p, axis=-1, keepdims=True)
            ph, plow = split(p)
            o = halves_sum(mm(ph, vals) + mm(plow, vals)) / total
            oh[sub, :], ol[sub, :] = split(o)
            level = top * SCALE2 + jnp.log2(total)
            for u in range(size // UNIT):
                tile = jnp.broadcast_to(level[u * UNIT : (u + 1) * UNIT], (UNIT, UNIT))
                lse[0, :, pl.ds(pl.multiple_of(first + at + u * UNIT, UNIT), UNIT)] = tile.T[0:8]

    for_sets(segs, units, body)


def attend(segs, qkv):
    t = qkv.shape[0]
    head = lambda first: pl.BlockSpec((t, 2 * HEAD_DIM), lambda i, *_: (0, first + i))
    return pl.pallas_call(
        attend_kernel,
        grid_spec=pltpu.PrefetchScalarGridSpec(
            num_scalar_prefetch=1,
            grid=(HEADS,),
            in_specs=[head(0), head(HEADS), head(2 * HEADS)],
            out_specs=[cols_of(t, HEAD_DIM)] * 2
            + [pl.BlockSpec((1, 8, t), lambda i, *_: (i, 0, 0))],
        ),
        out_shape=[shape_of((t, D), bf16)] * 2 + [shape_of((HEADS, 8, t))],
        compiler_params=params(),
        cost_estimate=cost(2, 16),
        name="attend",
    )(segs, qkv, qkv, qkv)


def attend_back_kernel(
    segs, q, k, v, do, oh, ol, lse, done, dqh, dql, dkh, dkl, dvh, dvl, gq, gv, done_out, drow, qsum, vsum
):
    units = q.shape[0] // UNIT
    for u in range(units):
        cut = slice(u * UNIT, (u + 1) * UNIT)
        grad = do[cut, :].astype(f32)
        out = oh[cut, :].astype(f32) + ol[cut, :].astype(f32)
        tile = (halves_sum(grad) * out).T
        drow[:, cut] = jnp.broadcast_to(col_sum(tile), (8, UNIT))
    done_out[...] = done[...]
    qsum[...] = jnp.zeros_like(qsum)
    vsum[...] = jnp.zeros_like(vsum)

    def body(first, n):
        rows = pl.ds(first, n)
        keys, vals = k[rows, :], v[rows, :]
        dk = dv = None
        for at, size in pieces(n):
            sub = pl.ds(pl.multiple_of(first + at, UNIT), size)
            qs, grad = q[sub, :], do[sub, :]
            scores = mm(keys, twice(qs[:, :HEAD_DIM]), NT) + mm(keys, twice(qs[:, HEAD_DIM:]), NT)
            p = jnp.exp2(scores * SCALE2 - lse[0, 0:1, sub])
            dp = mm(vals, twice(grad[:, :HEAD_DIM]), NT) + mm(vals, twice(grad[:, HEAD_DIM:]), NT)
            ds = p * (dp - drow[0:1, sub])
            ph, plow = split(p)
            dsh, dsl = split(ds)
            dv_part = mm(ph, grad) + mm(plow, grad)
            dk_part = mm(dsh, qs) + mm(dsl, qs)
            dv = dv_part if dv is None else dv + dv_part
            dk = dk_part if dk is None else dk + dk_part
            dq = halves_sum(mm(dsh, keys, TN) + mm(dsl, keys, TN)) * SCALE
            dqh[sub, :], dql[sub, :] = split(dq)
            qsum[0:1, :] += col_sum(dq)
        dk = halves_sum(dk) * SCALE
        dv = halves_sum(dv)
        dkh[rows, :], dkl[rows, :] = split(dk)
        dvh[rows, :], dvl[rows, :] = split(dv)
        vsum[0:1, :] += col_sum(dv)

    for_sets(segs, units, body)
    gq[...] = qsum[0:1, :]
    gv[...] = vsum[0:1, :]


def attend_back(segs, qkv, do, oh, ol, lse, done):
    t = qkv.shape[0]
    head = lambda first: pl.BlockSpec((t, 2 * HEAD_DIM), lambda i, *_: (0, first + i))
    return pl.pallas_call(
        attend_back_kernel,
        grid_spec=pltpu.PrefetchScalarGridSpec(
            num_scalar_prefetch=1,
            grid=(HEADS,),
            in_specs=[head(0), head(HEADS), head(2 * HEADS), head(0)]
            + [cols_of(t, HEAD_DIM)] * 2
            + [pl.BlockSpec((1, 8, t), lambda i, *_: (i, 0, 0)), rows_of(t // HEADS, D)],
            out_specs=[cols_of(t, HEAD_DIM)] * 6
            + [cols_of(1, HEAD_DIM)] * 2
            + [rows_of(t // HEADS, D)],
            scratch_shapes=[
                pltpu.VMEM((8, t), f32),
                pltpu.VMEM((8, HEAD_DIM), f32),
                pltpu.VMEM((8, HEAD_DIM), f32),
            ],
        ),
        out_shape=[shape_of((t, D), bf16)] * 6 + [shape_of((1, D))] * 2 + [shape_of((t, D))],
        compiler_params=params(),
        cost_estimate=cost(5, 36),
        name="attend_back",
    )(segs, qkv, qkv, qkv, do, oh, ol, lse, done)


MESH = pl.DeviceIdType.MESH
CHUNK = 256
AHEAD, SPREAD, SWAP, USE = 4, 2, 5, 7


def wait_bytes(ref, sem):
    pltpu.make_async_copy(ref, ref, sem).wait()


def gather_kernel(
    w, own_small, x, cot, sets,
    full, small, th, tl, ch, cl, gs8, qkv, oh, ol, lse,
    pieces, own, xbuf, cbuf, hhb, hlb, thb, tlb, chb, clb, wbuf, qkvb, ohb, olb,
    small_send, small_recv, own_sem, send_sem, core_send, own_recv,
    z_recv, x_recv, y_recv, fx_recv, fy_recv, core_recv, in_sem, out_sem, w_sem, q_sem,
):
    rep, rows = lax.axis_index("rep"), lax.axis_index("rows")
    z, c = rows // 2, rows % 2
    x_next, y_next = rep // 2 * 2 + (1 - rep % 2), (1 - rep // 2) * 2 + rep % 2
    shard = w.shape[0]
    quarter, half = shard // 4, shard // 8
    chunks = w.shape[1] // CHUNK
    proj_chunks = 3 * D // CHUNK
    per = D // CHUNK

    x_in = pltpu.make_async_copy(x, xbuf, in_sem.at[0])
    c_in = pltpu.make_async_copy(cot, cbuf, in_sem.at[1])
    x_in.start()
    c_in.start()
    own_in = pltpu.make_async_copy(w, own, own_sem)
    own_in.start()

    barrier = pltpu.get_barrier_semaphore()
    peers = [(rep, (rows + k) % 8) for k in range(1, 8)] + [(x_next, rows), (y_next, rows)]
    for peer in peers:
        pl.semaphore_signal(barrier, inc=1, device_id=peer, device_id_type=MESH)
    pl.semaphore_wait(barrier, len(peers))

    def send(src, dst, sem, recv, device):
        pltpu.make_async_remote_copy(
            src_ref=src, dst_ref=dst, send_sem=sem, recv_sem=recv, device_id=device,
            device_id_type=MESH,
        ).start()

    for k in range(1, 8):
        send(own_small, pieces.at[k - 1], small_send.at[k - 1], small_recv.at[k - 1], (rep, (rows + k) % 8))

    def column(t):
        return jnp.where(t < proj_chunks, t % 3 * per + t // 3, t)

    def cols(t):
        return pl.ds(pl.multiple_of(column(t) * CHUNK, CHUNK), CHUNK)

    def place(zz, first, count, t):
        at = (zz * 2 + c) * shard + first
        return full.at[pl.ds(pl.multiple_of(at, half), count), cols(t)]

    def start_z(t):
        src = w.at[pl.ds(pl.multiple_of(rep * quarter, quarter), quarter), cols(t)]
        for k in range(1, 4):
            send(src, place(z, rep * quarter, quarter, t), send_sem, z_recv.at[t], (rep, (z + k) % 4 * 2 + c))

    for t in range(AHEAD):
        start_z(t)
    send(w, full.at[pl.ds(rows * shard, shard), :], core_send, own_recv, (rep, z * 2 + 1 - c))

    for k in range(1, 8):
        pltpu.make_async_copy(own_small, pieces.at[k - 1], small_recv.at[k - 1]).wait()
        pltpu.make_async_copy(own_small, pieces.at[k - 1], small_send.at[k - 1]).wait()
    width = own_small.shape[1]
    small[:, pl.ds(pl.multiple_of(rows * width, width), width)] = own_small[...]
    for k in range(1, 8):
        at = pl.multiple_of((rows + 8 - k) % 8 * width, width)
        small[:, pl.ds(at, width)] = pieces[k - 1]

    own_in.wait()
    own_out = pltpu.make_async_copy(own, full.at[pl.ds(rows * shard, shard), :], own_sem)
    own_out.start()
    x_in.wait()

    def norm_rows(i, carry):
        at = pl.ds(pl.multiple_of(i * 128, 128), 128)
        normed, _ = norm_parts(xbuf[at, :])
        hhb[at, :], hlb[at, :] = split(normed * small[0:1, :] + small[1:2, :])
        return carry

    lax.fori_loop(0, x.shape[0] // 128, norm_rows, 0)
    outs = [
        pltpu.make_async_copy(buf, ref, out_sem.at[i])
        for i, (buf, ref) in enumerate(
            ((thb, th), (tlb, tl), (chb, ch), (clb, cl), (ohb, oh), (olb, ol))
        )
    ]
    own_out.wait()
    wait_bytes(w, own_recv)

    def wide(t):
        return pl.ds(pl.multiple_of(column(t) * 2 * CHUNK, 2 * CHUNK), 2 * CHUNK)

    def q_out(t):
        return pltpu.make_async_copy(qkvb.at[:, wide(t)], qkv.at[:, wide(t)], q_sem.at[t])

    def attend_rows(a):
        head, start = a // 2, a % 2 * 512
        at = pl.ds(pl.multiple_of(start, 512), 512)

        def part(kind):
            return pl.ds(pl.multiple_of((kind * HEADS + head) * 256, 256), 256)

        keys = qkvb[:, part(1)]
        qs = qkvb[at, part(0)]
        scores = mm(qs, twice(keys[:, :HEAD_DIM]), NT) + mm(qs, twice(keys[:, HEAD_DIM:]), NT)
        parts = []
        for u in range(512 // UNIT):
            own_set = sets[:, pl.ds(pl.multiple_of(start + u * UNIT, UNIT), UNIT)][:, 0:1]
            cut = scores[u * UNIT : (u + 1) * UNIT]
            parts.append(jnp.where(own_set == sets[...], cut, -1e30))
        scores = jnp.concatenate(parts, axis=0)
        top = jnp.max(scores, axis=-1, keepdims=True)
        p = jnp.exp2((scores - top) * SCALE2)
        total = jnp.sum(p, axis=-1, keepdims=True)
        ph, plow = split(p)
        vals = qkvb[:, part(2)]
        out = halves_sum(mm(ph, vals) + mm(plow, vals)) / total
        lanes = pl.ds(pl.multiple_of(head * HEAD_DIM, HEAD_DIM), HEAD_DIM)
        ohb[at, lanes], olb[at, lanes] = split(out)
        level = top * SCALE2 + jnp.log2(total)
        for u in range(512 // UNIT):
            tile = jnp.broadcast_to(level[u * UNIT : (u + 1) * UNIT], (UNIT, UNIT))
            lse[head, :, pl.ds(pl.multiple_of(start + u * UNIT, UNIT), UNIT)] = tile.T[0:8]

    def step(s, carry):
        @pl.when(s < chunks)
        def _():
            wait_bytes(w.at[0 : 3 * quarter, 0:CHUNK], z_recv.at[s])
            for k in range(1, 4):
                part = place((z + k) % 4, rep * quarter, quarter, s)
                send(part, part, send_sem, x_recv.at[s], (x_next, rows))
                send(part, part, send_sem, y_recv.at[s], (y_next, rows))

        @pl.when(s + AHEAD < chunks)
        def _():
            start_z(s + AHEAD)

        @pl.when(jnp.logical_and(s >= SPREAD, s < chunks + SPREAD))
        def _():
            t = s - SPREAD
            wait_bytes(w.at[0 : 3 * quarter, 0:CHUNK], x_recv.at[t])
            wait_bytes(w.at[0 : 3 * quarter, 0:CHUNK], y_recv.at[t])
            for k in range(1, 4):
                part = place((z + k) % 4, x_next * quarter, half, t)
                send(part, part, send_sem, fy_recv.at[t], (y_next, rows))
                part = place((z + k) % 4, y_next * quarter + half, half, t)
                send(part, part, send_sem, fx_recv.at[t], (x_next, rows))

        @pl.when(jnp.logical_and(s >= SWAP, s < chunks + SWAP))
        def _():
            t = s - SWAP
            wait_bytes(w.at[0 : 3 * half, 0:CHUNK], fx_recv.at[t])
            wait_bytes(w.at[0 : 3 * half, 0:CHUNK], fy_recv.at[t])
            for k in range(1, 4):
                part = place((z + k) % 4, 0, shard, t)
                send(part, part, core_send, core_recv.at[t], (rep, z * 2 + 1 - c))

        @pl.when(s >= USE)
        def _():
            wait_bytes(full.at[0 : 3 * shard, 0:CHUNK], core_recv.at[s - USE])

        @pl.when(jnp.logical_and(s >= USE, s < proj_chunks + USE))
        def _():
            t = s - USE
            load = pltpu.make_async_copy(full.at[:, cols(t)], wbuf, w_sem)
            load.start()
            load.wait()
            wh, wl = split(wbuf[...])
            kind = t % 3
            at = pl.ds(pl.multiple_of(t // 3 * CHUNK, CHUNK), CHUNK)
            bias = jnp.where(kind == 0, small[2:3, at], jnp.where(kind == 2, small[3:4, at], 0.0))
            qkvb[:, wide(t)] = pair_heads(*split(mm3(hhb[...], hlb[...], wh, wl) + bias))
            q_out(t).start()

        begun, later = s - USE - 3, s - USE - proj_chunks
        a = jnp.where(later < 0, begun // 2, (proj_chunks - 2) // 2 + later)
        due = jnp.logical_or(later >= 0, begun % 2 == 0)

        @pl.when(jnp.logical_and(jnp.logical_and(begun >= 0, due), a < HEADS * 2))
        def _():
            attend_rows(a)

        @pl.when(s == 1)
        def _():
            c_in.wait()

            def split_rows(i, total):
                at = pl.ds(pl.multiple_of(i * 128, 128), 128)
                value = cbuf[at, :]
                chb[at, :], clb[at, :] = split(value)
                return total + col_sum(value)

            gs8[...] = lax.fori_loop(0, cot.shape[0] // 128, split_rows, jnp.zeros((1, D), f32))
            outs[2].start()
            outs[3].start()

        @pl.when(s == 3)
        def _():
            thb[...] = hhb[...].T
            tlb[...] = hlb[...].T
            outs[0].start()
            outs[1].start()

        return carry

    lax.fori_loop(0, chunks + USE, step, 0)
    outs[4].start()
    outs[5].start()
    for t in range(proj_chunks):
        q_out(t).wait()
    for copy in outs:
        copy.wait()
    wait_bytes(full.at[0 : 3 * quarter + 6 * quarter + 6 * half, :], send_sem)
    wait_bytes(full.at[0 : 4 * shard, :], core_send)


def gather(weights, small_params, x, cot, segment_ids):
    shard, width = weights.shape
    t = x.shape[0]
    chunks = width // CHUNK
    hbm = pl.BlockSpec(memory_space=pl.ANY)
    vmem = pl.BlockSpec(memory_space=pltpu.VMEM)
    dma = pltpu.SemaphoreType.DMA
    return pl.pallas_call(
        gather_kernel,
        in_specs=[hbm, vmem, hbm, hbm, vmem],
        out_specs=[hbm, vmem, hbm, hbm, hbm, hbm, vmem, hbm, hbm, hbm, vmem],
        out_shape=[shape_of((8 * shard, width)), shape_of((9, D))]
        + [shape_of((D, t), bf16)] * 2
        + [shape_of((t, D), bf16)] * 2
        + [shape_of((1, D)), shape_of((t, 6 * D), bf16)]
        + [shape_of((t, D), bf16)] * 2
        + [shape_of((HEADS, 8, t))],
        scratch_shapes=[pltpu.VMEM((7,) + small_params.shape, f32), pltpu.VMEM((shard, width), f32)]
        + [pltpu.VMEM((t, D), f32)] * 2
        + [pltpu.VMEM((t, D), bf16)] * 2
        + [pltpu.VMEM((D, t), bf16)] * 2
        + [pltpu.VMEM((t, D), bf16)] * 2
        + [pltpu.VMEM((D, CHUNK), f32), pltpu.VMEM((t, 6 * D), bf16)]
        + [pltpu.VMEM((t, D), bf16)] * 2
        + [dma((7,)), dma((7,)), dma, dma, dma, dma]
        + [dma((chunks,))] * 6
        + [dma((2,)), dma((6,)), dma, dma((3 * D // CHUNK,))],
        compiler_params=pltpu.CompilerParams(
            vmem_limit_bytes=60 * 2**20, collective_id=0, has_side_effects=True
        ),
        cost_estimate=cost(3, 64),
        name="gather",
    )(weights, small_params, x, cot, segment_ids)


def remote(src, dst, sem, recv, device):
    pltpu.make_async_remote_copy(
        src_ref=src, dst_ref=dst, send_sem=sem, recv_sem=recv, device_id=device, device_id_type=MESH
    ).start()


def greet(peers):
    barrier = pltpu.get_barrier_semaphore()
    for peer in peers:
        pl.semaphore_signal(barrier, inc=1, device_id=peer, device_id_type=MESH)
    return lambda: pl.semaphore_wait(barrier, len(peers))


def col_chunk(t):
    return pl.ds(pl.multiple_of(t * CHUNK, CHUNK), CHUNK)


class Summing:
    def __init__(self, bufs, sems):
        self.bufs, self.sems = bufs, sems
        rep, rows = lax.axis_index("rep"), lax.axis_index("rows")
        self.rep, self.px, self.py, self.z, self.c = rep, rep % 2, rep // 2, rows // 2, rows % 2
        self.x_peer = (self.py * 2 + 1 - self.px, rows)
        self.y_peer = ((1 - self.py) * 2 + self.px, rows)

    @staticmethod
    def scratch(chunks):
        buf = lambda *shape: pltpu.VMEM(shape + (16, CHUNK), f32)
        dma = pltpu.SemaphoreType.DMA
        return [
            buf(3, 4, 2, 2, 2, 2),
            buf(chunks, 4, 2, 2, 2),
            buf(chunks, 4, 2),
            buf(chunks, 4, 2),
            buf(chunks, 4),
            buf(chunks, 4),
            buf(chunks, 4, 2),
            buf(chunks, 3, 2),
        ], [dma((3,)), dma] + [dma((chunks,))] * 6

    def free(self, t):
        wait_bytes(self.bufs[0].at[t % 3, :, self.c], self.sems[0].at[t % 3])

    def push(self, t):
        gbuf, core_in = self.bufs[:2]
        to = (self.rep, self.z * 2 + 1 - self.c)
        remote(
            gbuf.at[t % 3, :, 1 - self.c], core_in.at[t], self.sems[0].at[t % 3],
            self.sems[2].at[t], to,
        )

    def halve(self, t):
        gbuf, core_in, a1, b1 = self.bufs[:4]
        _, sent, core_recv, a1_recv, b1_recv = self.sems[:5]
        wait_bytes(core_in.at[t], core_recv.at[t])
        core_in[t] = core_in[t] + gbuf[t % 3, :, self.c]
        remote(core_in.at[t, :, :, 1 - self.px, 0], a1.at[t], sent, a1_recv.at[t], self.x_peer)
        remote(core_in.at[t, :, 1 - self.py, :, 1], b1.at[t], sent, b1_recv.at[t], self.y_peer)

    def quarter(self, t):
        _, core_in, a1, b1, a2, b2 = self.bufs[:6]
        _, sent, _, a1_recv, b1_recv, a2_recv, b2_recv = self.sems[:7]
        wait_bytes(a1.at[t], a1_recv.at[t])
        a1[t] = a1[t] + core_in[t, :, :, self.px, 0]
        remote(a1.at[t, :, 1 - self.py], a2.at[t], sent, a2_recv.at[t], self.y_peer)
        wait_bytes(b1.at[t], b1_recv.at[t])
        b1[t] = b1[t] + core_in[t, :, self.py, :, 1]
        remote(b1.at[t, :, 1 - self.px], b2.at[t], sent, b2_recv.at[t], self.x_peer)

    def along_z(self, t):
        a1, b1, a2, b2, zsrc, z_in = self.bufs[2:]
        _, sent, _, _, _, a2_recv, b2_recv, z_recv = self.sems
        wait_bytes(a2.at[t], a2_recv.at[t])
        zsrc[t, :, 0] = a1[t, :, self.py] + a2[t]
        wait_bytes(b2.at[t], b2_recv.at[t])
        zsrc[t, :, 1] = b1[t, :, self.px] + b2[t]
        for k in range(1, 4):
            to = (self.z + k) % 4
            remote(zsrc.at[t, to], z_in.at[t, k - 1], sent, z_recv.at[t], (self.rep, to * 2 + self.c))

    def z_sum(self, t):
        zsrc, z_in = self.bufs[6:]
        wait_bytes(z_in.at[t], self.sems[7].at[t])
        return (zsrc[t, self.z] + z_in[t, 0]) + (z_in[t, 1] + z_in[t, 2])

    def finish(self):
        a1, b1, a2, b2, _, z_in = self.bufs[2:]
        for ref in (a1, b1, a2, b2, z_in):
            wait_bytes(ref, self.sems[1])
        for i in range(3):
            wait_bytes(self.bufs[0].at[i, :, self.c], self.sems[0].at[i])


class Spreading:
    def __init__(self, total, sems, summing):
        self.total, self.sems, self.peers = total, sems, (summing.x_peer, summing.y_peer)
        self.rep = summing.rep

    @staticmethod
    def scratch(chunks):
        dma = pltpu.SemaphoreType.DMA
        return [dma] + [dma((chunks,))] * 4

    def share(self, t, value):
        self.total[t, self.rep] = value
        piece = self.total.at[t, self.rep]
        for recv, peer in zip(self.sems[1:3], self.peers):
            remote(piece, piece, self.sems[0], recv.at[t], peer)

    def forward(self, t):
        x_peer, y_peer = self.peers
        wait_bytes(self.total.at[t, 0], self.sems[1].at[t])
        piece = self.total.at[t, x_peer[0], 0]
        remote(piece, piece, self.sems[0], self.sems[4].at[t], y_peer)
        wait_bytes(self.total.at[t, 0], self.sems[2].at[t])
        piece = self.total.at[t, y_peer[0], 1]
        remote(piece, piece, self.sems[0], self.sems[3].at[t], x_peer)

    def landed(self, t):
        wait_bytes(self.total.at[t, 0, 0], self.sems[3].at[t])
        wait_bytes(self.total.at[t, 0, 0], self.sems[4].at[t])

    def sent(self):
        wait_bytes(self.total.at[:, 0:3], self.sems[0])


PUSH = (0, 1, 2, 3, 8, 9, 10, 11, 16, 17, 18, 19)
HALVE = (2, 3, 4, 5, 9, 10, 11, 12, 18, 19, 20, 21)
QUARTER = (5, 7, 8, 9, 10, 11, 12, 15, 21, 22, 23, 25)
ALONG_Z = (8, 9, 10, 11, 12, 13, 15, 18, 23, 24, 26, 27)
Z_SUM = (10, 11, 12, 13, 16, 17, 18, 20, 26, 27, 28, 29)
FORWARD = (12, 13, 16, 17, 18, 19, 20, 22)
FIRST_PUSH = 12


def planned(step, table):
    return sum(jnp.where(step == at, i + 1, 0) for i, at in enumerate(table)) - 1


def mid_kernel(
    oh, ol, x, ch, cl, w, s,
    out, dx1, do, total, part, gs,
    x1, h2h, h2l, uh, ul, acc, chb, clb, dzh, dzl, th, tl, wcol, wrow, *rest,
):
    bufs, sems, (in_sem, w_sem, out_sem, o_sem) = rest[:8], rest[8:16], rest[16:20]
    summing = Summing(bufs, sems)
    spreading = Spreading(total, rest[20:], summing)
    spread = total.shape[0]
    gbuf = bufs[0]
    rep, rows = lax.axis_index("rep"), lax.axis_index("rows")
    c = rows % 2
    peers = [(rep, (rows // 2 + k) % 4 * 2 + c) for k in range(1, 4)]
    peers += [(rep, rows // 2 * 2 + 1 - c), summing.x_peer, summing.y_peer]
    arrived = greet(peers)

    o_in = [pltpu.make_async_copy(oh, dzh, in_sem.at[0]), pltpu.make_async_copy(ol, dzl, in_sem.at[1])]
    x_in = pltpu.make_async_copy(x, x1, in_sem.at[2])
    c_in = [pltpu.make_async_copy(ch, chb, in_sem.at[3]), pltpu.make_async_copy(cl, clb, in_sem.at[4])]

    def load(g, start):
        for phase, matrix, by_rows in (
            (0, 3, False), (2, 4, False), (4, 5, True), (5, 4, False), (8, 3, True), (9, 5, False),
        ):

            @pl.when(g // 4 == phase)
            def _():
                if by_rows:
                    src = w.at[col_chunk(g % 4), matrix * D : (matrix + 1) * D]
                    copy = pltpu.make_async_copy(src, wrow.at[g % 2], w_sem.at[g % 2])
                else:
                    src = w.at[:, col_chunk(matrix * (D // CHUNK) + g % 4)]
                    copy = pltpu.make_async_copy(src, wcol.at[g % 2], w_sem.at[g % 2])
                copy.start() if start else copy.wait()

    load(0, True)
    for copy in o_in + [x_in] + c_in:
        copy.start()
    arrived()
    for copy in o_in + [x_in]:
        copy.wait()

    def o_again(at, n):
        return [
            pltpu.make_async_copy(src.at[:, at], dst.at[:, at], o_sem.at[n, i])
            for i, (src, dst) in enumerate(((oh, dzh), (ol, dzl)))
        ]

    def do_out(n, buf):
        target = do.at[:, pl.ds(pl.multiple_of(n * 2 * CHUNK, 2 * CHUNK), 2 * CHUNK)]
        at = pl.ds(pl.multiple_of(n % 2 * 2 * CHUNK, 2 * CHUNK), 2 * CHUNK)
        return pltpu.make_async_copy(buf.at[:, at], target, out_sem.at[8 + n])

    def step(g, carry):
        load(g + 1, True)

        def summed(t):
            value = summing.z_sum(t)

            @pl.when(t < spread)
            def _():
                spreading.share(t, value)

            @pl.when(t >= spread)
            def _():
                part[t - spread] = value

        for table, body in (
            (HALVE, summing.halve),
            (QUARTER, summing.quarter),
            (ALONG_Z, summing.along_z),
            (Z_SUM, summed),
            (FORWARD, spreading.forward),
        ):
            t = planned(g - FIRST_PUSH, table)
            pl.when(t >= 0)(functools.partial(body, t))

        load(g, False)
        n = g % 4
        at = col_chunk(n)

        def phase(p):
            return pl.when(g // 4 == p)

        def gradient(t, high, low):
            @pl.when(t >= 3)
            def _():
                summing.free(t)

            gbuf[t % 3] = mm3(th[...], tl[...], high, low).reshape(gbuf.shape[1:])
            summing.push(t)

        @phase(0)
        def _():
            wh, wl = split(wcol[g % 2])
            x1[:, at] += mm3(dzh[...], dzl[...], wh, wl) + s[4:5, at]

        @phase(1)
        def _():
            normed, _ = norm_parts(x1[at, :])
            h2h[at, :], h2l[at, :] = split(normed * s[5:6, :] + s[6:7, :])

        @phase(2)
        def _():
            wh, wl = split(wcol[g % 2])
            value = mm3(h2h[...], h2l[...], wh, wl) + s[7:8, at]
            square = value * value
            bent = jnp.tanh(ROOT * (value + 0.044715 * value * square))
            high, low = split(0.5 * value * (1.0 + bent))
            uh[:, at], ul[:, at] = high, low
            th[at, :], tl[at, :] = high.T, low.T
            acc[:, at] = 0.5 * (1.0 + bent) + 0.5 * value * (1.0 - bent * bent) * (
                ROOT * (1.0 + 3.0 * 0.044715 * square)
            )

        @phase(3)
        def _():
            @pl.when(n == 0)
            def _():
                for copy in c_in:
                    copy.wait()

            gradient(n, chb[:, at], clb[:, at])

        @phase(4)
        def _():
            wh, wl = split(wrow[g % 2])
            dz = mm3(chb[...], clb[...], wh, wl, NT) * acc[:, at]
            dzh[:, at], dzl[:, at] = split(dz)
            gs[3:4, at] = col_sum(dz)
            th[at, :], tl[at, :] = h2h[:, at].T, h2l[:, at].T

        @phase(5)
        def _():
            @pl.when(n == 0)
            def _():
                acc[...] = jnp.zeros_like(acc)

            gradient(4 + n, dzh[:, at], dzl[:, at])
            wh, wl = split(wcol[g % 2])

            def some_rows(i, done):
                r = col_chunk(i)
                acc[r, :] += mm3(dzh[r, at], dzl[r, at], wh, wl, NT)
                return done

            lax.fori_loop(0, acc.shape[0] // CHUNK, some_rows, 0)
            for copy in o_again(at, n):
                copy.start()

        @phase(6)
        def _():
            @pl.when(n == 0)
            def _():
                gs[0:3, :] = jnp.zeros((3, D), f32)
            for copy in o_again(at, n):
                copy.wait()
            th[at, :], tl[at, :] = dzh[:, at].T, dzl[:, at].T
            dh2 = acc[at, :]
            normed, rstd = norm_parts(x1[at, :])
            cot = chb[at, :].astype(f32) + clb[at, :].astype(f32)
            grad = cot + norm_back(dh2, normed, rstd, s[5:6, :])
            acc[at, :] = grad
            pltpu.make_async_copy(acc.at[at, :], dx1.at[at, :], out_sem.at[n]).start()
            h2h[at, :], h2l[at, :] = split(grad)
            gs[0:1, :] += col_sum(grad)
            gs[1:2, :] += col_sum(dh2 * normed)
            gs[2:3, :] += col_sum(dh2)

        @phase(7)
        def _():
            gradient(8 + n, h2h[:, at], h2l[:, at])

        @phase(8)
        def _():
            wh, wl = split(wrow[g % 2])
            value = pair_heads(*split(mm3(h2h[...], h2l[...], wh, wl, NT)))
            wide = pl.ds(pl.multiple_of(n % 2 * 2 * CHUNK, 2 * CHUNK), 2 * CHUNK)
            for i, buf in enumerate((dzh, dzl)):

                @pl.when(n // 2 == i)
                def _():
                    buf[:, wide] = value
                    do_out(n, buf).start()

        @phase(9)
        def _():
            wh, wl = split(wcol[g % 2])
            x1[:, at] += mm3(uh[...], ul[...], wh, wl) + s[8:9, at]
            pltpu.make_async_copy(x1.at[:, at], out.at[:, at], out_sem.at[4 + n]).start()

        return carry

    lax.fori_loop(0, FIRST_PUSH + Z_SUM[-1] + 1, step, 0)
    for n in range(4):
        at = col_chunk(n)
        pltpu.make_async_copy(acc.at[at, :], dx1.at[at, :], out_sem.at[n]).wait()
        pltpu.make_async_copy(x1.at[:, at], out.at[:, at], out_sem.at[4 + n]).wait()
        do_out(n, (dzh, dzl)[n // 2]).wait()
    summing.finish()
    for t in range(spread):
        spreading.landed(t)
    spreading.sent()


def mid(oh, ol, x, ch, cl, full, small):
    t = x.shape[0]
    hbm = pl.BlockSpec(memory_space=pl.ANY)
    vmem = pl.BlockSpec(memory_space=pltpu.VMEM)
    dma = pltpu.SemaphoreType.DMA
    chunks, spread = len(PUSH), len(FORWARD)
    bufs, sems = Summing.scratch(chunks)
    wide, pair = pltpu.VMEM((t, D), f32), [pltpu.VMEM((t, D), bf16)] * 2
    return pl.pallas_call(
        mid_kernel,
        in_specs=[hbm] * 6 + [vmem],
        out_specs=[hbm, hbm, hbm, vmem, vmem, vmem],
        out_shape=[
            shape_of((t, D)),
            shape_of((t, D)),
            shape_of((t, 2 * D), bf16),
            shape_of((spread, 4, 2, 16, CHUNK)),
            shape_of((chunks - spread, 2, 16, CHUNK)),
            shape_of((4, D)),
        ],
        scratch_shapes=[wide, *pair, *pair, wide, *pair, *pair, *pair]
        + [pltpu.VMEM((2, D, CHUNK), f32), pltpu.VMEM((2, CHUNK, D), f32)]
        + bufs
        + sems
        + [dma((5,)), dma((2,)), dma((12,)), dma((4, 2))]
        + Spreading.scratch(spread),
        compiler_params=pltpu.CompilerParams(
            vmem_limit_bytes=60 * 2**20, collective_id=2, has_side_effects=True
        ),
        cost_estimate=cost(9, 60),
        name="mid",
    )(oh, ol, x, ch, cl, full, small)


MAKE = tuple(range(12))
BACK = tuple(range(12, 24))
LAST_HALVE = (2, 3, 4, 5, 6, 7, 8, 9, 10, 11, 12, 13)
LAST_QUARTER = (6, 8, 9, 10, 12, 13, 15, 16, 18, 19, 21, 22)
LAST_Z = (9, 11, 12, 13, 15, 16, 18, 19, 21, 22, 24, 25)
LAST_SUM = (12, 14, 15, 16, 18, 19, 21, 22, 24, 25, 26, 27)
LAST_FORWARD = (14, 16, 17, 18, 20, 21, 23, 24, 26, 27, 28, 29)
NORM = 24


def last_kernel(
    th_in, tl_in, dqh, dql, dkh, dkl, dvh, dvl, w, x, dx1, part, earlier, gs2, gs3, gs4567, gs8, small_in,
    out, total, small_total, norm,
    th, tl, dbuf, wbuf, acc, xbuf, dxbuf, spart, srow, srep, norm_in, *rest,
):
    bufs, sems = rest[:8], rest[8:16]
    h_sem, d_in, w_in, ln_in, ln_out, s_send, s_recv, r_send, r_recv, n_send, n_recv = rest[21:]
    summing = Summing(bufs, sems)
    spreading = Spreading(total, rest[16:21], summing)
    gbuf = bufs[0]
    rep, rows = lax.axis_index("rep"), lax.axis_index("rows")
    before, chunks = part.shape[0], bufs[1].shape[0]
    per = D // CHUNK
    t_rows = x.shape[0]
    arrived = greet(
        [(rep, (rows + k) % 8) for k in range(1, 8)] + [((rep + k) % 4, rows) for k in range(1, 4)]
    )

    h_in = [pltpu.make_async_copy(th_in, th, h_sem.at[0]), pltpu.make_async_copy(tl_in, tl, h_sem.at[1])]

    def load(step, start):
        slot = step % 2
        made, back = planned(step, MAKE), planned(step, BACK)
        u = jnp.maximum(made, back)

        def move(copy):
            copy.start() if start else copy.wait()

        for j, (high, low) in enumerate(((dqh, dql), (dkh, dkl), (dvh, dvl))):

            @pl.when(jnp.logical_and(u >= 0, u // per == j))
            def _():
                for i, source in enumerate((high, low)):
                    move(
                        pltpu.make_async_copy(
                            source.at[:, col_chunk(u % per)], dbuf.at[slot, i], d_in.at[slot, i]
                        )
                    )

        @pl.when(back >= 0)
        def _():
            move(pltpu.make_async_copy(w.at[:, col_chunk(back)], wbuf.at[slot], w_in.at[slot]))

        @pl.when(jnp.logical_and(step >= NORM, step < NORM + 4))
        def _():
            at = col_chunk(step - NORM)
            move(pltpu.make_async_copy(x.at[at, :], xbuf.at[slot], ln_in.at[slot, 0]))
            move(pltpu.make_async_copy(dx1.at[at, :], dxbuf.at[slot], ln_in.at[slot, 1]))

    for copy in h_in:
        copy.start()
    load(0, True)
    acc[...] = jnp.zeros_like(acc)
    arrived()
    for t in range(before):
        spreading.share(t, part[t])
    for copy in h_in:
        copy.wait()

    def step(s, carry):
        load(s + 1, True)
        for table, body in (
            (LAST_HALVE, summing.halve),
            (LAST_QUARTER, summing.quarter),
            (LAST_Z, summing.along_z),
            (LAST_SUM, lambda t: spreading.share(before + t, summing.z_sum(t))),
            (LAST_FORWARD, lambda t: spreading.forward(before + t)),
        ):
            t = planned(s, table)
            pl.when(t >= 0)(functools.partial(body, t))

        @pl.when(jnp.logical_and(s >= 2, s < 2 + before))
        def _():
            spreading.forward(s - 2)

        load(s, False)
        made, back = planned(s, MAKE), planned(s, BACK)

        @pl.when(made >= 3)
        def _():
            summing.free(made)

        @pl.when(made >= 0)
        def _():
            grad = mm3(th[...], tl[...], dbuf[s % 2, 0], dbuf[s % 2, 1])
            gbuf[made % 3] = grad.reshape(gbuf.shape[1:])
            summing.push(made)

        @pl.when(back >= 0)
        def _():
            wh, wl = split(wbuf[s % 2])

            def some_rows(i, done):
                at = col_chunk(i)
                acc[at, :] += mm3(dbuf[s % 2, 0, at, :], dbuf[s % 2, 1, at, :], wh, wl, NT)
                return done

            lax.fori_loop(0, t_rows // CHUNK, some_rows, 0)

        @pl.when(jnp.logical_and(s >= NORM, s < NORM + 4))
        def _():
            at = col_chunk(s - NORM)
            dh = acc[at, :]
            normed, rstd = norm_parts(xbuf[s % 2])
            acc[at, :] = dxbuf[s % 2] + norm_back(dh, normed, rstd, small_in[0:1, :])
            pltpu.make_async_copy(acc.at[at, :], out.at[at, :], ln_out.at[s - NORM]).start()
            gs = jnp.concatenate([col_sum(dh * normed), col_sum(dh)], axis=0)
            for j in range(8):
                piece = gs[:, j * 128 : (j + 1) * 128]

                @pl.when(s == NORM)
                def _():
                    spart[j, 0:2] = piece
                    for row, rest_of in ((2, gs2), (3, gs3), (4, gs4567), (8, gs8)):
                        spart[j, row : row + rest_of.shape[0]] = rest_of[:, j * 128 : (j + 1) * 128]

                @pl.when(s > NORM)
                def _():
                    spart[j, 0:2] += piece

        @pl.when(s == NORM + 4)
        def _():
            for k in range(1, 8):
                to = (rows + k) % 8
                remote(spart.at[to], srow.at[k - 1], s_send.at[k - 1], s_recv.at[k - 1], (rep, to))

        @pl.when(s == NORM + 5)
        def _():
            mine = spart[rows]
            for k in range(1, 8):
                wait_bytes(srow.at[k - 1], s_recv.at[k - 1])
                mine = mine + srow[k - 1]
            srep[rep] = mine
            for k in range(1, 4):
                piece = srep.at[rep]
                remote(piece, piece, r_send.at[k - 1], r_recv.at[k - 1], ((rep + k) % 4, rows))

        return carry

    lax.fori_loop(0, NORM + 6, step, 0)
    for k in range(1, 4):
        wait_bytes(srep.at[0], r_recv.at[k - 1])
    small = (srep[0] + srep[1]) + (srep[2] + srep[3])
    small_total[...] = small

    def squares(ref, t):
        value = ref[t].reshape(128, CHUNK)
        return jnp.sum((value * value).reshape(16, 8, CHUNK), axis=0)

    def one_earlier(t, carry):
        return carry + squares(earlier, t)

    def one(t, carry):
        spreading.landed(t)
        return carry + squares(total, t)

    mats = lax.fori_loop(0, earlier.shape[0], one_earlier, jnp.zeros((8, CHUNK), f32))
    mats = lax.fori_loop(0, before + chunks, one, mats)
    mine = jnp.sum(mats) + jnp.sum(small * small)
    norm_in[rows] = jnp.full((8, 128), mine, f32)
    for k in range(1, 8):
        piece = norm_in.at[rows]
        remote(piece, piece, n_send.at[k - 1], n_recv.at[k - 1], (rep, (rows + k) % 8))
    summing.finish()
    spreading.sent()
    for i in range(4):
        at = pl.ds(i * CHUNK, CHUNK)
        pltpu.make_async_copy(acc.at[at, :], out.at[at, :], ln_out.at[i]).wait()
    for k in range(1, 8):
        wait_bytes(srow.at[k - 1], s_send.at[k - 1])
    for k in range(1, 4):
        wait_bytes(srep.at[0], r_send.at[k - 1])
    for k in range(1, 8):
        wait_bytes(norm_in.at[0], n_recv.at[k - 1])
    value = norm_in[0]
    for j in range(1, 8):
        value = value + norm_in[j]
    norm[...] = jnp.sqrt(value)
    for k in range(1, 8):
        wait_bytes(norm_in.at[0], n_send.at[k - 1])


def last(th, tl, grads, full, x, dx1, part, earlier, gs, small):
    t = x.shape[0]
    chunks = 3 * D // CHUNK
    every = chunks + part.shape[0]
    hbm = pl.BlockSpec(memory_space=pl.ANY)
    vmem = pl.BlockSpec(memory_space=pltpu.VMEM)
    dma = pltpu.SemaphoreType.DMA
    bufs, sems = Summing.scratch(chunks)
    return pl.pallas_call(
        last_kernel,
        in_specs=[hbm] * 11 + [vmem] * 7,
        out_specs=[hbm, vmem, vmem, vmem],
        out_shape=[
            shape_of((t, D)),
            shape_of((every, 4, 2, 16, CHUNK)),
            shape_of((9, 128)),
            shape_of((8, 128)),
        ],
        scratch_shapes=[
            pltpu.VMEM((D, t), bf16),
            pltpu.VMEM((D, t), bf16),
            pltpu.VMEM((2, 2, t, CHUNK), bf16),
            pltpu.VMEM((2, D, CHUNK), f32),
            pltpu.VMEM((t, D), f32),
            pltpu.VMEM((2, CHUNK, D), f32),
            pltpu.VMEM((2, CHUNK, D), f32),
            pltpu.VMEM((8, 9, 128), f32),
            pltpu.VMEM((7, 9, 128), f32),
            pltpu.VMEM((4, 9, 128), f32),
            pltpu.VMEM((8, 8, 128), f32),
        ]
        + bufs
        + sems
        + Spreading.scratch(every)
        + [dma((2,)), dma((2, 2)), dma((2,)), dma((2, 2)), dma((4,))]
        + [dma((7,)), dma((7,)), dma((3,)), dma((3,)), dma((7,)), dma((7,))],
        compiler_params=pltpu.CompilerParams(
            vmem_limit_bytes=60 * 2**20, collective_id=1, has_side_effects=True
        ),
        cost_estimate=cost(6, 90),
        name="last",
    )(th, tl, *grads, full, x, dx1, part, earlier, *gs, small)


def adam_step(parameter, gradient, first_moment, second_moment, average):
    first_new = 0.9 * first_moment + 0.1 * gradient
    second_new = 0.999 * second_moment + 0.001 * gradient * gradient
    first_hat = first_new * (1.0 / (1.0 - 0.9**STEP))
    second_hat = second_new * (1.0 / (1.0 - 0.999**STEP))
    parameter_new = parameter - 0.05 * (
        first_hat / (jnp.sqrt(second_hat) + 1e-08) + 0.05 * parameter
    )
    average_new = 0.99 * average + 0.01 * parameter_new
    return (parameter_new, first_new, second_new, average_new)


CLIP = 0.25 * math.sqrt(6 * D * D + 9 * D)


def adam_kernel(
    grad_a, grad_b, norm, w, first, second, average, gs, p_s, first_s, second_s, average_s,
    clipped, new_w, first_o, second_o, average_o, low,
    clipped_so, new_so, first_so, second_so, average_so, low_so, norm_out,
):
    norm_out[0] = jnp.max(norm[...])
    factor = jnp.minimum(1.0, CLIP / norm[0:1, 0:1])
    early = pl.program_id(0) < 2
    for j in range(D // CHUNK):
        at = slice(j * CHUNK, (j + 1) * CHUNK)
        value = jnp.where(early, grad_a[j], grad_b[j]).reshape(w.shape[0], CHUNK) * factor
        clipped[:, at] = value
        news = adam_step(w[:, at], value, first[:, at], second[:, at], average[:, at])
        for ref, new in zip((new_w, first_o, second_o, average_o), news):
            ref[:, at] = new
        low[:, at] = news[0].astype(bf16)

    @pl.when(pl.program_id(0) == 0)
    def _():
        value = gs[...] * factor
        clipped_so[...] = value
        news = adam_step(p_s[...], value, first_s[...], second_s[...], average_s[...])
        for ref, new in zip((new_so, first_so, second_so, average_so), news):
            ref[...] = new
        low_so[...] = news[0].astype(bf16)


def adam(earlier, total, norm, mats, gs, smalls):
    shard, width = mats[0].shape
    block = pl.BlockSpec((shard, D), lambda i: (0, jnp.where(i < 3, 5 - i, i - 3)))
    cut = (D // CHUNK,) + total.shape[1:]
    grads = [
        pl.BlockSpec(cut, lambda i: (jnp.minimum(i, 1), 0, 0, 0, 0)),
        pl.BlockSpec(cut, lambda i: (jnp.maximum(i - 2, 0), 0, 0, 0, 0)),
    ]
    small = whole(gs.shape)
    return pl.pallas_call(
        adam_kernel,
        grid=(width // D,),
        in_specs=grads + [whole(norm.shape)] + [block] * 4 + [small] * 5,
        out_specs=[block] * 6 + [small] * 6 + [pl.BlockSpec(memory_space=pltpu.SMEM)],
        out_shape=[shape_of((shard, width))] * 5
        + [shape_of((shard, width), bf16)]
        + [shape_of(gs.shape)] * 5
        + [shape_of(gs.shape, bf16), shape_of((1,))],
        compiler_params=params(),
        cost_estimate=cost(0, 32),
        name="adam",
    )(earlier, total, norm, *mats, gs, *smalls)


def split_once(w, wh, wl):
    @pl.when(pl.program_id(0) == 0)
    def _():
        wh[...], wl[...] = split(w[...])


def out_proj_kernel(oh, ol, w, x, s, x1, h2h, h2l, wh, wl):
    split_once(w, wh, wl)
    value = x[...] + mm3(oh[...], ol[...], wh[...], wl[...]) + s[4:5]
    x1[...] = value
    normed, _ = norm_parts(value)
    h2h[...], h2l[...] = split(normed * s[5:6] + s[6:7])


def out_proj(oh, ol, w, x, small, bm=256):
    t = x.shape[0]
    return pl.pallas_call(
        out_proj_kernel,
        grid=(t // bm,),
        in_specs=[rows_of(bm, D)] * 2 + [matrix(3), rows_of(bm, D), whole((9, D))],
        out_specs=[rows_of(bm, D)] * 3,
        out_shape=[shape_of((t, D)), shape_of((t, D), bf16), shape_of((t, D), bf16)],
        scratch_shapes=[pltpu.VMEM((D, D), bf16)] * 2,
        compiler_params=params(),
        cost_estimate=cost(1, 20),
        name="out_proj",
    )(oh, ol, w, x, small)


def up_kernel(hh, hl, w, s, z, uh, ul):
    wh, wl = split(w[...])
    value = mm3(hh[...], hl[...], wh, wl) + s[7:8]
    z[...] = value
    bent = jnp.tanh(ROOT * (value + 0.044715 * value * value * value))
    uh[...], ul[...] = split(0.5 * value * (1.0 + bent))


def up(hh, hl, w, small, bn=256):
    t = hh.shape[0]
    return pl.pallas_call(
        up_kernel,
        grid=(FF // bn,),
        in_specs=[whole((t, D))] * 2 + [cols_of(D, bn, 4 * D // bn), cols_of(9, bn)],
        out_specs=[cols_of(t, bn)] * 3,
        out_shape=[shape_of((t, FF)), shape_of((t, FF), bf16), shape_of((t, FF), bf16)],
        compiler_params=params(),
        cost_estimate=cost(1, 16),
        name="up",
    )(hh, hl, w, small)


def down_kernel(uh, ul, w, x1, s, out):
    wh, wl = split(w[...])
    out[...] = x1[...] + mm3(uh[...], ul[...], wh, wl) + s[8:9]


def down(uh, ul, w, x1, small, bn=256):
    t = uh.shape[0]
    return pl.pallas_call(
        down_kernel,
        grid=(D // bn,),
        in_specs=[whole((t, FF))] * 2
        + [cols_of(FF, bn, 5 * D // bn), cols_of(t, bn), cols_of(9, bn)],
        out_specs=cols_of(t, bn),
        out_shape=shape_of((t, D)),
        compiler_params=params(),
        cost_estimate=cost(1, 16),
        name="down",
    )(uh, ul, w, x1, small)


def outer_kernel(ah, al, dh, dl, out, th, tl):
    @pl.when(pl.program_id(0) == 0)
    def _():
        th[...] = ah[...].T
        tl[...] = al[...].T

    out[...] = mm3(th[...], tl[...], dh[...], dl[...])


def outer(ah, al, dh, dl, bn=256):
    t, m = ah.shape
    n = dh.shape[1]
    return pl.pallas_call(
        outer_kernel,
        grid=(n // bn,),
        in_specs=[whole((t, m))] * 2 + [cols_of(t, bn)] * 2,
        out_specs=cols_of(m, bn),
        out_shape=shape_of((m, n)),
        scratch_shapes=[pltpu.VMEM((m, t), bf16)] * 2,
        compiler_params=params(),
        cost_estimate=cost(1, 12),
        name="outer",
    )(ah, al, dh, dl)


def down_back_kernel(ch, cl, w, z, dzh, dzl, gs7):
    wh, wl = split(w[...])
    du = mm3(ch[...], cl[...], wh, wl, NT)
    value = z[...]
    square = value * value
    bent = jnp.tanh(ROOT * (value + 0.044715 * value * square))
    slope = 0.5 * (1.0 + bent) + 0.5 * value * (1.0 - bent * bent) * (
        ROOT * (1.0 + 3.0 * 0.044715 * square)
    )
    dz = du * slope
    dzh[...], dzl[...] = split(dz)
    gs7[...] = col_sum(dz)


def down_back(ch, cl, w, z, bn=256):
    t = ch.shape[0]
    return pl.pallas_call(
        down_back_kernel,
        grid=(FF // bn,),
        in_specs=[whole((t, D))] * 2 + [rows_of(bn, D, 5), cols_of(t, bn)],
        out_specs=[cols_of(t, bn)] * 2 + [cols_of(1, bn)],
        out_shape=[shape_of((t, FF), bf16)] * 2 + [shape_of((1, FF))],
        compiler_params=params(),
        cost_estimate=cost(1, 16),
        name="down_back",
    )(ch, cl, w, z)


def up_back_kernel(dzh, dzl, w, x1, cot, s, dx1, dxh, dxl, gs4, gs5, gs6, wh, wl):
    split_once(w, wh, wl)
    dh2 = mm3(dzh[...], dzl[...], wh[...], wl[...], NT)
    normed, rstd = norm_parts(x1[...])
    grad = cot[...] + norm_back(dh2, normed, rstd, s[5:6])
    dx1[...] = grad
    dxh[...], dxl[...] = split(grad)
    add_up(gs4, col_sum(grad))
    add_up(gs5, col_sum(dh2 * normed))
    add_up(gs6, col_sum(dh2))


def up_back(dzh, dzl, w, x1, cot, small, bm=256):
    t = x1.shape[0]
    return pl.pallas_call(
        up_back_kernel,
        grid=(t // bm,),
        in_specs=[rows_of(bm, FF)] * 2 + [matrix(4)] + [rows_of(bm, D)] * 2 + [whole((9, D))],
        out_specs=[rows_of(bm, D)] * 3 + [whole((1, D))] * 3,
        out_shape=[shape_of((t, D)), shape_of((t, D), bf16), shape_of((t, D), bf16)]
        + [shape_of((1, D))] * 3,
        scratch_shapes=[pltpu.VMEM((D, FF), bf16)] * 2,
        compiler_params=params(),
        cost_estimate=cost(1, 24),
        name="up_back",
    )(dzh, dzl, w, x1, cot, small)


def out_proj_back_kernel(dxh, dxl, w, do):
    wh, wl = split(w[...])
    do[...] = pair_heads(*split(mm3(dxh[...], dxl[...], wh, wl, NT)))


def out_proj_back(dxh, dxl, w, bn=256):
    t = dxh.shape[0]
    return pl.pallas_call(
        out_proj_back_kernel,
        grid=(D // bn,),
        in_specs=[whole((t, D))] * 2 + [rows_of(bn, D, 3)],
        out_specs=cols_of(t, 2 * bn),
        out_shape=shape_of((t, 2 * D), bf16),
        compiler_params=params(),
        cost_estimate=cost(1, 12),
        name="out_proj_back",
    )(dxh, dxl, w)


def proj_back_kernel(
    dqh, dql, dkh, dkl, dvh, dvl, wq, wk, wv, x, dx1, s, out, gs0, gs1, wh, wl
):
    @pl.when(pl.program_id(0) == 0)
    def _():
        for j, w in enumerate((wq, wk, wv)):
            wh[j], wl[j] = split(w[...])

    dh = mm3(dqh[...], dql[...], wh[0], wl[0], NT)
    dh += mm3(dkh[...], dkl[...], wh[1], wl[1], NT)
    dh += mm3(dvh[...], dvl[...], wh[2], wl[2], NT)
    normed, rstd = norm_parts(x[...])
    out[...] = dx1[...] + norm_back(dh, normed, rstd, s[0:1])
    add_up(gs0, col_sum(dh * normed))
    add_up(gs1, col_sum(dh))


def proj_back(grads, w, x, dx1, small, bm=256):
    t = x.shape[0]
    return pl.pallas_call(
        proj_back_kernel,
        grid=(t // bm,),
        in_specs=[rows_of(bm, D)] * 6 + [matrix(j) for j in range(3)] + [rows_of(bm, D)] * 2 + [whole((9, D))],
        out_specs=[rows_of(bm, D)] + [whole((1, D))] * 2,
        out_shape=[shape_of((t, D))] + [shape_of((1, D))] * 2,
        scratch_shapes=[pltpu.VMEM((3, D, D), bf16)] * 2,
        compiler_params=params(),
        cost_estimate=cost(3, 36),
        name="proj_back",
    )(*grads, w, w, w, x, dx1, small)


def set_bounds(segment_ids):
    ids = segment_ids[0, ::UNIT]
    order, sets = (ids - ids[0])[None, :], jnp.arange(SETS, dtype=jnp.int32)[:, None]
    lengths = jnp.sum((order == sets).astype(jnp.int32), axis=1)
    firsts = jnp.sum((order < sets).astype(jnp.int32), axis=1)
    return jnp.stack([firsts, lengths], axis=1).reshape(-1).astype(jnp.int32)


def shards(
    reps,
    latents,
    cotangent,
    segment_ids,
    weights,
    small_params,
    first_mats,
    second_mats,
    average_mats,
    first_small,
    second_small,
    average_small,
):
    segs = set_bounds(segment_ids)
    x, cot = latents[0], cotangent[0]
    fast = reps == 4 and weights.shape[0] * 8 == D and x.shape[0] == D
    if fast:
        full, small, th, tl, ch, cl, gs8, qkv, oh, ol, lse = gather(
            weights, small_params, x, cot, segment_ids
        )
    else:
        full, small = (
            lax.all_gather(weights, "rows", axis=0, tiled=True),
            lax.all_gather(small_params, "rows", axis=1, tiled=True),
        )
        bias = jnp.concatenate([small[2], jnp.zeros((D,), f32), small[3]])[None]
        hh, hl, ch, cl, gs8 = prep(x, cot, small)
        qkv = proj(hh, hl, full, bias)
        oh, ol, lse = attend(segs, qkv)
    if fast:
        output, dx1, do, earlier, part, gs4567 = mid(oh, ol, x, ch, cl, full, small)
    else:
        x1, h2h, h2l = out_proj(oh, ol, full, x, small)
        z, uh, ul = up(h2h, h2l, full, small)
        output = down(uh, ul, full, x1, small)
        g_down = outer(uh, ul, ch, cl)
        dzh, dzl, gs7 = down_back(ch, cl, full, z)
        g_up = outer(h2h, h2l, dzh, dzl)
        dx1, dxh, dxl, gs4, gs5, gs6 = up_back(dzh, dzl, full, x1, cot, small)
        g_out = outer(oh, ol, dxh, dxl)
        do = out_proj_back(dxh, dxl, full)
        gs4567 = jnp.concatenate([gs4, gs5, gs6, gs7], axis=0)
    *grads, gs2, gs3, output = attend_back(segs, qkv, do, oh, ol, lse, output)
    gs_rest = (gs2, gs3, gs4567, gs8)
    if fast:
        token_grad, total, small_total, norm = last(
            th, tl, grads, full, x, dx1, part, earlier, gs_rest, small
        )
        (
            clipped_mats, new_weights, first_mats_out, second_mats_out, average_mats_out, low_mats,
            clipped_small, new_small, first_small_out, second_small_out, average_small_out, low_small,
            norm,
        ) = adam(
            earlier, total, norm, (weights, first_mats, second_mats, average_mats), small_total,
            (small_params, first_small, second_small, average_small),
        )
    else:
        g_qkv = [outer(hh, hl, grads[2 * j], grads[2 * j + 1]) for j in range(3)]
        token_grad, gs0, gs1 = proj_back(grads, full, x, dx1, small)
        weight_grad = jnp.concatenate(g_qkv + [g_out, g_up, g_down], axis=1)
        small_grad = jnp.concatenate([gs0, gs1, *gs_rest], axis=0)
        part_weights, part_small = (
            lax.psum_scatter(weight_grad, "rows", scatter_dimension=0, tiled=True),
            lax.psum_scatter(small_grad, "rows", scatter_dimension=1, tiled=True),
        )
        sum_weights, sum_small = lax.psum((part_weights, part_small), "rep")
        squares = lax.psum(
            jnp.sum(sum_weights * sum_weights) + jnp.sum(sum_small * sum_small), "rows"
        )
        norm = jnp.sqrt(squares).reshape(1)
        factor = jnp.minimum(1.0, CLIP / norm[0])
        clipped_mats = sum_weights * factor
        clipped_small = sum_small * factor
        new_weights, first_mats_out, second_mats_out, average_mats_out = adam_step(
            weights, clipped_mats, first_mats, second_mats, average_mats
        )
        new_small, first_small_out, second_small_out, average_small_out = adam_step(
            small_params, clipped_small, first_small, second_small, average_small
        )
        low_mats, low_small = new_weights.astype(bf16), new_small.astype(bf16)
    return (
        output[None],
        token_grad[None],
        norm,
        clipped_mats,
        clipped_small,
        new_weights,
        new_small,
        first_mats_out,
        second_mats_out,
        average_mats_out,
        first_small_out,
        second_small_out,
        average_small_out,
        low_mats,
        low_small,
    )


def solution(mesh):
    tokens, mats, small = P("rep", "rows", None), P("rows", None), P(None, "rows")
    in_specs = (tokens, tokens, P("rep", "rows")) + (mats, small) + (mats,) * 3 + (small,) * 3
    out_specs = (
        (tokens, tokens, P(), mats, small, mats, small) + (mats,) * 3 + (small,) * 3 + (mats, small)
    )
    step = functools.partial(shards, mesh.shape["rep"])
    return jax.shard_map(step, mesh=mesh, in_specs=in_specs, out_specs=out_specs, check_vma=False)
```
